32 devices in a mesh: section: 4 (over y, x), seq: 8 (over z, core).
Axes of the slice: x: 2, y: 2, z: 4, core: 2. Of those that a mesh axis runs over, the one named last changes fastest.
Arguments:
- queries: bfloat16 [4, 1024, 4096], P('section', 'seq'), may hold values from -120 to 120
- grad_out: bfloat16 [4, 1024, 4096], P('section', 'seq'), may hold values from -6 to 6
- keys: bfloat16 [1024, 1024], P('seq', 'section'), may hold values from -5.5 to 5.5
- values: bfloat16 [1024, 1024], P('seq', 'section'), may hold values from -6 to 6
- key_first: int32 [8], P('seq'), may hold values from 0 to 7, as said below
Outputs:
- grad_queries: bfloat16 [4, 1024, 4096], P('section', 'seq')
- grad_keys: float32 [1024, 1024], P('seq', 'section')
- grad_values: float32 [1024, 1024], P('seq', 'section')
The draws below stay inside these ranges and needn't reach their ends.
Inputs may be any that keep to these rules, and one draw needn't show every extreme that they name: s - 1 <= key_first[s] <= s and key_first[s] >= 0; in every draw some shard s >= 1 has key_first[s] = s - 1.
All inputs are finite; a program needn't handle non-finite values.
Results may differ from the reference program's by a relative error of at most 0.008.
Values may be sent and summed in bfloat16 or wider, within the bound.
No kernel may reach another device: no remote copies, remote signals or barrier semaphores. Data moves between devices by JAX's collectives and lax.ppermute only.
A program may use at most 64 MiB of HBM per device.

```python
import math
import jax
import jax.numpy as jnp
from jax import lax

HEADS = 32
KV_HEADS = 8
HEAD_DIM = 128
TQ = 128
SPAN = 2
SHARDS = 8
LAYERS = 4
NTOK = 1024
Q_WIDTH = 4096
KV_WIDTH = 1024


def cache_rows(key):
    kv_width = KV_HEADS * HEAD_DIM
    drawn = jnp.clip(jax.random.normal(jax.random.fold_in(key, 11), (NTOK, kv_width), jnp.float32), -5.0, 5.0)
    return drawn


def draw_keys(key, part):
    return cache_rows(key).astype(jnp.bfloat16)


def draw_queries(key, part):
    q_width = HEADS * HEAD_DIM
    drawn = jnp.clip(jax.random.normal(jax.random.fold_in(key, 21), (LAYERS, NTOK, q_width), jnp.float32), -5.0, 5.0)
    return drawn.astype(jnp.bfloat16)


def draw_key_first(key, part):
    shard_ids = jnp.arange(SHARDS, dtype=jnp.int32)
    reach_back = jax.random.randint(jax.random.fold_in(key, 31), (SHARDS,), 0, SPAN)
    chosen = jax.random.randint(jax.random.fold_in(key, 32), (), SPAN - 1, SHARDS)
    reach_back = jnp.where(shard_ids == chosen, SPAN - 1, reach_back)
    return jnp.maximum(shard_ids - reach_back, 0).astype(jnp.int32)


def level_of(own_key, dims, cuts, least, top_value):
    gain = 1.0
    for dim, parts in cuts:
        steps = jax.random.uniform(jax.random.fold_in(jax.random.fold_in(own_key, 6), dim), (parts,), jnp.float32, least / len(cuts), top_value / len(cuts))
        gain = gain * jnp.repeat(jnp.exp(steps), dims[dim] // parts).reshape((-1,) + (1,) * (len(dims) - 1 - dim))
    return gain


def scatter_about(key, dims, scale, bound, cuts=(), held_as=jnp.bfloat16):
    drawn = jax.random.normal(key, dims, jnp.float32) * scale
    if len(cuts) > 0:
        drawn = level_of(key, dims, cuts, -0.22, 0.18) * drawn
    return jnp.clip(drawn, min=-bound, max=bound).astype(held_as)


def setup_inputs(seed: int = 0) -> dict:
    key_of = jax.random.split(jax.random.key(seed), 6)
    return {
        "queries": draw_queries(jax.random.fold_in(key_of[5], 71), 0),
        "grad_out": scatter_about(key_of[1], (LAYERS, NTOK, Q_WIDTH), 1.0, 6.0, ((0, 4), (1, 8))),
        "keys": draw_keys(jax.random.fold_in(key_of[5], 71), 0),
        "values": scatter_about(key_of[3], (NTOK, KV_WIDTH), 1.0, 6.0, ((0, 8), (1, 4))),
        "key_first": draw_key_first(jax.random.fold_in(key_of[5], 71), 0),
    }


masked_score = -1e+30

def shard_grads(query_rows, grad_rows, key_win, value_win, key_start, shard_index):
    group_size = HEADS // KV_HEADS
    key_count = SPAN * TQ
    score_scale = 1.0 / math.sqrt(HEAD_DIM)
    q_float = query_rows.astype(jnp.float32).reshape(TQ, KV_HEADS, group_size, HEAD_DIM)
    g_float = grad_rows.astype(jnp.float32).reshape(TQ, KV_HEADS, group_size, HEAD_DIM)
    k_float = key_win.astype(jnp.float32).reshape(key_count, KV_HEADS, HEAD_DIM)
    v_float = value_win.astype(jnp.float32).reshape(key_count, KV_HEADS, HEAD_DIM)
    q_pos = shard_index * TQ + jnp.arange(TQ, dtype=jnp.int32)
    k_pos = (shard_index - SPAN + 1) * TQ + jnp.arange(key_count, dtype=jnp.int32)
    visible = (k_pos[None, :] >= key_start * TQ) & (k_pos[None, :] <= q_pos[:, None])
    scores = jnp.einsum('ikgd,tkd->kgit', q_float, k_float) * score_scale
    scores = jnp.where(visible, scores, masked_score)
    row_max = lax.optimization_barrier(jnp.max(scores, axis=-1, keepdims=True))
    weights = jnp.exp(scores - row_max)
    weights = weights / lax.optimization_barrier(jnp.sum(weights, axis=-1, keepdims=True))
    dprob = jnp.einsum('ikgd,tkd->kgit', g_float, v_float)
    row_dot = lax.optimization_barrier(jnp.sum(weights * dprob, axis=-1, keepdims=True))
    dscore = (weights * (dprob - row_dot) * score_scale).astype(jnp.bfloat16)
    wround = weights.astype(jnp.bfloat16)
    dscore, wround = lax.optimization_barrier((dscore, wround))
    ds_float = dscore.astype(jnp.float32)
    w_float = wround.astype(jnp.float32)
    grad_q = jnp.einsum('kgit,tkd->ikgd', ds_float, k_float).reshape(TQ, HEADS * HEAD_DIM).astype(jnp.bfloat16)
    grad_k = jnp.einsum('kgit,ikgd->tkd', ds_float, q_float).reshape(key_count, KV_HEADS * HEAD_DIM)
    grad_v = jnp.einsum('kgit,ikgd->tkd', w_float, g_float).reshape(key_count, KV_HEADS * HEAD_DIM)
    return (grad_q, grad_k, grad_v)

def reference(queries, grad_out, keys, values, key_first):
    kv_width = KV_HEADS * HEAD_DIM
    zero_rows = jnp.zeros(((SPAN - 1) * TQ, kv_width), keys.dtype)
    keys_pad = jnp.concatenate([zero_rows, keys], axis=0)
    values_pad = jnp.concatenate([zero_rows, values], axis=0)

    def per_layer(running, layer_in):
        q_layer, g_layer = layer_in

        def per_shard(shard_index):
            start = shard_index * TQ
            q_rows = lax.dynamic_slice_in_dim(q_layer, start, TQ, 0)
            g_rows = lax.dynamic_slice_in_dim(g_layer, start, TQ, 0)
            key_win = lax.dynamic_slice_in_dim(keys_pad, start, SPAN * TQ, 0)
            value_win = lax.dynamic_slice_in_dim(values_pad, start, SPAN * TQ, 0)
            key_start = lax.dynamic_index_in_dim(key_first, shard_index, 0, keepdims=False)
            return shard_grads(q_rows, g_rows, key_win, value_win, key_start, shard_index)
        grad_q, grad_k, grad_v = lax.map(per_shard, jnp.arange(SHARDS, dtype=jnp.int32))
        return ((running[0] + grad_k, running[1] + grad_v), grad_q.reshape(NTOK, HEADS * HEAD_DIM))
    zero_acc = jnp.zeros((SHARDS, SPAN * TQ, kv_width), jnp.float32)
    (key_wins, value_wins), grad_queries = lax.scan(per_layer, (zero_acc, zero_acc), (queries, grad_out))
    key_wins = key_wins.reshape(SHARDS, SPAN, TQ, kv_width)
    value_wins = value_wins.reshape(SHARDS, SPAN, TQ, kv_width)
    summed_k = jnp.zeros((SHARDS + SPAN - 1, TQ, kv_width), jnp.float32)
    summed_v = jnp.zeros((SHARDS + SPAN - 1, TQ, kv_width), jnp.float32)
    for window_slot in range(SPAN):
        summed_k = summed_k.at[window_slot:window_slot + SHARDS].add(key_wins[:, window_slot])
        summed_v = summed_v.at[window_slot:window_slot + SHARDS].add(value_wins[:, window_slot])
    grad_keys = summed_k[SPAN - 1:].reshape(NTOK, kv_width)
    grad_values = summed_v[SPAN - 1:].reshape(NTOK, kv_width)
    return (grad_queries, grad_keys, grad_values)
```

```python
import functools
import math

import jax
import jax.numpy as jnp
from jax import lax
from jax.experimental import pallas as pl
from jax.experimental.pallas import tpu as pltpu
from jax.sharding import PartitionSpec as P

HEADS = 32
KV_HEADS = 8
HEAD_DIM = 128
GROUP = HEADS // KV_HEADS
MASKED = -1e30
SCALE = 1.0 / math.sqrt(HEAD_DIM)
EXP2_SCALE = SCALE * math.log2(math.e)

NT = (((1,), (1,)), ((), ()))
NN = (((1,), (0,)), ((), ()))
TN = (((0,), (0,)), ((), ()))


def passed_along(x, axis, by):
    size = lax.axis_size(axis)
    pairs = [(i, i + by) for i in range(size) if 0 <= i + by < size]
    return lax.ppermute(x, axis, pairs)


def swapped(x, axis, flip):
    size = lax.axis_size(axis)
    return lax.ppermute(x, axis, [(i, i ^ flip) for i in range(size)])


def dot(a, b, dims):
    return lax.dot_general(a, b, dims, preferred_element_type=jnp.float32)


def group_grads(q4, g4, k2, v2, bias, causal):
    tok = k2.shape[0] // 2
    scores = dot(k2, q4, NT)
    dprob = dot(v2, g4, NT)
    s_prev = scores[:tok] + bias
    s_own = jnp.where(causal, scores[tok:], MASKED)
    top = jnp.maximum(
        jnp.max(s_prev, axis=0, keepdims=True), jnp.max(s_own, axis=0, keepdims=True)
    )
    s_all = jnp.concatenate([s_prev, s_own], axis=0)
    p = jnp.exp2((s_all - top) * EXP2_SCALE)
    total = jnp.sum(p, axis=0, keepdims=True)
    mixed = jnp.sum(p * dprob, axis=0, keepdims=True)
    inv = 1.0 / total
    row_dot = mixed * inv
    w = p * inv
    dscore = (w * (dprob - row_dot) * SCALE).astype(jnp.bfloat16)
    wround = w.astype(jnp.bfloat16)
    dk = dot(dscore, q4, NN)
    dv = dot(wround, g4, NN)
    dq_t = dot(k2, dscore, TN)
    return dq_t, dk, dv


def attention_kernel(slices, seen_ref, place_ref, q_ref, g_ref, *refs):
    own_refs, prev_refs = refs[:slices], refs[slices : 2 * slices]
    dq_ref, own_out, prev_out = refs[2 * slices :]
    _, tok, width = own_refs[0].shape
    bias = jnp.where(seen_ref[0] > 0, 0.0, MASKED).astype(jnp.float32)
    key_pos = lax.broadcasted_iota(jnp.int32, (tok, GROUP * tok), 0)
    query_pos = lax.broadcasted_iota(jnp.int32, (tok, GROUP * tok), 1) % tok
    causal = key_pos <= query_pos
    per_slice = width // HEAD_DIM
    for flip in range(slices):
        j = place_ref[0] ^ flip
        own_ref, prev_ref = own_refs[flip], prev_refs[flip]
        for h in range(per_slice):
            cols = slice(h * HEAD_DIM, (h + 1) * HEAD_DIM)
            first = (j * per_slice + h) * GROUP
            heads = [
                pl.ds(pl.multiple_of((first + a) * HEAD_DIM, HEAD_DIM), HEAD_DIM)
                for a in range(GROUP)
            ]
            q4 = jnp.concatenate([q_ref[:, c] for c in heads], axis=0)
            g4 = jnp.concatenate([g_ref[:, c] for c in heads], axis=0)
            k2 = jnp.concatenate([prev_ref[0, :, cols], own_ref[0, :, cols]], axis=0)
            v2 = jnp.concatenate([prev_ref[1, :, cols], own_ref[1, :, cols]], axis=0)
            dq_t, dk, dv = group_grads(q4, g4, k2, v2, bias, causal)
            for a in range(GROUP):
                dq_ref[:, heads[a]] = dq_t[:, a * tok : (a + 1) * tok].T.astype(dq_ref.dtype)
            prev_out[j, 0, :, cols] = dk[:tok].astype(prev_out.dtype)
            own_out[j, 0, :, cols] = dk[tok:]
            prev_out[j, 1, :, cols] = dv[:tok].astype(prev_out.dtype)
            own_out[j, 1, :, cols] = dv[tok:]


def body(queries, grad_out, keys, values, key_first):
    shard_index = lax.axis_index("seq")
    slices = lax.axis_size("section")
    seen = (key_first < shard_index).astype(jnp.int32)
    place = lax.axis_index("section").astype(jnp.int32).reshape(1)
    pair = jnp.stack([keys, values])
    own = [pair] + [swapped(pair, "section", flip) for flip in range(1, slices)]
    prev = [passed_along(part, "seq", 1) for part in own]
    vmem = pl.BlockSpec(memory_space=pltpu.VMEM)
    smem = pl.BlockSpec(memory_space=pltpu.SMEM)
    grads = (slices,) + pair.shape
    dq, own_grads, prev_grads = pl.pallas_call(
        functools.partial(attention_kernel, slices),
        out_shape=(
            jax.ShapeDtypeStruct(queries.shape[1:], jnp.bfloat16),
            jax.ShapeDtypeStruct(grads, jnp.float32),
            jax.ShapeDtypeStruct(grads, jnp.bfloat16),
        ),
        in_specs=[smem, smem] + [vmem] * (2 + 2 * slices),
        out_specs=(vmem, vmem, vmem),
        compiler_params=pltpu.CompilerParams(vmem_limit_bytes=40 * 1024 * 1024),
        name="attention_backward",
    )(seen, place, queries[0], grad_out[0], *own, *prev)
    later = passed_along(prev_grads, "seq", -1)
    summed = (own_grads + later.astype(jnp.float32)).astype(jnp.bfloat16)
    shares = lax.all_to_all(summed, "section", split_axis=0, concat_axis=0, tiled=True)
    owned = jnp.sum(shares.astype(jnp.float32), axis=0)
    return (dq[None], owned[0], owned[1])


def solution(mesh):
    placed = (
        P("section", "seq", None),
        P("section", "seq", None),
        P("seq", "section"),
        P("seq", "section"),
        P("seq"),
    )
    return jax.shard_map(
        body,
        mesh=mesh,
        in_specs=placed,
        out_specs=(P("section", "seq", None), P("seq", "section"), P("seq", "section")),
        check_vma=False,
    )
```

```python
import functools
import math

import jax
import jax.numpy as jnp
from jax import lax
from jax.experimental import pallas as pl
from jax.experimental.pallas import tpu as pltpu
from jax.sharding import PartitionSpec as P

HEADS = 32
KV_HEADS = 8
HEAD_DIM = 128
GROUP = HEADS // KV_HEADS
MASKED = -1e30
SCALE = 1.0 / math.sqrt(HEAD_DIM)
EXP2_SCALE = SCALE * math.log2(math.e)

NT = (((1,), (1,)), ((), ()))
NN = (((1,), (0,)), ((), ()))
TN = (((0,), (0,)), ((), ()))


def paired(x, parity, by):
    size = lax.axis_size("seq")
    pairs = [(i, i + by) for i in range(size) if i % 2 == parity and 0 <= i + by < size]
    return lax.ppermute(x, "seq", pairs)


def seq_swapped(x, parity):
    size = lax.axis_size("seq")
    firsts = [i for i in range(size - 1) if i % 2 == parity]
    return lax.ppermute(x, "seq", [p for i in firsts for p in ((i, i + 1), (i + 1, i))])


def swapped(x, axis, flip):
    size = lax.axis_size(axis)
    return lax.ppermute(x, axis, [(i, i ^ flip) for i in range(size)])


def dot(a, b, dims):
    return lax.dot_general(a, b, dims, preferred_element_type=jnp.float32)


def group_grads(q4, g4, k2, v2, bias, causal):
    tok = k2.shape[0] // 2
    scores = dot(k2, q4, NT)
    dprob = dot(v2, g4, NT)
    s_prev = scores[:tok] + bias
    s_own = jnp.where(causal, scores[tok:], MASKED)
    top = jnp.maximum(
        jnp.max(s_prev, axis=0, keepdims=True), jnp.max(s_own, axis=0, keepdims=True)
    )
    s_all = jnp.concatenate([s_prev, s_own], axis=0)
    p = jnp.exp2((s_all - top) * EXP2_SCALE)
    total = jnp.sum(p, axis=0, keepdims=True)
    mixed = jnp.sum(p * dprob, axis=0, keepdims=True)
    inv = 1.0 / total
    row_dot = mixed * inv
    w = p * inv
    dscore = (w * (dprob - row_dot) * SCALE).astype(jnp.bfloat16)
    wround = w.astype(jnp.bfloat16)
    dk = dot(dscore, q4, NN)
    dv = dot(wround, g4, NN)
    dq_t = dot(k2, dscore, TN)
    return dq_t, dk, dv


def attention_kernel(slices, seen_ref, place_ref, q_hbm, g_hbm, *refs):
    own_refs, even_refs, odd_refs = (refs[i * slices : (i + 1) * slices] for i in range(3))
    dq_hbm = refs[3 * slices]
    own_outs, prev_outs = (refs[i * slices + 1 : (i + 1) * slices + 1] for i in (3, 4))
    q_buf, g_buf, dq_buf, q_sem, g_sem, dq_sem = refs[5 * slices + 1 :]
    _, tok, width = own_refs[0].shape
    q_width = width * GROUP
    spans = [
        pl.ds(pl.multiple_of((place_ref[0] ^ flip) * q_width, q_width), q_width)
        for flip in range(slices)
    ]
    q_copies, g_copies, dq_copies = [], [], []
    for flip, span in enumerate(spans):
        q_copies.append(pltpu.make_async_copy(q_hbm.at[:, span], q_buf.at[flip], q_sem.at[flip]))
        g_copies.append(pltpu.make_async_copy(g_hbm.at[:, span], g_buf.at[flip], g_sem.at[flip]))
        dq_copies.append(pltpu.make_async_copy(dq_buf.at[flip], dq_hbm.at[:, span], dq_sem.at[flip]))
        q_copies[flip].start()
        g_copies[flip].start()
    bias = jnp.where(seen_ref[0] > 0, 0.0, MASKED).astype(jnp.float32)
    key_pos = lax.broadcasted_iota(jnp.int32, (tok, GROUP * tok), 0)
    query_pos = lax.broadcasted_iota(jnp.int32, (tok, GROUP * tok), 1) % tok
    causal = key_pos <= query_pos
    for flip in range(slices):
        q_copies[flip].wait()
        g_copies[flip].wait()
        for h in range(width // HEAD_DIM):
            cols = slice(h * HEAD_DIM, (h + 1) * HEAD_DIM)
            heads = [
                slice((h * GROUP + a) * HEAD_DIM, (h * GROUP + a + 1) * HEAD_DIM)
                for a in range(GROUP)
            ]
            q4 = jnp.concatenate([q_buf[flip, :, c] for c in heads], axis=0)
            g4 = jnp.concatenate([g_buf[flip, :, c] for c in heads], axis=0)
            k2, v2 = [
                jnp.concatenate(
                    [
                        even_refs[flip][kind, :, cols] + odd_refs[flip][kind, :, cols],
                        own_refs[flip][kind, :, cols],
                    ],
                    axis=0,
                )
                for kind in range(2)
            ]
            dq_t, dk, dv = group_grads(q4, g4, k2, v2, bias, causal)
            for a in range(GROUP):
                dq_buf[flip, :, heads[a]] = dq_t[:, a * tok : (a + 1) * tok].T.astype(jnp.bfloat16)
            for kind, grad in enumerate((dk, dv)):
                prev_outs[flip][kind, :, cols] = grad[:tok].astype(jnp.bfloat16)
                own_outs[flip][kind, :, cols] = grad[tok:]
        dq_copies[flip].start()
    for copy in dq_copies:
        copy.wait()


def body(queries, grad_out, keys, values, key_first):
    shard_index = lax.axis_index("seq")
    slices = lax.axis_size("section")
    seen = (key_first < shard_index).astype(jnp.int32)
    place = lax.axis_index("section").astype(jnp.int32).reshape(1)
    pair = jnp.stack([keys, values])
    own = [pair] + [swapped(pair, "section", flip) for flip in range(1, slices)]
    from_even = [paired(part, 0, 1) for part in own]
    from_odd = [paired(part, 1, 1) for part in own]
    vmem = pl.BlockSpec(memory_space=pltpu.VMEM)
    smem = pl.BlockSpec(memory_space=pltpu.SMEM)
    hbm = pl.BlockSpec(memory_space=pl.ANY)
    chunk = pltpu.VMEM((slices, keys.shape[0], GROUP * keys.shape[1]), jnp.bfloat16)
    outs = pl.pallas_call(
        functools.partial(attention_kernel, slices),
        out_shape=[jax.ShapeDtypeStruct(queries.shape[1:], jnp.bfloat16)]
        + [jax.ShapeDtypeStruct(pair.shape, jnp.float32)] * slices
        + [jax.ShapeDtypeStruct(pair.shape, jnp.bfloat16)] * slices,
        in_specs=[smem, smem, hbm, hbm] + [vmem] * (3 * slices),
        out_specs=[hbm] + [vmem] * (2 * slices),
        scratch_shapes=[chunk] * 3 + [pltpu.SemaphoreType.DMA((slices,))] * 3,
        compiler_params=pltpu.CompilerParams(vmem_limit_bytes=40 * 1024 * 1024),
        name="attention_backward",
    )(seen, place, queries[0], grad_out[0], *own, *from_even, *from_odd)
    dq, own_grads, prev_grads = outs[0], outs[1 : slices + 1], outs[slices + 1 :]
    total = None
    for flip in reversed(range(slices)):
        later = jnp.where(
            shard_index % 2 == 0,
            seq_swapped(prev_grads[flip], 0),
            seq_swapped(prev_grads[flip], 1),
        )
        part = own_grads[flip] + later.astype(jnp.float32)
        if flip:
            part = swapped(part.astype(jnp.bfloat16), "section", flip).astype(jnp.float32)
        total = part if total is None else total + part
    return (dq[None], total[0], total[1])


def solution(mesh):
    placed = (
        P("section", "seq", None),
        P("section", "seq", None),
        P("seq", "section"),
        P("seq", "section"),
        P("seq"),
    )
    return jax.shard_map(
        body,
        mesh=mesh,
        in_specs=placed,
        out_specs=(P("section", "seq", None), P("seq", "section"), P("seq", "section")),
        check_vma=False,
    )
```

```python
import functools
import math

import jax
import jax.numpy as jnp
from jax import lax
from jax.experimental import pallas as pl
from jax.experimental.pallas import tpu as pltpu
from jax.sharding import PartitionSpec as P

HEADS = 32
KV_HEADS = 8
HEAD_DIM = 128
GROUP = HEADS // KV_HEADS
MASKED = -1e30
SCALE = 1.0 / math.sqrt(HEAD_DIM)
EXP2_SCALE = SCALE * math.log2(math.e)

NT = (((1,), (1,)), ((), ()))
NN = (((1,), (0,)), ((), ()))
TN = (((0,), (0,)), ((), ()))


def exchanged(x, partner_of):
    sections, shards = lax.axis_size("section"), lax.axis_size("seq")
    pairs = []
    for i in range(sections):
        for s in range(shards):
            j, t = partner_of(i, s, shards)
            pairs.append((i * shards + s, j * shards + t))
    return lax.ppermute(x, ("section", "seq"), pairs)


def swap_section(x, flip):
    return exchanged(x, lambda i, s, shards: (i ^ flip, s))


def swap_section_even(x, flip):
    return exchanged(x, lambda i, s, shards: (i if s % 2 else i ^ flip, s))


def swap_chip(x):
    return exchanged(x, lambda i, s, shards: (i, s ^ 1))


def swap_across(x):
    def partner_of(i, s, shards):
        t = s + 1 if s % 2 else s - 1
        return i, t if 0 <= t < shards else s

    return exchanged(x, partner_of)


def dot(a, b, dims):
    return lax.dot_general(a, b, dims, preferred_element_type=jnp.float32)


def group_grads(q4, g4, k2, v2, bias, causal):
    tok = k2.shape[0] // 2
    scores = dot(k2, q4, NT)
    dprob = dot(v2, g4, NT)
    s_prev = scores[:tok] + bias
    s_own = jnp.where(causal, scores[tok:], MASKED)
    top = jnp.maximum(
        jnp.max(s_prev, axis=0, keepdims=True), jnp.max(s_own, axis=0, keepdims=True)
    )
    s_all = jnp.concatenate([s_prev, s_own], axis=0)
    p = jnp.exp2((s_all - top) * EXP2_SCALE)
    total = jnp.sum(p, axis=0, keepdims=True)
    mixed = jnp.sum(p * dprob, axis=0, keepdims=True)
    inv = 1.0 / total
    row_dot = mixed * inv
    w = p * inv
    dscore = (w * (dprob - row_dot) * SCALE).astype(jnp.bfloat16)
    wround = w.astype(jnp.bfloat16)
    dk = dot(dscore, q4, NN)
    dv = dot(wround, g4, NN)
    dq_t = dot(k2, dscore, TN)
    return dq_t, dk, dv


def attention_kernel(slices, flags_ref, q_hbm, g_hbm, chip_ref, *refs):
    own_refs, spread_refs = refs[:slices], refs[slices : 2 * slices]
    dq_hbm, prev_all = refs[2 * slices : 2 * slices + 2]
    own_outs = refs[2 * slices + 2 : 3 * slices + 2]
    prev_outs = refs[3 * slices + 2 : 4 * slices + 1]
    prev_buf, q_buf, g_buf, dq_buf, q_sem, g_sem, dq_sem = refs[4 * slices + 1 :]
    _, tok, width = own_refs[0].shape
    q_width = width * GROUP
    seen, odd, place = flags_ref[0], flags_ref[1], flags_ref[2]
    spans = [
        pl.ds(pl.multiple_of((place ^ flip) * q_width, q_width), q_width)
        for flip in range(slices)
    ]
    q_copies, g_copies, dq_copies = [], [], []
    for flip, span in enumerate(spans):
        q_copies.append(pltpu.make_async_copy(q_hbm.at[:, span], q_buf.at[flip], q_sem.at[flip]))
        g_copies.append(pltpu.make_async_copy(g_hbm.at[:, span], g_buf.at[flip], g_sem.at[flip]))
        dq_copies.append(pltpu.make_async_copy(dq_buf.at[flip], dq_hbm.at[:, span], dq_sem.at[flip]))
        q_copies[flip].start()
        g_copies[flip].start()

    @pl.when(odd > 0)
    def _():
        prev_buf[...] = chip_ref[...]

    @pl.when(odd == 0)
    def _():
        for flip in range(slices):
            prev_buf[flip] = spread_refs[flip][...]

    bias = jnp.where(seen > 0, 0.0, MASKED).astype(jnp.float32)
    key_pos = lax.broadcasted_iota(jnp.int32, (tok, GROUP * tok), 0)
    query_pos = lax.broadcasted_iota(jnp.int32, (tok, GROUP * tok), 1) % tok
    causal = key_pos <= query_pos
    for flip in range(slices):
        q_copies[flip].wait()
        g_copies[flip].wait()
        for h in range(width // HEAD_DIM):
            cols = slice(h * HEAD_DIM, (h + 1) * HEAD_DIM)
            heads = [
                slice((h * GROUP + a) * HEAD_DIM, (h * GROUP + a + 1) * HEAD_DIM)
                for a in range(GROUP)
            ]
            q4 = jnp.concatenate([q_buf[flip, :, c] for c in heads], axis=0)
            g4 = jnp.concatenate([g_buf[flip, :, c] for c in heads], axis=0)
            k2, v2 = [
                jnp.concatenate([prev_buf[flip, kind, :, cols], own_refs[flip][kind, :, cols]], axis=0)
                for kind in range(2)
            ]
            dq_t, dk, dv = group_grads(q4, g4, k2, v2, bias, causal)
            for a in range(GROUP):
                dq_buf[flip, :, heads[a]] = dq_t[:, a * tok : (a + 1) * tok].T.astype(jnp.bfloat16)
            for kind, grad in enumerate((dk, dv)):
                earlier = grad[:tok].astype(jnp.bfloat16)
                prev_all[flip, kind, :, cols] = earlier
                if flip:
                    prev_outs[flip - 1][kind, :, cols] = earlier
                own_outs[flip][kind, :, cols] = grad[tok:]
        dq_copies[flip].start()
    for copy in dq_copies:
        copy.wait()


def body(queries, grad_out, keys, values, key_first):
    shard_index = lax.axis_index("seq")
    last_shard = lax.axis_size("seq") - 1
    slices = lax.axis_size("section")
    odd = shard_index % 2
    seen = key_first[0] < shard_index
    flags = jnp.stack([seen.astype(jnp.int32), odd, lax.axis_index("section")]).astype(jnp.int32)
    pair = jnp.stack([keys, values])
    across = swap_across(pair)
    order = sorted(range(1, slices), reverse=True)
    own, spread = {0: pair}, {0: across}
    for flip in order:
        own[flip] = swap_section(pair, flip)
    for flip in order:
        spread[flip] = swap_section_even(across, flip)
    chip = swap_chip(jnp.stack([own[flip] for flip in range(slices)]))
    vmem = pl.BlockSpec(memory_space=pltpu.VMEM)
    smem = pl.BlockSpec(memory_space=pltpu.SMEM)
    hbm = pl.BlockSpec(memory_space=pltpu.HBM)
    chunk = pltpu.VMEM((slices, keys.shape[0], GROUP * keys.shape[1]), jnp.bfloat16)
    outs = pl.pallas_call(
        functools.partial(attention_kernel, slices),
        out_shape=[
            jax.ShapeDtypeStruct(queries.shape[1:], jnp.bfloat16),
            jax.ShapeDtypeStruct(chip.shape, jnp.bfloat16),
        ]
        + [jax.ShapeDtypeStruct(pair.shape, jnp.float32)] * slices
        + [jax.ShapeDtypeStruct(pair.shape, jnp.bfloat16)] * (slices - 1),
        in_specs=[smem, hbm, hbm] + [vmem] * (1 + 2 * slices),
        out_specs=[hbm] + [vmem] * (2 * slices),
        scratch_shapes=[pltpu.VMEM(chip.shape, jnp.bfloat16)]
        + [chunk] * 3
        + [pltpu.SemaphoreType.DMA((slices,))] * 3,
        compiler_params=pltpu.CompilerParams(vmem_limit_bytes=40 * 1024 * 1024),
        name="attention_backward",
    )(
        flags,
        queries[0],
        grad_out[0],
        chip,
        *[own[flip] for flip in range(slices)],
        *[spread[flip] for flip in range(slices)],
    )
    dq, prev_all = outs[:2]
    own_grads, prev_grads = outs[2 : slices + 2], outs[slices + 2 :]
    early = prev_all[0].astype(jnp.float32)
    for flip in order:
        early = early + swap_section_even(prev_grads[flip - 1], flip).astype(jnp.float32)
    later = swap_chip(prev_all).astype(jnp.float32)
    parts = [
        own_grads[flip] + jnp.where(odd == 0, later[flip], 0.0) for flip in range(slices)
    ]
    total = parts[0]
    for flip in order:
        total = total + swap_section(parts[flip].astype(jnp.bfloat16), flip).astype(jnp.float32)
    landed = swap_across(early.astype(jnp.bfloat16)).astype(jnp.float32)
    total = total + jnp.where((odd == 1) & (shard_index < last_shard), landed, 0.0)
    return (dq[None], total[0], total[1])


def solution(mesh):
    placed = (
        P("section", "seq", None),
        P("section", "seq", None),
        P("seq", "section"),
        P("seq", "section"),
        P("seq"),
    )
    return jax.shard_map(
        body,
        mesh=mesh,
        in_specs=placed,
        out_specs=(P("section", "seq", None), P("seq", "section"), P("seq", "section")),
        check_vma=False,
    )
```

```python
import functools
import math

import jax
import jax.numpy as jnp
from jax import lax
from jax.experimental import pallas as pl
from jax.experimental.pallas import tpu as pltpu
from jax.sharding import PartitionSpec as P

HEADS = 32
KV_HEADS = 8
HEAD_DIM = 128
GROUP = HEADS // KV_HEADS
MASKED = -1e30
SCALE = 1.0 / math.sqrt(HEAD_DIM)
EXP2_SCALE = SCALE * math.log2(math.e)

NT = (((1,), (1,)), ((), ()))
NN = (((1,), (0,)), ((), ()))
TN = (((0,), (0,)), ((), ()))


def exchanged(x, partner_of):
    sections, shards = lax.axis_size("section"), lax.axis_size("seq")
    pairs = []
    for i in range(sections):
        for s in range(shards):
            j, t = partner_of(i, s, shards)
            pairs.append((i * shards + s, j * shards + t))
    return lax.ppermute(x, ("section", "seq"), pairs)


def swap_section(x, flip):
    return exchanged(x, lambda i, s, shards: (i ^ flip, s))


def rotate_seq(x, by):
    return exchanged(x, lambda i, s, shards: (i, (s + by) % shards))


def dot(a, b, dims):
    return lax.dot_general(a, b, dims, preferred_element_type=jnp.float32)


def group_grads(q4, g4, k2, v2, bias, causal):
    tok = k2.shape[0] // 2
    scores = dot(k2, q4, NT)
    dprob = dot(v2, g4, NT)
    s_prev = scores[:tok] + bias
    s_own = jnp.where(causal, scores[tok:], MASKED)
    top = jnp.maximum(
        jnp.max(s_prev, axis=0, keepdims=True), jnp.max(s_own, axis=0, keepdims=True)
    )
    s_all = jnp.concatenate([s_prev, s_own], axis=0)
    p = jnp.exp2((s_all - top) * EXP2_SCALE)
    total = jnp.sum(p, axis=0, keepdims=True)
    mixed = jnp.sum(p * dprob, axis=0, keepdims=True)
    inv = 1.0 / total
    row_dot = mixed * inv
    w = p * inv
    dscore = (w * (dprob - row_dot) * SCALE).astype(jnp.bfloat16)
    wround = w.astype(jnp.bfloat16)
    dk = dot(dscore, q4, NN)
    dv = dot(wround, g4, NN)
    dq_t = dot(k2, dscore, TN)
    return dq_t, dk, dv


def attention_kernel(slices, flags_ref, q_hbm, g_hbm, *refs):
    own_refs, prev_refs = refs[:slices], refs[slices : 2 * slices]
    dq_hbm = refs[2 * slices]
    own_outs, prev_outs = (refs[i * slices + 1 : (i + 1) * slices + 1] for i in (2, 3))
    q_buf, g_buf, dq_buf, q_sem, g_sem, dq_sem = refs[4 * slices + 1 :]
    _, tok, width = own_refs[0].shape
    q_width = width * GROUP
    seen, place = flags_ref[0], flags_ref[1]
    spans = [
        pl.ds(pl.multiple_of((place ^ flip) * q_width, q_width), q_width)
        for flip in range(slices)
    ]
    q_copies, g_copies, dq_copies = [], [], []
    for flip, span in enumerate(spans):
        q_copies.append(pltpu.make_async_copy(q_hbm.at[:, span], q_buf.at[flip], q_sem.at[flip]))
        g_copies.append(pltpu.make_async_copy(g_hbm.at[:, span], g_buf.at[flip], g_sem.at[flip]))
        dq_copies.append(pltpu.make_async_copy(dq_buf.at[flip], dq_hbm.at[:, span], dq_sem.at[flip]))
        q_copies[flip].start()
        g_copies[flip].start()
    bias = jnp.where(seen > 0, 0.0, MASKED).astype(jnp.float32)
    key_pos = lax.broadcasted_iota(jnp.int32, (tok, GROUP * tok), 0)
    query_pos = lax.broadcasted_iota(jnp.int32, (tok, GROUP * tok), 1) % tok
    causal = key_pos <= query_pos
    for flip in range(slices):
        q_copies[flip].wait()
        g_copies[flip].wait()
        for h in range(width // HEAD_DIM):
            cols = slice(h * HEAD_DIM, (h + 1) * HEAD_DIM)
            heads = [
                slice((h * GROUP + a) * HEAD_DIM, (h * GROUP + a + 1) * HEAD_DIM)
                for a in range(GROUP)
            ]
            q4 = jnp.concatenate([q_buf[flip, :, c] for c in heads], axis=0)
            g4 = jnp.concatenate([g_buf[flip, :, c] for c in heads], axis=0)
            k2, v2 = [
                jnp.concatenate([prev_refs[flip][kind, :, cols], own_refs[flip][kind, :, cols]], axis=0)
                for kind in range(2)
            ]
            dq_t, dk, dv = group_grads(q4, g4, k2, v2, bias, causal)
            for a in range(GROUP):
                dq_buf[flip, :, heads[a]] = dq_t[:, a * tok : (a + 1) * tok].T.astype(jnp.bfloat16)
            for kind, grad in enumerate((dk, dv)):
                prev_outs[flip][kind, :, cols] = grad[:tok].astype(jnp.bfloat16)
                own_outs[flip][kind, :, cols] = grad[tok:]
        dq_copies[flip].start()
    for copy in dq_copies:
        copy.wait()


def body(queries, grad_out, keys, values, key_first):
    slices = lax.axis_size("section")
    seen = key_first[0] < lax.axis_index("seq")
    flags = jnp.stack([seen.astype(jnp.int32), lax.axis_index("section").astype(jnp.int32)])
    pair = jnp.stack([keys, values])
    own = [pair] + [swap_section(pair, flip) for flip in range(1, slices)]
    prev = [rotate_seq(part, 1) for part in own]
    vmem = pl.BlockSpec(memory_space=pltpu.VMEM)
    smem = pl.BlockSpec(memory_space=pltpu.SMEM)
    hbm = pl.BlockSpec(memory_space=pltpu.HBM)
    chunk = pltpu.VMEM((slices, keys.shape[0], GROUP * keys.shape[1]), jnp.bfloat16)
    outs = pl.pallas_call(
        functools.partial(attention_kernel, slices),
        out_shape=[jax.ShapeDtypeStruct(queries.shape[1:], jnp.bfloat16)]
        + [jax.ShapeDtypeStruct(pair.shape, jnp.float32)] * slices
        + [jax.ShapeDtypeStruct(pair.shape, jnp.bfloat16)] * slices,
        in_specs=[smem, hbm, hbm] + [vmem] * (2 * slices),
        out_specs=[hbm] + [vmem] * (2 * slices),
        scratch_shapes=[chunk] * 3 + [pltpu.SemaphoreType.DMA((slices,))] * 3,
        compiler_params=pltpu.CompilerParams(vmem_limit_bytes=24 * 1024 * 1024),
        name="attention_backward",
    )(
        flags,
        pltpu.with_memory_space_constraint(queries[0], pltpu.HBM),
        pltpu.with_memory_space_constraint(grad_out[0], pltpu.HBM),
        *own,
        *prev,
    )
    dq, own_grads, prev_grads = outs[0], outs[1 : slices + 1], outs[slices + 1 :]
    total = None
    for flip in reversed(range(slices)):
        part = own_grads[flip] + rotate_seq(prev_grads[flip], -1).astype(jnp.float32)
        if flip:
            part = swap_section(part.astype(jnp.bfloat16), flip).astype(jnp.float32)
        total = part if total is None else total + part
    return (dq[None], total[0], total[1])


def solution(mesh):
    placed = (
        P("section", "seq", None),
        P("section", "seq", None),
        P("seq", "section"),
        P("seq", "section"),
        P("seq"),
    )
    return jax.shard_map(
        body,
        mesh=mesh,
        in_specs=placed,
        out_specs=(P("section", "seq", None), P("seq", "section"), P("seq", "section")),
        check_vma=False,
    )
```

```python
import functools
import math

import jax
import jax.numpy as jnp
from jax import lax
from jax.experimental import pallas as pl
from jax.experimental.pallas import tpu as pltpu
from jax.sharding import PartitionSpec as P

HEADS = 32
KV_HEADS = 8
HEAD_DIM = 128
GROUP = HEADS // KV_HEADS
MASKED = -1e30
SCALE = 1.0 / math.sqrt(HEAD_DIM)
EXP2_SCALE = SCALE * math.log2(math.e)

NT = (((1,), (1,)), ((), ()))
NN = (((1,), (0,)), ((), ()))
TN = (((0,), (0,)), ((), ()))


def exchanged(x, partner_of):
    sections, shards = lax.axis_size("section"), lax.axis_size("seq")
    pairs = []
    for i in range(sections):
        for s in range(shards):
            j, t = partner_of(i, s, shards)
            pairs.append((i * shards + s, j * shards + t))
    return lax.ppermute(x, ("section", "seq"), pairs)


def swap_section(x, flip):
    return exchanged(x, lambda i, s, shards: (i ^ flip, s))


def rotate_seq(x, by):
    return exchanged(x, lambda i, s, shards: (i, (s + by) % shards))


def dot(a, b, dims):
    return lax.dot_general(a, b, dims, preferred_element_type=jnp.float32)


def group_grads(q4, g4, k2, v2, bias, causal):
    tok = k2.shape[0] // 2
    scores = dot(k2, q4, NT)
    dprob = dot(v2, g4, NT)
    s_prev = scores[:tok] + bias
    s_own = jnp.where(causal, scores[tok:], MASKED)
    top = jnp.maximum(
        jnp.max(s_prev, axis=0, keepdims=True), jnp.max(s_own, axis=0, keepdims=True)
    )
    s_all = jnp.concatenate([s_prev, s_own], axis=0)
    p = jnp.exp2((s_all - top) * EXP2_SCALE)
    total = jnp.sum(p, axis=0, keepdims=True)
    mixed = jnp.sum(p * dprob, axis=0, keepdims=True)
    inv = 1.0 / total
    row_dot = mixed * inv
    w = p * inv
    dscore = (w * (dprob - row_dot) * SCALE).astype(jnp.bfloat16)
    wround = w.astype(jnp.bfloat16)
    dk = dot(dscore, q4, NN)
    dv = dot(wround, g4, NN)
    dq_t = dot(k2, dscore, TN)
    return dq_t, dk, dv


def load_kernel(slices, flags_ref, q_hbm, g_hbm, *refs):
    q_outs, g_outs = refs[:slices], refs[slices : 2 * slices]
    bias_out, sems = refs[2 * slices :]
    place = flags_ref[1]
    width = q_outs[0].shape[1]
    copies = []
    for flip in range(slices):
        span = pl.ds(pl.multiple_of((place ^ flip) * width, width), width)
        copies.append(pltpu.make_async_copy(q_hbm.at[:, span], q_outs[flip], sems.at[0, flip]))
        copies.append(pltpu.make_async_copy(g_hbm.at[:, span], g_outs[flip], sems.at[1, flip]))
    for copy in copies:
        copy.start()
    bias_out[...] = jnp.full(bias_out.shape, jnp.where(flags_ref[0] > 0, 0.0, MASKED), jnp.float32)
    for copy in copies:
        copy.wait()


def store_kernel(slices, flags_ref, *refs):
    dq_ins, dq_hbm, sems = refs[:slices], refs[slices], refs[slices + 1]
    place = flags_ref[1]
    width = dq_ins[0].shape[1]
    copies = []
    for flip in range(slices):
        span = pl.ds(pl.multiple_of((place ^ flip) * width, width), width)
        copies.append(pltpu.make_async_copy(dq_ins[flip], dq_hbm.at[:, span], sems.at[flip]))
    for copy in copies:
        copy.start()
    for copy in copies:
        copy.wait()


def attention_kernel(bias_ref, q_ref, g_ref, own_ref, prev_ref, bias_out, dq_out, own_out, prev_out):
    _, tok, width = own_ref.shape
    bias_out[...] = bias_ref[...]
    bias = bias_ref[0:1, 0:1]
    key_pos = lax.broadcasted_iota(jnp.int32, (tok, GROUP * tok), 0)
    query_pos = lax.broadcasted_iota(jnp.int32, (tok, GROUP * tok), 1) % tok
    causal = key_pos <= query_pos
    for h in range(width // HEAD_DIM):
        cols = slice(h * HEAD_DIM, (h + 1) * HEAD_DIM)
        heads = [
            slice((h * GROUP + a) * HEAD_DIM, (h * GROUP + a + 1) * HEAD_DIM)
            for a in range(GROUP)
        ]
        q4 = jnp.concatenate([q_ref[:, c] for c in heads], axis=0)
        g4 = jnp.concatenate([g_ref[:, c] for c in heads], axis=0)
        k2, v2 = [
            jnp.concatenate([prev_ref[kind, :, cols], own_ref[kind, :, cols]], axis=0)
            for kind in range(2)
        ]
        dq_t, dk, dv = group_grads(q4, g4, k2, v2, bias, causal)
        for a in range(GROUP):
            dq_out[:, heads[a]] = dq_t[:, a * tok : (a + 1) * tok].T.astype(jnp.bfloat16)
        for kind, grad in enumerate((dk, dv)):
            prev_out[kind, :, cols] = grad[:tok].astype(jnp.bfloat16)
            own_out[kind, :, cols] = grad[tok:]


def body(queries, grad_out, keys, values, key_first):
    slices = lax.axis_size("section")
    tok, width = keys.shape
    q_width = GROUP * width
    seen = key_first[0] < lax.axis_index("seq")
    flags = jnp.stack([seen.astype(jnp.int32), lax.axis_index("section").astype(jnp.int32)])
    vmem = pl.BlockSpec(memory_space=pltpu.VMEM)
    smem = pl.BlockSpec(memory_space=pltpu.SMEM)
    hbm = pl.BlockSpec(memory_space=pltpu.HBM)
    params = pltpu.CompilerParams(vmem_limit_bytes=16 * 1024 * 1024)
    q_slice = jax.ShapeDtypeStruct((tok, q_width), jnp.bfloat16)
    tile = jax.ShapeDtypeStruct((8, 128), jnp.float32)

    pair = jnp.stack([keys, values])
    loaded = pl.pallas_call(
        functools.partial(load_kernel, slices),
        out_shape=[q_slice] * (2 * slices) + [tile],
        in_specs=[smem, hbm, hbm],
        out_specs=[vmem] * (2 * slices + 1),
        scratch_shapes=[pltpu.SemaphoreType.DMA((2, slices))],
        compiler_params=params,
        name="load_slices",
    )(
        flags,
        pltpu.with_memory_space_constraint(queries[0], pltpu.HBM),
        pltpu.with_memory_space_constraint(grad_out[0], pltpu.HBM),
    )
    bias = loaded[-1]
    total, dq_parts = None, []
    for flip in range(slices):
        own = swap_section(pair, flip) if flip else pair
        prev = rotate_seq(own, 1)
        bias, dq_part, own_grads, prev_grads = pl.pallas_call(
            attention_kernel,
            out_shape=[
                tile,
                q_slice,
                jax.ShapeDtypeStruct(pair.shape, jnp.float32),
                jax.ShapeDtypeStruct(pair.shape, jnp.bfloat16),
            ],
            in_specs=[vmem] * 5,
            out_specs=[vmem] * 4,
            compiler_params=params,
            name="attention_backward",
        )(bias, loaded[flip], loaded[slices + flip], own, prev)
        dq_parts.append(dq_part)
        part = own_grads + rotate_seq(prev_grads, -1).astype(jnp.float32)
        if flip:
            part = swap_section(part.astype(jnp.bfloat16), flip).astype(jnp.float32)
        total = part if total is None else total + part
    dq = pl.pallas_call(
        functools.partial(store_kernel, slices),
        out_shape=jax.ShapeDtypeStruct(queries.shape[1:], jnp.bfloat16),
        in_specs=[smem] + [vmem] * slices,
        out_specs=hbm,
        scratch_shapes=[pltpu.SemaphoreType.DMA((slices,))],
        compiler_params=params,
        name="store_slices",
    )(flags, *dq_parts)
    return (dq[None], total[0], total[1])


def solution(mesh):
    placed = (
        P("section", "seq", None),
        P("section", "seq", None),
        P("seq", "section"),
        P("seq", "section"),
        P("seq"),
    )
    return jax.shard_map(
        body,
        mesh=mesh,
        in_specs=placed,
        out_specs=(P("section", "seq", None), P("seq", "section"), P("seq", "section")),
        check_vma=False,
    )
```

```python
import functools
import math

import jax
import jax.numpy as jnp
from jax import lax
from jax.experimental import pallas as pl
from jax.experimental.pallas import tpu as pltpu
from jax.sharding import PartitionSpec as P

HEADS = 32
KV_HEADS = 8
HEAD_DIM = 128
GROUP = HEADS // KV_HEADS
MASKED = -1e30
SCALE = 1.0 / math.sqrt(HEAD_DIM)
EXP2_SCALE = SCALE * math.log2(math.e)

NT = (((1,), (1,)), ((), ()))
NN = (((1,), (0,)), ((), ()))
TN = (((0,), (0,)), ((), ()))


def exchanged(x, partner_of):
    sections, shards = lax.axis_size("section"), lax.axis_size("seq")
    pairs = []
    for i in range(sections):
        for s in range(shards):
            j, t = partner_of(i, s, shards)
            pairs.append((i * shards + s, j * shards + t))
    return lax.ppermute(x, ("section", "seq"), pairs)


def swap_section(x, flip):
    return exchanged(x, lambda i, s, shards: (i ^ flip, s))


def rotate_seq(x, by):
    return exchanged(x, lambda i, s, shards: (i, (s + by) % shards))


def dot(a, b, dims):
    return lax.dot_general(a, b, dims, preferred_element_type=jnp.float32)


def group_grads(q4, g4, k2, v2, bias, causal):
    tok = k2.shape[0] // 2
    scores = dot(k2, q4, NT)
    dprob = dot(v2, g4, NT)
    s_prev = scores[:tok] + bias
    s_own = jnp.where(causal, scores[tok:], MASKED)
    top = jnp.maximum(
        jnp.max(s_prev, axis=0, keepdims=True), jnp.max(s_own, axis=0, keepdims=True)
    )
    s_all = jnp.concatenate([s_prev, s_own], axis=0)
    p = jnp.exp2((s_all - top) * EXP2_SCALE)
    total = jnp.sum(p, axis=0, keepdims=True)
    mixed = jnp.sum(p * dprob, axis=0, keepdims=True)
    inv = 1.0 / total
    row_dot = mixed * inv
    w = p * inv
    dscore = (w * (dprob - row_dot) * SCALE).astype(jnp.bfloat16)
    wround = w.astype(jnp.bfloat16)
    dk = dot(dscore, q4, NN)
    dv = dot(wround, g4, NN)
    dq_t = dot(k2, dscore, TN)
    return dq_t, dk, dv


def load_kernel(slices, first_ref, q_hbm, g_hbm, *refs):
    q_outs, g_outs = refs[:slices], refs[slices : 2 * slices]
    bias_out, sems = refs[2 * slices :]
    place = lax.axis_index("section")
    width = q_outs[0].shape[1]
    copies = []
    for flip in range(slices):
        span = pl.ds(pl.multiple_of((place ^ flip) * width, width), width)
        copies.append(pltpu.make_async_copy(q_hbm.at[:, span], q_outs[flip], sems.at[0, flip]))
        copies.append(pltpu.make_async_copy(g_hbm.at[:, span], g_outs[flip], sems.at[1, flip]))
    for copy in copies:
        copy.start()
    seen = first_ref[0] < lax.axis_index("seq")
    bias_out[...] = jnp.full(bias_out.shape, jnp.where(seen, 0.0, MASKED), jnp.float32)
    for copy in copies:
        copy.wait()


def store_kernel(slices, *refs):
    dq_ins, dq_hbm, sems = refs[:slices], refs[slices], refs[slices + 1]
    place = lax.axis_index("section")
    width = dq_ins[0].shape[1]
    copies = []
    for flip in range(slices):
        span = pl.ds(pl.multiple_of((place ^ flip) * width, width), width)
        copies.append(pltpu.make_async_copy(dq_ins[flip], dq_hbm.at[:, span], sems.at[flip]))
    for copy in copies:
        copy.start()
    for copy in copies:
        copy.wait()


def attention_kernel(bias_ref, q_ref, g_ref, own_ref, prev_ref, bias_out, dq_out, own_out, prev_out):
    _, tok, width = own_ref.shape
    bias_out[...] = bias_ref[...]
    bias = bias_ref[0:1, 0:1]
    key_pos = lax.broadcasted_iota(jnp.int32, (tok, GROUP * tok), 0)
    query_pos = lax.broadcasted_iota(jnp.int32, (tok, GROUP * tok), 1) % tok
    causal = key_pos <= query_pos
    for h in range(width // HEAD_DIM):
        cols = slice(h * HEAD_DIM, (h + 1) * HEAD_DIM)
        heads = [
            slice((h * GROUP + a) * HEAD_DIM, (h * GROUP + a + 1) * HEAD_DIM)
            for a in range(GROUP)
        ]
        q4 = jnp.concatenate([q_ref[:, c] for c in heads], axis=0)
        g4 = jnp.concatenate([g_ref[:, c] for c in heads], axis=0)
        k2, v2 = [
            jnp.concatenate([prev_ref[kind, :, cols], own_ref[kind, :, cols]], axis=0)
            for kind in range(2)
        ]
        dq_t, dk, dv = group_grads(q4, g4, k2, v2, bias, causal)
        for a in range(GROUP):
            dq_out[:, heads[a]] = dq_t[:, a * tok : (a + 1) * tok].T.astype(jnp.bfloat16)
        for kind, grad in enumerate((dk, dv)):
            prev_out[kind, :, cols] = grad[:tok].astype(jnp.bfloat16)
            own_out[kind, :, cols] = grad[tok:]


def after(x, token):
    return lax.optimization_barrier((x, token))[0]


def body(queries, grad_out, keys, values, key_first):
    slices = lax.axis_size("section")
    tok, width = keys.shape
    q_width = GROUP * width
    vmem = pl.BlockSpec(memory_space=pltpu.VMEM)
    hbm = pl.BlockSpec(memory_space=pltpu.HBM)
    params = pltpu.CompilerParams(vmem_limit_bytes=16 * 1024 * 1024)
    q_slice = jax.ShapeDtypeStruct((tok, q_width), jnp.bfloat16)
    tile = jax.ShapeDtypeStruct((8, 128), jnp.float32)
    order = [0] + list(range(slices - 1, 0, -1))

    pair = jnp.stack([keys, values])
    own = {0: pair}
    for flip in order[1:]:
        own[flip] = swap_section(pair, flip)
    prev = {0: rotate_seq(pair, 1)}
    loaded = pl.pallas_call(
        functools.partial(load_kernel, slices),
        out_shape=[q_slice] * (2 * slices) + [tile],
        in_specs=[pl.BlockSpec(memory_space=pltpu.SMEM), hbm, hbm],
        out_specs=[vmem] * (2 * slices + 1),
        scratch_shapes=[pltpu.SemaphoreType.DMA((2, slices))],
        compiler_params=params,
        name="load_slices",
    )(
        key_first,
        pltpu.with_memory_space_constraint(queries[0], pltpu.HBM),
        pltpu.with_memory_space_constraint(grad_out[0], pltpu.HBM),
    )
    bias = loaded[-1]
    prev[order[1]] = rotate_seq(after(own[order[1]], bias), 1)
    total, dq_parts, parts = None, {}, []
    for step, flip in enumerate(order):
        if step >= 3:
            bias = after(bias, parts[step - 2])
        bias, dq_parts[flip], own_grads, prev_grads = pl.pallas_call(
            attention_kernel,
            out_shape=[
                tile,
                q_slice,
                jax.ShapeDtypeStruct(pair.shape, jnp.float32),
                jax.ShapeDtypeStruct(pair.shape, jnp.bfloat16),
            ],
            in_specs=[vmem] * 5,
            out_specs=[vmem] * 4,
            compiler_params=params,
            name="attention_backward",
        )(bias, loaded[flip], loaded[slices + flip], own[flip], prev[flip])
        if step == 0:
            for later in order[2:]:
                prev[later] = rotate_seq(after(own[later], bias), 1)
        part = own_grads + rotate_seq(prev_grads, -1).astype(jnp.float32)
        if flip:
            part = part.astype(jnp.bfloat16)
            parts.append(part)
            part = swap_section(part, flip).astype(jnp.float32)
        else:
            parts.append(part)
        total = part if total is None else total + part
    dq = pl.pallas_call(
        functools.partial(store_kernel, slices),
        out_shape=jax.ShapeDtypeStruct(queries.shape[1:], jnp.bfloat16),
        in_specs=[vmem] * slices,
        out_specs=hbm,
        scratch_shapes=[pltpu.SemaphoreType.DMA((slices,))],
        compiler_params=params,
        name="store_slices",
    )(*[dq_parts[flip] for flip in range(slices)])
    return (dq[None], total[0], total[1])


def solution(mesh):
    placed = (
        P("section", "seq", None),
        P("section", "seq", None),
        P("seq", "section"),
        P("seq", "section"),
        P("seq"),
    )
    return jax.shard_map(
        body,
        mesh=mesh,
        in_specs=placed,
        out_specs=(P("section", "seq", None), P("seq", "section"), P("seq", "section")),
        check_vma=False,
    )
```

```python
import functools
import math

import jax
import jax.numpy as jnp
from jax import lax
from jax.experimental import pallas as pl
from jax.experimental.pallas import tpu as pltpu
from jax.sharding import PartitionSpec as P

HEADS = 32
KV_HEADS = 8
HEAD_DIM = 128
GROUP = HEADS // KV_HEADS
MASKED = -1e30
SCALE = 1.0 / math.sqrt(HEAD_DIM)
EXP2_SCALE = SCALE * math.log2(math.e)

NT = (((1,), (1,)), ((), ()))
NN = (((1,), (0,)), ((), ()))
TN = (((0,), (0,)), ((), ()))


def exchanged(x, partner_of):
    sections, shards = lax.axis_size("section"), lax.axis_size("seq")
    pairs = []
    for i in range(sections):
        for s in range(shards):
            j, t = partner_of(i, s, shards)
            pairs.append((i * shards + s, j * shards + t))
    return lax.ppermute(x, ("section", "seq"), pairs)


def swap_section(x, flip):
    return exchanged(x, lambda i, s, shards: (i ^ flip, s))


def rotate_seq(x, by):
    return exchanged(x, lambda i, s, shards: (i, (s + by) % shards))


def dot(a, b, dims):
    return lax.dot_general(a, b, dims, preferred_element_type=jnp.float32)


def group_grads(q4, g4, k2, v2, bias, causal):
    tok = k2.shape[0] // 2
    scores = dot(k2, q4, NT)
    dprob = dot(v2, g4, NT)
    s_prev = scores[:tok] + bias
    s_own = jnp.where(causal, scores[tok:], MASKED)
    top = jnp.maximum(
        jnp.max(s_prev, axis=0, keepdims=True), jnp.max(s_own, axis=0, keepdims=True)
    )
    s_all = jnp.concatenate([s_prev, s_own], axis=0)
    p = jnp.exp2((s_all - top) * EXP2_SCALE)
    total = jnp.sum(p, axis=0, keepdims=True)
    mixed = jnp.sum(p * dprob, axis=0, keepdims=True)
    inv = 1.0 / total
    row_dot = mixed * inv
    w = p * inv
    dscore = (w * (dprob - row_dot) * SCALE).astype(jnp.bfloat16)
    wround = w.astype(jnp.bfloat16)
    dk = dot(dscore, q4, NN)
    dv = dot(wround, g4, NN)
    dq_t = dot(k2, dscore, TN)
    return dq_t, dk, dv


def load_kernel(slices, first_ref, q_hbm, g_hbm, *refs):
    q_outs, g_outs = refs[:slices], refs[slices : 2 * slices]
    bias_out, sems = refs[2 * slices :]
    place = lax.axis_index("section")
    width = q_outs[0].shape[1]
    copies = []
    for flip in range(slices):
        span = pl.ds(pl.multiple_of((place ^ flip) * width, width), width)
        copies.append(pltpu.make_async_copy(q_hbm.at[:, span], q_outs[flip], sems.at[0, flip]))
        copies.append(pltpu.make_async_copy(g_hbm.at[:, span], g_outs[flip], sems.at[1, flip]))
    for copy in copies:
        copy.start()
    seen = first_ref[0] < lax.axis_index("seq")
    bias_out[...] = jnp.full(bias_out.shape, jnp.where(seen, 0.0, MASKED), jnp.float32)
    for copy in copies:
        copy.wait()


def store_kernel(slices, *refs):
    dq_ins, dq_hbm, sems = refs[:slices], refs[slices], refs[slices + 1]
    place = lax.axis_index("section")
    width = dq_ins[0].shape[1]
    copies = []
    for flip in range(slices):
        span = pl.ds(pl.multiple_of((place ^ flip) * width, width), width)
        copies.append(pltpu.make_async_copy(dq_ins[flip], dq_hbm.at[:, span], sems.at[flip]))
    for copy in copies:
        copy.start()
    for copy in copies:
        copy.wait()


def attention_kernel(bias_ref, q_ref, g_ref, own_ref, prev_ref, *outs):
    _, tok, width = own_ref.shape
    dq_out, own_out, prev_out = outs[-3:]
    for tile_out in outs[:-3]:
        tile_out[...] = bias_ref[...]
    bias = bias_ref[0:1, 0:1]
    key_pos = lax.broadcasted_iota(jnp.int32, (tok, GROUP * tok), 0)
    query_pos = lax.broadcasted_iota(jnp.int32, (tok, GROUP * tok), 1) % tok
    causal = key_pos <= query_pos
    for h in range(width // HEAD_DIM):
        cols = slice(h * HEAD_DIM, (h + 1) * HEAD_DIM)
        heads = [
            slice((h * GROUP + a) * HEAD_DIM, (h * GROUP + a + 1) * HEAD_DIM)
            for a in range(GROUP)
        ]
        q4 = jnp.concatenate([q_ref[:, c] for c in heads], axis=0)
        g4 = jnp.concatenate([g_ref[:, c] for c in heads], axis=0)
        k2, v2 = [
            jnp.concatenate([prev_ref[kind, :, cols], own_ref[kind, :, cols]], axis=0)
            for kind in range(2)
        ]
        dq_t, dk, dv = group_grads(q4, g4, k2, v2, bias, causal)
        for a in range(GROUP):
            dq_out[:, heads[a]] = dq_t[:, a * tok : (a + 1) * tok].T.astype(jnp.bfloat16)
        for kind, grad in enumerate((dk, dv)):
            prev_out[kind, :, cols] = grad[:tok].astype(jnp.bfloat16)
            own_out[kind, :, cols] = grad[tok:]


def after(x, token):
    return lax.optimization_barrier((x, token))[0]


def body(queries, grad_out, keys, values, key_first):
    slices = lax.axis_size("section")
    tok, width = keys.shape
    q_width = GROUP * width
    vmem = pl.BlockSpec(memory_space=pltpu.VMEM)
    hbm = pl.BlockSpec(memory_space=pltpu.HBM)
    params = pltpu.CompilerParams(vmem_limit_bytes=16 * 1024 * 1024)
    q_slice = jax.ShapeDtypeStruct((tok, q_width), jnp.bfloat16)
    tile = jax.ShapeDtypeStruct((8, 128), jnp.float32)
    order = list(range(slices - 1, -1, -1))

    pair = jnp.stack([keys, values])
    own = {flip: swap_section(pair, flip) for flip in order[:-1]}
    own[0] = pair
    prev = {0: rotate_seq(pair, 1)}
    loaded = pl.pallas_call(
        functools.partial(load_kernel, slices),
        out_shape=[q_slice] * (2 * slices) + [tile],
        in_specs=[pl.BlockSpec(memory_space=pltpu.SMEM), hbm, hbm],
        out_specs=[vmem] * (2 * slices + 1),
        scratch_shapes=[pltpu.SemaphoreType.DMA((2, slices))],
        compiler_params=params,
        name="load_slices",
    )(
        key_first,
        pltpu.with_memory_space_constraint(queries[0], pltpu.HBM),
        pltpu.with_memory_space_constraint(grad_out[0], pltpu.HBM),
    )
    bias = loaded[-1]
    prev[order[0]] = rotate_seq(after(own[order[0]], bias), 1)
    for flip in order[1:-1]:
        prev[flip] = rotate_seq(own[flip], 1)
    bias = after(bias, [prev[0]] + [own[flip] for flip in order])
    total, dq_parts, parts = None, {}, []
    nothing = pl.CostEstimate(flops=0, transcendentals=0, bytes_accessed=0)
    for step, flip in enumerate(order):
        last = step == slices - 1
        if step >= 2:
            bias = after(bias, parts[step - 2])
        *_, dq_parts[flip], own_grads, prev_grads = out = pl.pallas_call(
            attention_kernel,
            out_shape=[tile] * (not last)
            + [
                q_slice,
                jax.ShapeDtypeStruct(pair.shape, jnp.float32),
                jax.ShapeDtypeStruct(pair.shape, jnp.bfloat16),
            ],
            in_specs=[vmem] * 5,
            out_specs=[vmem] * (3 if last else 4),
            compiler_params=params,
            cost_estimate=nothing if step < slices - 2 else None,
            name="attention_backward",
        )(bias, loaded[flip], loaded[slices + flip], own[flip], prev[flip])
        bias = out[0]
        part = own_grads + rotate_seq(prev_grads, -1).astype(jnp.float32)
        if flip:
            part = part.astype(jnp.bfloat16)
            parts.append(part)
            part = swap_section(part, flip).astype(jnp.float32)
        total = part if total is None else total + part
    dq = pl.pallas_call(
        functools.partial(store_kernel, slices),
        out_shape=jax.ShapeDtypeStruct(queries.shape[1:], jnp.bfloat16),
        in_specs=[vmem] * slices,
        out_specs=hbm,
        scratch_shapes=[pltpu.SemaphoreType.DMA((slices,))],
        compiler_params=params,
        name="store_slices",
    )(*[dq_parts[flip] for flip in range(slices)])
    return (dq[None], total[0], total[1])


def solution(mesh):
    placed = (
        P("section", "seq", None),
        P("section", "seq", None),
        P("seq", "section"),
        P("seq", "section"),
        P("seq"),
    )
    return jax.shard_map(
        body,
        mesh=mesh,
        in_specs=placed,
        out_specs=(P("section", "seq", None), P("seq", "section"), P("seq", "section")),
        check_vma=False,
    )
```

```python
import functools
import math

import jax
import jax.numpy as jnp
from jax import lax
from jax.experimental import pallas as pl
from jax.experimental.pallas import tpu as pltpu
from jax.sharding import PartitionSpec as P

HEADS = 32
KV_HEADS = 8
HEAD_DIM = 128
GROUP = HEADS // KV_HEADS
MASKED = -1e30
SCALE = 1.0 / math.sqrt(HEAD_DIM)
EXP2_SCALE = SCALE * math.log2(math.e)

NT = (((1,), (1,)), ((), ()))
NN = (((1,), (0,)), ((), ()))
TN = (((0,), (0,)), ((), ()))


def exchanged(x, partner_of):
    sections, shards = lax.axis_size("section"), lax.axis_size("seq")
    pairs = []
    for i in range(sections):
        for s in range(shards):
            j, t = partner_of(i, s, shards)
            pairs.append((i * shards + s, j * shards + t))
    return lax.ppermute(x, ("section", "seq"), pairs)


def swap_section(x, flip):
    return exchanged(x, lambda i, s, shards: (i ^ flip, s))


def rotate_seq(x, by):
    return exchanged(x, lambda i, s, shards: (i, (s + by) % shards))


def dot(a, b, dims):
    return lax.dot_general(a, b, dims, preferred_element_type=jnp.float32)


def group_grads(q4, g4, k2, v2, bias, causal):
    tok = k2.shape[0] // 2
    scores = dot(k2, q4, NT)
    dprob = dot(v2, g4, NT)
    s_prev = scores[:tok] + bias
    s_own = jnp.where(causal, scores[tok:], MASKED)
    top = jnp.maximum(
        jnp.max(s_prev, axis=0, keepdims=True), jnp.max(s_own, axis=0, keepdims=True)
    )
    s_all = jnp.concatenate([s_prev, s_own], axis=0)
    p = jnp.exp2((s_all - top) * EXP2_SCALE)
    total = jnp.sum(p, axis=0, keepdims=True)
    mixed = jnp.sum(p * dprob, axis=0, keepdims=True)
    inv = 1.0 / total
    row_dot = mixed * inv
    w = p * inv
    dscore = (w * (dprob - row_dot) * SCALE).astype(jnp.bfloat16)
    wround = w.astype(jnp.bfloat16)
    dk = dot(dscore, q4, NN)
    dv = dot(wround, g4, NN)
    dq_t = dot(k2, dscore, TN)
    return dq_t, dk, dv


def load_kernel(slices, first_ref, q_hbm, g_hbm, *refs):
    q_outs, g_outs = refs[:slices], refs[slices : 2 * slices]
    bias_out, sems = refs[2 * slices :]
    place = lax.axis_index("section")
    width = q_outs[0].shape[1]
    copies = []
    for flip in range(slices):
        span = pl.ds(pl.multiple_of((place ^ flip) * width, width), width)
        copies.append(pltpu.make_async_copy(q_hbm.at[:, span], q_outs[flip], sems.at[0, flip]))
        copies.append(pltpu.make_async_copy(g_hbm.at[:, span], g_outs[flip], sems.at[1, flip]))
    for copy in copies:
        copy.start()
    seen = first_ref[0] < lax.axis_index("seq")
    bias_out[...] = jnp.full(bias_out.shape, jnp.where(seen, 0.0, MASKED), jnp.float32)
    for copy in copies:
        copy.wait()


def store_kernel(slices, *refs):
    dq_ins, dq_hbm, sems = refs[:slices], refs[slices], refs[slices + 1]
    place = lax.axis_index("section")
    width = dq_ins[0].shape[1]
    copies = []
    for flip in range(slices):
        span = pl.ds(pl.multiple_of((place ^ flip) * width, width), width)
        copies.append(pltpu.make_async_copy(dq_ins[flip], dq_hbm.at[:, span], sems.at[flip]))
    for copy in copies:
        copy.start()
    for copy in copies:
        copy.wait()


def attention_kernel(bias_ref, q_ref, g_ref, own_ref, prev_ref, *outs):
    _, tok, width = own_ref.shape
    dq_out, own_out, prev_out = outs[-3:]
    for tile_out in outs[:-3]:
        tile_out[...] = bias_ref[...]
    bias = bias_ref[0:1, 0:1]
    key_pos = lax.broadcasted_iota(jnp.int32, (tok, GROUP * tok), 0)
    query_pos = lax.broadcasted_iota(jnp.int32, (tok, GROUP * tok), 1) % tok
    causal = key_pos <= query_pos
    for h in range(width // HEAD_DIM):
        cols = slice(h * HEAD_DIM, (h + 1) * HEAD_DIM)
        heads = [
            slice((h * GROUP + a) * HEAD_DIM, (h * GROUP + a + 1) * HEAD_DIM)
            for a in range(GROUP)
        ]
        q4 = jnp.concatenate([q_ref[:, c] for c in heads], axis=0)
        g4 = jnp.concatenate([g_ref[:, c] for c in heads], axis=0)
        k2, v2 = [
            jnp.concatenate([prev_ref[kind, :, cols], own_ref[kind, :, cols]], axis=0)
            for kind in range(2)
        ]
        dq_t, dk, dv = group_grads(q4, g4, k2, v2, bias, causal)
        for a in range(GROUP):
            dq_out[:, heads[a]] = dq_t[:, a * tok : (a + 1) * tok].T.astype(jnp.bfloat16)
        for kind, grad in enumerate((dk, dv)):
            prev_out[kind, :, cols] = grad[:tok].astype(jnp.bfloat16)
            own_out[kind, :, cols] = grad[tok:]


def after(x, token):
    return lax.optimization_barrier((x, token))[0]


def body(queries, grad_out, keys, values, key_first):
    slices = lax.axis_size("section")
    tok, width = keys.shape
    q_width = GROUP * width
    vmem = pl.BlockSpec(memory_space=pltpu.VMEM)
    hbm = pl.BlockSpec(memory_space=pltpu.HBM)
    params = pltpu.CompilerParams(vmem_limit_bytes=16 * 1024 * 1024)
    q_slice = jax.ShapeDtypeStruct((tok, q_width), jnp.bfloat16)
    tile = jax.ShapeDtypeStruct((8, 128), jnp.float32)
    order = [0] + list(range(slices - 1, 0, -1))

    pair = jnp.stack([keys, values])
    own = {flip: swap_section(pair, flip) for flip in order[1:]}
    own[0] = pair
    prev = {0: rotate_seq(pair, 1)}
    loaded = pl.pallas_call(
        functools.partial(load_kernel, slices),
        out_shape=[q_slice] * (2 * slices) + [tile],
        in_specs=[pl.BlockSpec(memory_space=pltpu.SMEM), hbm, hbm],
        out_specs=[vmem] * (2 * slices + 1),
        scratch_shapes=[pltpu.SemaphoreType.DMA((2, slices))],
        compiler_params=params,
        name="load_slices",
    )(
        key_first,
        pltpu.with_memory_space_constraint(queries[0], pltpu.HBM),
        pltpu.with_memory_space_constraint(grad_out[0], pltpu.HBM),
    )
    bias = loaded[-1]
    prev[order[1]] = rotate_seq(after(own[order[1]], bias), 1)
    for flip in order[2:]:
        prev[flip] = rotate_seq(own[flip], 1)
    bias = after(bias, [own[flip] for flip in order])
    total, dq_parts, parts = None, {}, []
    for step, flip in enumerate(order):
        last = step == slices - 1
        *_, dq_parts[flip], own_grads, prev_grads = out = pl.pallas_call(
            attention_kernel,
            out_shape=[tile] * (not last)
            + [
                q_slice,
                jax.ShapeDtypeStruct(pair.shape, jnp.float32),
                jax.ShapeDtypeStruct(pair.shape, jnp.bfloat16),
            ],
            in_specs=[vmem] * 5,
            out_specs=[vmem] * (3 if last else 4),
            compiler_params=params,
            name="attention_backward",
        )(bias, loaded[flip], loaded[slices + flip], own[flip], prev[flip])
        bias = out[0]
        parts.append((own_grads, prev_grads))
    for flip, (own_grads, prev_grads) in zip(order[1:], parts[1:]):
        part = own_grads + rotate_seq(prev_grads, -1).astype(jnp.float32)
        part = part.astype(jnp.bfloat16)
        landed = swap_section(part, flip).astype(jnp.float32)
        first_landed = landed if total is None else first_landed
        total = landed if total is None else total + landed
    own_grads, prev_grads = parts[0]
    total = total + (own_grads + rotate_seq(after(prev_grads, (part, first_landed)), -1).astype(jnp.float32))
    dq = pl.pallas_call(
        functools.partial(store_kernel, slices),
        out_shape=jax.ShapeDtypeStruct(queries.shape[1:], jnp.bfloat16),
        in_specs=[vmem] * slices,
        out_specs=hbm,
        scratch_shapes=[pltpu.SemaphoreType.DMA((slices,))],
        compiler_params=params,
        name="store_slices",
    )(*[dq_parts[flip] for flip in range(slices)])
    return (dq[None], total[0], total[1])


def solution(mesh):
    placed = (
        P("section", "seq", None),
        P("section", "seq", None),
        P("seq", "section"),
        P("seq", "section"),
        P("seq"),
    )
    return jax.shard_map(
        body,
        mesh=mesh,
        in_specs=placed,
        out_specs=(P("section", "seq", None), P("seq", "section"), P("seq", "section")),
        check_vma=False,
    )
```

```python
import functools
import math

import jax
import jax.numpy as jnp
from jax import lax
from jax.experimental import pallas as pl
from jax.experimental.pallas import tpu as pltpu
from jax.sharding import PartitionSpec as P

HEADS = 32
KV_HEADS = 8
HEAD_DIM = 128
GROUP = HEADS // KV_HEADS
MASKED = -1e30
SCALE = 1.0 / math.sqrt(HEAD_DIM)
EXP2_SCALE = SCALE * math.log2(math.e)

NT = (((1,), (1,)), ((), ()))
NN = (((1,), (0,)), ((), ()))
TN = (((0,), (0,)), ((), ()))


def exchanged(x, partner_of):
    sections, shards = lax.axis_size("section"), lax.axis_size("seq")
    pairs = []
    for i in range(sections):
        for s in range(shards):
            j, t = partner_of(i, s, shards)
            pairs.append((i * shards + s, j * shards + t))
    return lax.ppermute(x, ("section", "seq"), pairs)


def swap_section(x, flip):
    return exchanged(x, lambda i, s, shards: (i ^ flip, s))


def rotate_seq(x, by):
    return exchanged(x, lambda i, s, shards: (i, (s + by) % shards))


def dot(a, b, dims):
    return lax.dot_general(a, b, dims, preferred_element_type=jnp.float32)


def group_grads(q4, g4, k2, v2, bias, causal):
    tok = k2.shape[0] // 2
    scores = dot(k2, q4, NT)
    dprob = dot(v2, g4, NT)
    s_prev = scores[:tok] + bias
    s_own = jnp.where(causal, scores[tok:], MASKED)
    top = jnp.maximum(
        jnp.max(s_prev, axis=0, keepdims=True), jnp.max(s_own, axis=0, keepdims=True)
    )
    s_all = jnp.concatenate([s_prev, s_own], axis=0)
    p = jnp.exp2((s_all - top) * EXP2_SCALE)
    total = jnp.sum(p, axis=0, keepdims=True)
    mixed = jnp.sum(p * dprob, axis=0, keepdims=True)
    inv = 1.0 / total
    row_dot = mixed * inv
    w = p * inv
    dscore = (w * (dprob - row_dot) * SCALE).astype(jnp.bfloat16)
    wround = w.astype(jnp.bfloat16)
    dk = dot(dscore, q4, NN)
    dv = dot(wround, g4, NN)
    dq_t = dot(k2, dscore, TN)
    return dq_t, dk, dv


def load_kernel(slices, first_ref, q_hbm, g_hbm, *refs):
    q_outs, g_outs = refs[:slices], refs[slices : 2 * slices]
    bias_out, sems = refs[2 * slices :]
    place = lax.axis_index("section")
    width = q_outs[0].shape[1]
    copies = []
    for flip in range(slices):
        span = pl.ds(pl.multiple_of((place ^ flip) * width, width), width)
        copies.append(pltpu.make_async_copy(q_hbm.at[:, span], q_outs[flip], sems.at[0, flip]))
        copies.append(pltpu.make_async_copy(g_hbm.at[:, span], g_outs[flip], sems.at[1, flip]))
    for copy in copies:
        copy.start()
    seen = first_ref[0] < lax.axis_index("seq")
    bias_out[...] = jnp.full(bias_out.shape, jnp.where(seen, 0.0, MASKED), jnp.float32)
    for copy in copies:
        copy.wait()


def store_kernel(slices, *refs):
    dq_ins, dq_hbm, sems = refs[:slices], refs[slices], refs[slices + 1]
    place = lax.axis_index("section")
    width = dq_ins[0].shape[1]
    copies = []
    for flip in range(slices):
        span = pl.ds(pl.multiple_of((place ^ flip) * width, width), width)
        copies.append(pltpu.make_async_copy(dq_ins[flip], dq_hbm.at[:, span], sems.at[flip]))
    for copy in copies:
        copy.start()
    for copy in copies:
        copy.wait()


def attention_kernel(bias_ref, q_ref, g_ref, own_ref, prev_ref, *refs):
    _, tok, width = own_ref.shape
    dq_out, own_out, prev_out = refs[-3:]
    for ref in refs[:-3]:
        if ref.dtype == jnp.float32:
            ref[...] = bias_ref[...]
        else:
            prev_out[1] = ref[...]
            prev_out = prev_out.at[0]
    bias = bias_ref[0:1, 0:1]
    key_pos = lax.broadcasted_iota(jnp.int32, (tok, GROUP * tok), 0)
    query_pos = lax.broadcasted_iota(jnp.int32, (tok, GROUP * tok), 1) % tok
    causal = key_pos <= query_pos
    for h in range(width // HEAD_DIM):
        cols = slice(h * HEAD_DIM, (h + 1) * HEAD_DIM)
        heads = [
            slice((h * GROUP + a) * HEAD_DIM, (h * GROUP + a + 1) * HEAD_DIM)
            for a in range(GROUP)
        ]
        q4 = jnp.concatenate([q_ref[:, c] for c in heads], axis=0)
        g4 = jnp.concatenate([g_ref[:, c] for c in heads], axis=0)
        k2, v2 = [
            jnp.concatenate([prev_ref[kind, :, cols], own_ref[kind, :, cols]], axis=0)
            for kind in range(2)
        ]
        dq_t, dk, dv = group_grads(q4, g4, k2, v2, bias, causal)
        for a in range(GROUP):
            dq_out[:, heads[a]] = dq_t[:, a * tok : (a + 1) * tok].T.astype(jnp.bfloat16)
        for kind, grad in enumerate((dk, dv)):
            prev_out[kind, :, cols] = grad[:tok].astype(jnp.bfloat16)
            own_out[kind, :, cols] = grad[tok:]


def after(x, token):
    return lax.optimization_barrier((x, token))[0]


def body(queries, grad_out, keys, values, key_first):
    slices = lax.axis_size("section")
    tok, width = keys.shape
    q_width = GROUP * width
    vmem = pl.BlockSpec(memory_space=pltpu.VMEM)
    hbm = pl.BlockSpec(memory_space=pltpu.HBM)
    params = pltpu.CompilerParams(vmem_limit_bytes=16 * 1024 * 1024)
    q_slice = jax.ShapeDtypeStruct((tok, q_width), jnp.bfloat16)
    tile = jax.ShapeDtypeStruct((8, 128), jnp.float32)
    order = [0] + list(range(slices - 1, 0, -1))

    pair = jnp.stack([keys, values])
    own = {flip: swap_section(pair, flip) for flip in order[1:]}
    own[0] = pair
    prev = {0: rotate_seq(pair, 1)}
    loaded = pl.pallas_call(
        functools.partial(load_kernel, slices),
        out_shape=[q_slice] * (2 * slices) + [tile],
        in_specs=[pl.BlockSpec(memory_space=pltpu.SMEM), hbm, hbm],
        out_specs=[vmem] * (2 * slices + 1),
        scratch_shapes=[pltpu.SemaphoreType.DMA((2, slices))],
        compiler_params=params,
        name="load_slices",
    )(
        key_first,
        pltpu.with_memory_space_constraint(queries[0], pltpu.HBM),
        pltpu.with_memory_space_constraint(grad_out[0], pltpu.HBM),
    )
    bias = loaded[-1]
    prev[order[1]] = rotate_seq(after(own[order[1]], bias), 1)
    for flip in order[2:]:
        prev[flip] = rotate_seq(own[flip], 1)
    bias = after(bias, [own[flip] for flip in order])
    total, dq_parts, own_grads, back = None, {}, {}, {}
    carry_step = slices - 2
    for step, flip in enumerate(order):
        last = step == slices - 1
        carried = [first_held] if step == carry_step else []
        held_shape = ((2,) if carried else ()) + pair.shape
        *_, dq_parts[flip], own_grads[flip], held = out = pl.pallas_call(
            attention_kernel,
            out_shape=[tile] * (not last)
            + [
                q_slice,
                jax.ShapeDtypeStruct(pair.shape, jnp.float32),
                jax.ShapeDtypeStruct(held_shape, jnp.bfloat16),
            ],
            in_specs=[vmem] * (5 + len(carried)),
            out_specs=[vmem] * (3 if last else 4),
            compiler_params=params,
            name="attention_backward",
        )(bias, loaded[flip], loaded[slices + flip], own[flip], prev[flip], *carried)
        bias = out[0]
        if step == 0:
            first_held = held
        elif carried:
            back[flip], back[0] = rotate_seq(held, -1)
        else:
            back[flip] = rotate_seq(held, -1)
    for flip in order[1:]:
        part = own_grads[flip] + back[flip].astype(jnp.float32)
        part = part.astype(jnp.bfloat16)
        landed = swap_section(part, flip).astype(jnp.float32)
        total = landed if total is None else total + landed
    total = total + (own_grads[0] + back[0].astype(jnp.float32))
    dq = pl.pallas_call(
        functools.partial(store_kernel, slices),
        out_shape=jax.ShapeDtypeStruct(queries.shape[1:], jnp.bfloat16),
        in_specs=[vmem] * slices,
        out_specs=hbm,
        scratch_shapes=[pltpu.SemaphoreType.DMA((slices,))],
        compiler_params=params,
        name="store_slices",
    )(*[dq_parts[flip] for flip in range(slices)])
    return (dq[None], total[0], total[1])


def solution(mesh):
    placed = (
        P("section", "seq", None),
        P("section", "seq", None),
        P("seq", "section"),
        P("seq", "section"),
        P("seq"),
    )
    return jax.shard_map(
        body,
        mesh=mesh,
        in_specs=placed,
        out_specs=(P("section", "seq", None), P("seq", "section"), P("seq", "section")),
        check_vma=False,
    )
```

```python
import functools
import math

import jax
import jax.numpy as jnp
from jax import lax
from jax.experimental import pallas as pl
from jax.experimental.pallas import tpu as pltpu
from jax.sharding import PartitionSpec as P

HEADS = 32
KV_HEADS = 8
HEAD_DIM = 128
GROUP = HEADS // KV_HEADS
MASKED = -1e30
SCALE = 1.0 / math.sqrt(HEAD_DIM)
EXP2_SCALE = SCALE * math.log2(math.e)

NT = (((1,), (1,)), ((), ()))
NN = (((1,), (0,)), ((), ()))
TN = (((0,), (0,)), ((), ()))


def exchanged(x, partner_of):
    sections, shards = lax.axis_size("section"), lax.axis_size("seq")
    pairs = []
    for i in range(sections):
        for s in range(shards):
            j, t = partner_of(i, s, shards)
            pairs.append((i * shards + s, j * shards + t))
    return lax.ppermute(x, ("section", "seq"), pairs)


def swap_section(x, flip):
    return exchanged(x, lambda i, s, shards: (i ^ flip, s))


def rotate_seq(x, by):
    return exchanged(x, lambda i, s, shards: (i, (s + by) % shards))


def dot(a, b, dims):
    return lax.dot_general(a, b, dims, preferred_element_type=jnp.float32)


def group_grads(q4, g4, k2, v2, bias, causal):
    tok = k2.shape[0] // 2
    scores = dot(k2, q4, NT)
    dprob = dot(v2, g4, NT)
    s_prev = scores[:tok] + bias
    s_own = jnp.where(causal, scores[tok:], MASKED)
    top = jnp.maximum(
        jnp.max(s_prev, axis=0, keepdims=True), jnp.max(s_own, axis=0, keepdims=True)
    )
    s_all = jnp.concatenate([s_prev, s_own], axis=0)
    p = jnp.exp2((s_all - top) * EXP2_SCALE)
    total = jnp.sum(p, axis=0, keepdims=True)
    mixed = jnp.sum(p * dprob, axis=0, keepdims=True)
    inv = 1.0 / total
    row_dot = mixed * inv
    w = p * inv
    dscore = (w * (dprob - row_dot) * SCALE).astype(jnp.bfloat16)
    wround = w.astype(jnp.bfloat16)
    dk = dot(dscore, q4, NN)
    dv = dot(wround, g4, NN)
    dq_t = dot(k2, dscore, TN)
    return dq_t, dk, dv


def load_kernel(slices, first_ref, q_hbm, g_hbm, *refs):
    q_outs, g_outs = refs[:slices], refs[slices : 2 * slices]
    bias_out, sems = refs[2 * slices :]
    place = lax.axis_index("section")
    width = q_outs[0].shape[1]
    copies = []
    for flip in range(slices):
        span = pl.ds(pl.multiple_of((place ^ flip) * width, width), width)
        copies.append(pltpu.make_async_copy(q_hbm.at[:, span], q_outs[flip], sems.at[0, flip]))
        copies.append(pltpu.make_async_copy(g_hbm.at[:, span], g_outs[flip], sems.at[1, flip]))
    for copy in copies:
        copy.start()
    seen = first_ref[0] < lax.axis_index("seq")
    bias_out[...] = jnp.full(bias_out.shape, jnp.where(seen, 0.0, MASKED), jnp.float32)
    for copy in copies:
        copy.wait()


def store_kernel(slices, *refs):
    dq_ins, dq_hbm, sems = refs[:slices], refs[slices], refs[slices + 1]
    place = lax.axis_index("section")
    width = dq_ins[0].shape[1]
    copies = []
    for flip in range(slices):
        span = pl.ds(pl.multiple_of((place ^ flip) * width, width), width)
        copies.append(pltpu.make_async_copy(dq_ins[flip], dq_hbm.at[:, span], sems.at[flip]))
    for copy in copies:
        copy.start()
    for copy in copies:
        copy.wait()


def attention_kernel(bias_ref, q_ref, g_ref, own_ref, prev_ref, *refs):
    _, tok, width = own_ref.shape
    dq_out, own_out, prev_out = refs[-3:]
    for ref in refs[:-3]:
        if ref.dtype == jnp.float32:
            ref[...] = bias_ref[...]
        else:
            prev_out[1] = ref[...]
            prev_out = prev_out.at[0]
    bias = bias_ref[0:1, 0:1]
    key_pos = lax.broadcasted_iota(jnp.int32, (tok, GROUP * tok), 0)
    query_pos = lax.broadcasted_iota(jnp.int32, (tok, GROUP * tok), 1) % tok
    causal = key_pos <= query_pos
    for h in range(width // HEAD_DIM):
        cols = slice(h * HEAD_DIM, (h + 1) * HEAD_DIM)
        heads = [
            slice((h * GROUP + a) * HEAD_DIM, (h * GROUP + a + 1) * HEAD_DIM)
            for a in range(GROUP)
        ]
        q4 = jnp.concatenate([q_ref[:, c] for c in heads], axis=0)
        g4 = jnp.concatenate([g_ref[:, c] for c in heads], axis=0)
        k2, v2 = [
            jnp.concatenate([prev_ref[kind, :, cols], own_ref[kind, :, cols]], axis=0)
            for kind in range(2)
        ]
        dq_t, dk, dv = group_grads(q4, g4, k2, v2, bias, causal)
        for a in range(GROUP):
            dq_out[:, heads[a]] = dq_t[:, a * tok : (a + 1) * tok].T.astype(jnp.bfloat16)
        for kind, grad in enumerate((dk, dv)):
            prev_out[kind, :, cols] = grad[:tok].astype(jnp.bfloat16)
            own_out[kind, :, cols] = grad[tok:]


def after(x, token):
    return lax.optimization_barrier((x, token))[0]


def body(queries, grad_out, keys, values, key_first):
    slices = lax.axis_size("section")
    tok, width = keys.shape
    q_width = GROUP * width
    vmem = pl.BlockSpec(memory_space=pltpu.VMEM)
    hbm = pl.BlockSpec(memory_space=pltpu.HBM)
    params = pltpu.CompilerParams(vmem_limit_bytes=16 * 1024 * 1024)
    q_slice = jax.ShapeDtypeStruct((tok, q_width), jnp.bfloat16)
    tile = jax.ShapeDtypeStruct((8, 128), jnp.float32)
    order = [0] + list(range(slices - 1, 0, -1))

    pair = jnp.stack([keys, values])
    own = {flip: swap_section(pair, flip) for flip in order[1:]}
    own[0] = pair
    prev = {0: rotate_seq(pair, 1)}
    loaded = pl.pallas_call(
        functools.partial(load_kernel, slices),
        out_shape=[q_slice] * (2 * slices) + [tile],
        in_specs=[pl.BlockSpec(memory_space=pltpu.SMEM), hbm, hbm],
        out_specs=[vmem] * (2 * slices + 1),
        scratch_shapes=[pltpu.SemaphoreType.DMA((2, slices))],
        compiler_params=params,
        name="load_slices",
    )(
        key_first,
        pltpu.with_memory_space_constraint(queries[0], pltpu.HBM),
        pltpu.with_memory_space_constraint(grad_out[0], pltpu.HBM),
    )
    bias = loaded[-1]
    prev[order[1]] = rotate_seq(after(own[order[1]], bias), 1)
    for flip in order[2:]:
        prev[flip] = rotate_seq(own[flip], 1)
    bias = after(bias, [own[flip] for flip in order])
    total, dq_parts, own_grads, back = None, {}, {}, {}
    carry_step = slices - 1
    for step, flip in enumerate(order):
        last = step == slices - 1
        carried = [first_held] if step == carry_step else []
        held_shape = ((2,) if carried else ()) + pair.shape
        *_, dq_parts[flip], own_grads[flip], held = out = pl.pallas_call(
            attention_kernel,
            out_shape=[tile] * (not last)
            + [
                q_slice,
                jax.ShapeDtypeStruct(pair.shape, jnp.float32),
                jax.ShapeDtypeStruct(held_shape, jnp.bfloat16),
            ],
            in_specs=[vmem] * (5 + len(carried)),
            out_specs=[vmem] * (3 if last else 4),
            compiler_params=params,
            name="attention_backward",
        )(bias, loaded[flip], loaded[slices + flip], own[flip], prev[flip], *carried)
        bias = out[0]
        if step == 0:
            first_held = held
        elif carried:
            back[flip], back[0] = rotate_seq(held, -1)
        else:
            back[flip] = rotate_seq(held, -1)
    for flip in order[1:]:
        part = own_grads[flip] + back[flip].astype(jnp.float32)
        part = part.astype(jnp.bfloat16)
        landed = swap_section(part, flip).astype(jnp.float32)
        total = landed if total is None else total + landed
    total = total + (own_grads[0] + back[0].astype(jnp.float32))
    dq = pl.pallas_call(
        functools.partial(store_kernel, slices),
        out_shape=jax.ShapeDtypeStruct(queries.shape[1:], jnp.bfloat16),
        in_specs=[vmem] * slices,
        out_specs=hbm,
        scratch_shapes=[pltpu.SemaphoreType.DMA((slices,))],
        compiler_params=params,
        name="store_slices",
    )(*[dq_parts[flip] for flip in range(slices)])
    return (dq[None], total[0], total[1])


def solution(mesh):
    placed = (
        P("section", "seq", None),
        P("section", "seq", None),
        P("seq", "section"),
        P("seq", "section"),
        P("seq"),
    )
    return jax.shard_map(
        body,
        mesh=mesh,
        in_specs=placed,
        out_specs=(P("section", "seq", None), P("seq", "section"), P("seq", "section")),
        check_vma=False,
    )
```

```python
import functools
import math

import jax
import jax.numpy as jnp
from jax import lax
from jax.experimental import pallas as pl
from jax.experimental.pallas import tpu as pltpu
from jax.sharding import PartitionSpec as P

HEADS = 32
KV_HEADS = 8
HEAD_DIM = 128
GROUP = HEADS // KV_HEADS
MASKED = -1e30
SCALE = 1.0 / math.sqrt(HEAD_DIM)
EXP2_SCALE = SCALE * math.log2(math.e)

NT = (((1,), (1,)), ((), ()))
NN = (((1,), (0,)), ((), ()))
TN = (((0,), (0,)), ((), ()))


def exchanged(x, partner_of):
    sections, shards = lax.axis_size("section"), lax.axis_size("seq")
    pairs = []
    for i in range(sections):
        for s in range(shards):
            j, t = partner_of(i, s, shards)
            pairs.append((i * shards + s, j * shards + t))
    return lax.ppermute(x, ("section", "seq"), pairs)


def swap_section(x, flip):
    return exchanged(x, lambda i, s, shards: (i ^ flip, s))


def rotate_seq(x, by):
    return exchanged(x, lambda i, s, shards: (i, (s + by) % shards))


def dot(a, b, dims):
    return lax.dot_general(a, b, dims, preferred_element_type=jnp.float32)


def group_grads(q4, g4, k2, v2, bias, causal):
    tok = k2.shape[0] // 2
    scores = dot(k2, q4, NT)
    dprob = dot(v2, g4, NT)
    dscores, wrounds = [], []
    for a in range(GROUP):
        head = slice(a * tok, (a + 1) * tok)
        s_prev = scores[:tok, head] + bias
        s_own = jnp.where(causal, scores[tok:, head], MASKED)
        top = jnp.max(jnp.maximum(s_prev, s_own), axis=0, keepdims=True)
        p_prev = jnp.exp2((s_prev - top) * EXP2_SCALE)
        p_own = jnp.exp2((s_own - top) * EXP2_SCALE)
        d_prev, d_own = dprob[:tok, head], dprob[tok:, head]
        inv = 1.0 / jnp.sum(p_prev + p_own, axis=0, keepdims=True)
        row_dot = jnp.sum(p_prev * d_prev + p_own * d_own, axis=0, keepdims=True) * inv
        w_prev, w_own = p_prev * inv, p_own * inv
        dscores.append(
            jnp.concatenate(
                [
                    (w_prev * (d_prev - row_dot) * SCALE).astype(jnp.bfloat16),
                    (w_own * (d_own - row_dot) * SCALE).astype(jnp.bfloat16),
                ],
                axis=0,
            )
        )
        wrounds.append(
            jnp.concatenate([w_prev.astype(jnp.bfloat16), w_own.astype(jnp.bfloat16)], axis=0)
        )
    dscore = jnp.concatenate(dscores, axis=1)
    wround = jnp.concatenate(wrounds, axis=1)
    dk = dot(dscore, q4, NN)
    dv = dot(wround, g4, NN)
    dq_t = dot(k2, dscore, TN).astype(jnp.bfloat16)
    return dq_t, dk, dv


def load_kernel(slices, first_ref, q_hbm, g_hbm, *refs):
    q_outs, g_outs = refs[:slices], refs[slices : 2 * slices]
    bias_out, sems = refs[2 * slices :]
    place = lax.axis_index("section")
    width = q_outs[0].shape[1]
    copies = []
    for flip in range(slices):
        span = pl.ds(pl.multiple_of((place ^ flip) * width, width), width)
        copies.append(pltpu.make_async_copy(q_hbm.at[:, span], q_outs[flip], sems.at[0, flip]))
        copies.append(pltpu.make_async_copy(g_hbm.at[:, span], g_outs[flip], sems.at[1, flip]))
    for copy in copies:
        copy.start()
    seen = first_ref[0] < lax.axis_index("seq")
    bias_out[...] = jnp.full(bias_out.shape, jnp.where(seen, 0.0, MASKED), jnp.float32)
    for copy in copies:
        copy.wait()


def store_kernel(slices, *refs):
    dq_ins, dq_hbm, sems = refs[:slices], refs[slices], refs[slices + 1]
    place = lax.axis_index("section")
    width = dq_ins[0].shape[1]
    copies = []
    for flip in range(slices):
        span = pl.ds(pl.multiple_of((place ^ flip) * width, width), width)
        copies.append(pltpu.make_async_copy(dq_ins[flip], dq_hbm.at[:, span], sems.at[flip]))
    for copy in copies:
        copy.start()
    for copy in copies:
        copy.wait()


def attention_kernel(bias_ref, q_ref, g_ref, own_ref, prev_ref, *refs):
    _, tok, width = own_ref.shape
    dq_out, own_out, prev_out = refs[-3:]
    for ref in refs[:-3]:
        if ref.dtype == jnp.float32:
            ref[...] = bias_ref[...]
        else:
            prev_out[1] = ref[...]
            prev_out = prev_out.at[0]
    bias = bias_ref[0:1, 0:1]
    key_pos = lax.broadcasted_iota(jnp.int32, (tok, tok), 0)
    query_pos = lax.broadcasted_iota(jnp.int32, (tok, tok), 1)
    causal = key_pos <= query_pos
    for h in range(width // HEAD_DIM):
        cols = slice(h * HEAD_DIM, (h + 1) * HEAD_DIM)
        heads = [
            slice((h * GROUP + a) * HEAD_DIM, (h * GROUP + a + 1) * HEAD_DIM)
            for a in range(GROUP)
        ]
        q4 = jnp.concatenate([q_ref[:, c] for c in heads], axis=0)
        g4 = jnp.concatenate([g_ref[:, c] for c in heads], axis=0)
        k2, v2 = [
            jnp.concatenate([prev_ref[kind, :, cols], own_ref[kind, :, cols]], axis=0)
            for kind in range(2)
        ]
        dq_t, dk, dv = group_grads(q4, g4, k2, v2, bias, causal)
        for a in range(GROUP):
            dq_out[:, heads[a]] = dq_t[:, a * tok : (a + 1) * tok].T
        for kind, grad in enumerate((dk, dv)):
            prev_out[kind, :, cols] = grad[:tok].astype(jnp.bfloat16)
            own_out[kind, :, cols] = grad[tok:]


def after(x, token):
    return lax.optimization_barrier((x, token))[0]


def body(queries, grad_out, keys, values, key_first):
    slices = lax.axis_size("section")
    tok, width = keys.shape
    q_width = GROUP * width
    vmem = pl.BlockSpec(memory_space=pltpu.VMEM)
    hbm = pl.BlockSpec(memory_space=pltpu.HBM)
    params = pltpu.CompilerParams(vmem_limit_bytes=16 * 1024 * 1024)
    q_slice = jax.ShapeDtypeStruct((tok, q_width), jnp.bfloat16)
    tile = jax.ShapeDtypeStruct((8, 128), jnp.float32)
    order = [0] + list(range(slices - 1, 0, -1))

    pair = jnp.stack([keys, values])
    own = {flip: swap_section(pair, flip) for flip in order[1:]}
    own[0] = pair
    prev = {0: rotate_seq(pair, 1)}
    loaded = pl.pallas_call(
        functools.partial(load_kernel, slices),
        out_shape=[q_slice] * (2 * slices) + [tile],
        in_specs=[pl.BlockSpec(memory_space=pltpu.SMEM), hbm, hbm],
        out_specs=[vmem] * (2 * slices + 1),
        scratch_shapes=[pltpu.SemaphoreType.DMA((2, slices))],
        compiler_params=params,
        name="load_slices",
    )(
        key_first,
        pltpu.with_memory_space_constraint(queries[0], pltpu.HBM),
        pltpu.with_memory_space_constraint(grad_out[0], pltpu.HBM),
    )
    bias = loaded[-1]
    prev[order[1]] = rotate_seq(after(own[order[1]], bias), 1)
    for flip in order[2:]:
        prev[flip] = rotate_seq(own[flip], 1)
    bias = after(bias, [own[flip] for flip in order])
    total, dq_parts, own_grads, back = None, {}, {}, {}
    carry_step = slices - 1
    for step, flip in enumerate(order):
        last = step == slices - 1
        carried = [first_held] if step == carry_step else []
        held_shape = ((2,) if carried else ()) + pair.shape
        *_, dq_parts[flip], own_grads[flip], held = out = pl.pallas_call(
            attention_kernel,
            out_shape=[tile] * (not last)
            + [
                q_slice,
                jax.ShapeDtypeStruct(pair.shape, jnp.float32),
                jax.ShapeDtypeStruct(held_shape, jnp.bfloat16),
            ],
            in_specs=[vmem] * (5 + len(carried)),
            out_specs=[vmem] * (3 if last else 4),
            compiler_params=params,
            name="attention_backward",
        )(bias, loaded[flip], loaded[slices + flip], own[flip], prev[flip], *carried)
        bias = out[0]
        if step == 0:
            first_held = held
        elif carried:
            back[flip], back[0] = rotate_seq(held, -1)
        else:
            back[flip] = rotate_seq(held, -1)
    for flip in order[1:]:
        part = own_grads[flip] + back[flip].astype(jnp.float32)
        part = part.astype(jnp.bfloat16)
        landed = swap_section(part, flip).astype(jnp.float32)
        total = landed if total is None else total + landed
    total = total + (own_grads[0] + back[0].astype(jnp.float32))
    dq = pl.pallas_call(
        functools.partial(store_kernel, slices),
        out_shape=jax.ShapeDtypeStruct(queries.shape[1:], jnp.bfloat16),
        in_specs=[vmem] * slices,
        out_specs=hbm,
        scratch_shapes=[pltpu.SemaphoreType.DMA((slices,))],
        compiler_params=params,
        name="store_slices",
    )(*[dq_parts[flip] for flip in range(slices)])
    return (dq[None], total[0], total[1])


def solution(mesh):
    placed = (
        P("section", "seq", None),
        P("section", "seq", None),
        P("seq", "section"),
        P("seq", "section"),
        P("seq"),
    )
    return jax.shard_map(
        body,
        mesh=mesh,
        in_specs=placed,
        out_specs=(P("section", "seq", None), P("seq", "section"), P("seq", "section")),
        check_vma=False,
    )
```

```python
import functools
import math

import jax
import jax.numpy as jnp
from jax import lax
from jax.experimental import pallas as pl
from jax.experimental.pallas import tpu as pltpu
from jax.sharding import PartitionSpec as P

HEADS = 32
KV_HEADS = 8
HEAD_DIM = 128
GROUP = HEADS // KV_HEADS
MASKED = -1e30
SCALE = 1.0 / math.sqrt(HEAD_DIM)
EXP2_SCALE = SCALE * math.log2(math.e)

NT = (((1,), (1,)), ((), ()))
NN = (((1,), (0,)), ((), ()))
TN = (((0,), (0,)), ((), ()))


def exchanged(x, partner_of):
    sections, shards = lax.axis_size("section"), lax.axis_size("seq")
    pairs = []
    for i in range(sections):
        for s in range(shards):
            j, t = partner_of(i, s, shards)
            pairs.append((i * shards + s, j * shards + t))
    return lax.ppermute(x, ("section", "seq"), pairs)


def swap_section(x, flip):
    return exchanged(x, lambda i, s, shards: (i ^ flip, s))


def rotate_seq(x, by):
    return exchanged(x, lambda i, s, shards: (i, (s + by) % shards))


def dot(a, b, dims):
    return lax.dot_general(a, b, dims, preferred_element_type=jnp.float32)


def softmax_grads(scores, dprob, bias, causal):
    tok = scores.shape[0] // 2
    dscores, wrounds = [], []
    for a in range(GROUP):
        head = slice(a * tok, (a + 1) * tok)
        s_prev = scores[:tok, head] + bias
        s_own = jnp.where(causal, scores[tok:, head], MASKED)
        top = jnp.max(jnp.maximum(s_prev, s_own), axis=0, keepdims=True)
        p_prev = jnp.exp2((s_prev - top) * EXP2_SCALE)
        p_own = jnp.exp2((s_own - top) * EXP2_SCALE)
        d_prev, d_own = dprob[:tok, head], dprob[tok:, head]
        inv = 1.0 / jnp.sum(p_prev + p_own, axis=0, keepdims=True)
        row_dot = jnp.sum(p_prev * d_prev + p_own * d_own, axis=0, keepdims=True) * inv
        w_prev, w_own = p_prev * inv, p_own * inv
        dscores.append(
            jnp.concatenate(
                [
                    (w_prev * (d_prev - row_dot) * SCALE).astype(jnp.bfloat16),
                    (w_own * (d_own - row_dot) * SCALE).astype(jnp.bfloat16),
                ],
                axis=0,
            )
        )
        wrounds.append(
            jnp.concatenate([w_prev.astype(jnp.bfloat16), w_own.astype(jnp.bfloat16)], axis=0)
        )
    return jnp.concatenate(dscores, axis=1), jnp.concatenate(wrounds, axis=1)


def load_kernel(slices, k_hbm, v_hbm, q_hbm, g_hbm, *refs):
    q_outs, g_outs = refs[:slices], refs[slices : 2 * slices]
    pair_out, sems, pair_sems = refs[2 * slices :]
    place = lax.axis_index("section")
    width = q_outs[0].shape[1]
    copies = [
        pltpu.make_async_copy(k_hbm, pair_out.at[0], pair_sems.at[0]),
        pltpu.make_async_copy(v_hbm, pair_out.at[1], pair_sems.at[1]),
    ]
    for flip in range(slices):
        span = pl.ds(pl.multiple_of((place ^ flip) * width, width), width)
        copies.append(pltpu.make_async_copy(q_hbm.at[:, span], q_outs[flip], sems.at[0, flip]))
        copies.append(pltpu.make_async_copy(g_hbm.at[:, span], g_outs[flip], sems.at[1, flip]))
    for copy in copies:
        copy.start()
    for copy in copies:
        copy.wait()


def store_kernel(slices, *refs):
    dq_ins, dq_hbm, sems = refs[:slices], refs[slices], refs[slices + 1]
    place = lax.axis_index("section")
    width = dq_ins[0].shape[1]
    copies = []
    for flip in range(slices):
        span = pl.ds(pl.multiple_of((place ^ flip) * width, width), width)
        copies.append(pltpu.make_async_copy(dq_ins[flip], dq_hbm.at[:, span], sems.at[flip]))
    for copy in copies:
        copy.start()
    for copy in copies:
        copy.wait()


def attention_kernel(bias_ref, q_ref, g_ref, own_ref, prev_ref, *refs):
    _, tok, width = own_ref.shape
    dq_out, own_out, prev_out = refs[-3:]
    for ref in refs[:-3]:
        if ref.dtype == jnp.float32:
            ref[...] = bias_ref[...]
        else:
            prev_out[1] = ref[...]
            prev_out = prev_out.at[0]
    bias = bias_ref[0:1, 0:1]
    key_pos = lax.broadcasted_iota(jnp.int32, (tok, tok), 0)
    query_pos = lax.broadcasted_iota(jnp.int32, (tok, tok), 1)
    causal = key_pos <= query_pos
    groups = []
    for h in range(width // HEAD_DIM):
        cols = slice(h * HEAD_DIM, (h + 1) * HEAD_DIM)
        heads = [
            slice((h * GROUP + a) * HEAD_DIM, (h * GROUP + a + 1) * HEAD_DIM)
            for a in range(GROUP)
        ]
        q4 = jnp.concatenate([q_ref[:, c] for c in heads], axis=0)
        g4 = jnp.concatenate([g_ref[:, c] for c in heads], axis=0)
        k2, v2 = [
            jnp.concatenate([prev_ref[kind, :, cols], own_ref[kind, :, cols]], axis=0)
            for kind in range(2)
        ]
        groups.append((cols, heads, q4, g4, k2, dot(k2, q4, NT), dot(v2, g4, NT)))
    rounded = [softmax_grads(scores, dprob, bias, causal) for *_, scores, dprob in groups]
    results = []
    for (_, _, q4, g4, k2, _, _), (dscore, wround) in zip(groups, rounded):
        dq_t = dot(k2, dscore, TN).astype(jnp.bfloat16)
        results.append((dq_t, dot(dscore, q4, NN), dot(wround, g4, NN)))
    for (cols, heads, *_), (dq_t, dk, dv) in zip(groups, results):
        for a, head in enumerate(heads):
            dq_out[:, head] = dq_t[:, a * tok : (a + 1) * tok].T
        for kind, grad in enumerate((dk, dv)):
            prev_out[kind, :, cols] = grad[:tok].astype(jnp.bfloat16)
            own_out[kind, :, cols] = grad[tok:]


def after(x, token):
    return lax.optimization_barrier((x, token))[0]


def body(queries, grad_out, keys, values, key_first):
    slices = lax.axis_size("section")
    tok, width = keys.shape
    q_width = GROUP * width
    vmem = pl.BlockSpec(memory_space=pltpu.VMEM)
    hbm = pl.BlockSpec(memory_space=pltpu.HBM)
    params = pltpu.CompilerParams(vmem_limit_bytes=16 * 1024 * 1024)
    q_slice = jax.ShapeDtypeStruct((tok, q_width), jnp.bfloat16)
    tile = jax.ShapeDtypeStruct((8, 128), jnp.float32)
    order = [0] + list(range(slices - 1, 0, -1))

    far = order[1]
    own = {far: jnp.stack([swap_section(keys, far), swap_section(values, far)])}
    loaded = pl.pallas_call(
        functools.partial(load_kernel, slices),
        out_shape=[q_slice] * (2 * slices)
        + [jax.ShapeDtypeStruct((2,) + keys.shape, jnp.bfloat16)],
        in_specs=[hbm] * 4,
        out_specs=[vmem] * (2 * slices + 1),
        scratch_shapes=[
            pltpu.SemaphoreType.DMA((2, slices)),
            pltpu.SemaphoreType.DMA((2,)),
        ],
        compiler_params=params,
        name="load_slices",
    )(
        *[pltpu.with_memory_space_constraint(x, pltpu.HBM) for x in (keys, values)],
        *[pltpu.with_memory_space_constraint(x[0], pltpu.HBM) for x in (queries, grad_out)],
    )
    pair = own[0] = loaded[-1]
    for flip in order[2:]:
        own[flip] = swap_section(pair, flip)
    prev = {0: rotate_seq(pair, 1)}
    seen = jnp.broadcast_to(key_first[:, None] < lax.axis_index("seq"), tile.shape)
    bias = jnp.where(seen, 0.0, MASKED).astype(tile.dtype)
    prev[order[1]] = rotate_seq(after(own[order[1]], bias), 1)
    for flip in order[2:]:
        prev[flip] = rotate_seq(own[flip], 1)
    bias = after(bias, [own[flip] for flip in order])
    total, dq_parts, own_grads, back = None, {}, {}, {}
    carry_step = slices - 1
    for step, flip in enumerate(order):
        last = step == slices - 1
        carried = [first_held] if step == carry_step else []
        held_shape = ((2,) if carried else ()) + pair.shape
        *_, dq_parts[flip], own_grads[flip], held = out = pl.pallas_call(
            attention_kernel,
            out_shape=[tile] * (not last)
            + [
                q_slice,
                jax.ShapeDtypeStruct(pair.shape, jnp.float32),
                jax.ShapeDtypeStruct(held_shape, jnp.bfloat16),
            ],
            in_specs=[vmem] * (5 + len(carried)),
            out_specs=[vmem] * (3 if last else 4),
            compiler_params=params,
            name="attention_backward",
        )(bias, loaded[flip], loaded[slices + flip], own[flip], prev[flip], *carried)
        bias = out[0]
        if step == 0:
            first_held = held
        elif carried:
            back[flip], back[0] = rotate_seq(held, -1)
        else:
            back[flip] = rotate_seq(held, -1)
    for flip in order[1:]:
        part = own_grads[flip] + back[flip].astype(jnp.float32)
        part = part.astype(jnp.bfloat16)
        landed = swap_section(part, flip).astype(jnp.float32)
        total = landed if total is None else total + landed
    total = total + (own_grads[0] + back[0].astype(jnp.float32))
    dq = pl.pallas_call(
        functools.partial(store_kernel, slices),
        out_shape=jax.ShapeDtypeStruct(queries.shape[1:], jnp.bfloat16),
        in_specs=[vmem] * slices,
        out_specs=hbm,
        scratch_shapes=[pltpu.SemaphoreType.DMA((slices,))],
        compiler_params=params,
        name="store_slices",
    )(*[dq_parts[flip] for flip in range(slices)])
    return (dq[None], total[0], total[1])


def solution(mesh):
    placed = (
        P("section", "seq", None),
        P("section", "seq", None),
        P("seq", "section"),
        P("seq", "section"),
        P("seq"),
    )
    return jax.shard_map(
        body,
        mesh=mesh,
        in_specs=placed,
        out_specs=(P("section", "seq", None), P("seq", "section"), P("seq", "section")),
        check_vma=False,
    )
```

```python
import functools
import math

import jax
import jax.numpy as jnp
from jax import lax
from jax.experimental import pallas as pl
from jax.experimental.pallas import tpu as pltpu
from jax.sharding import PartitionSpec as P

HEADS = 32
KV_HEADS = 8
HEAD_DIM = 128
GROUP = HEADS // KV_HEADS
MASKED = -1e30
SCALE = 1.0 / math.sqrt(HEAD_DIM)
EXP2_SCALE = SCALE * math.log2(math.e)

NT = (((1,), (1,)), ((), ()))
NN = (((1,), (0,)), ((), ()))
TN = (((0,), (0,)), ((), ()))


def exchanged(x, partner_of):
    sections, shards = lax.axis_size("section"), lax.axis_size("seq")
    pairs = []
    for i in range(sections):
        for s in range(shards):
            j, t = partner_of(i, s, shards)
            pairs.append((i * shards + s, j * shards + t))
    return lax.ppermute(x, ("section", "seq"), pairs)


def swap_section(x, flip):
    return exchanged(x, lambda i, s, shards: (i ^ flip, s))


def rotate_seq(x, by):
    return exchanged(x, lambda i, s, shards: (i, (s + by) % shards))


def dot(a, b, dims):
    return lax.dot_general(a, b, dims, preferred_element_type=jnp.float32)


def softmax_grads(scores, dprob, bias, causal):
    tok = causal.shape[0]
    dscores, wrounds = [], []
    for a in range(GROUP):
        head = slice(a * tok, (a + 1) * tok)
        parts = [jnp.where(causal, scores[-tok:, head], MASKED)]
        grads = [dprob[-tok:, head]]
        if bias is not None:
            parts.insert(0, scores[:tok, head] + bias)
            grads.insert(0, dprob[:tok, head])
        top = jnp.max(functools.reduce(jnp.maximum, parts), axis=0, keepdims=True)
        probs = [jnp.exp2((part - top) * EXP2_SCALE) for part in parts]
        inv = 1.0 / jnp.sum(sum(probs), axis=0, keepdims=True)
        mixed = sum(p * d for p, d in zip(probs, grads))
        row_dot = jnp.sum(mixed, axis=0, keepdims=True) * inv
        weights = [p * inv for p in probs]
        dscores.append([w * (d - row_dot) * SCALE for w, d in zip(weights, grads)])
        wrounds.append(weights)
    return [
        jnp.concatenate(
            [jnp.concatenate([x.astype(jnp.bfloat16) for x in parts], axis=0) for parts in heads],
            axis=1,
        )
        for heads in (dscores, wrounds)
    ]


def load_kernel(slices, first_ref, q_hbm, g_hbm, *refs):
    q_outs, g_outs = refs[:slices], refs[slices : 2 * slices]
    bias_out, sems = refs[2 * slices :]
    place = lax.axis_index("section")
    width = q_outs[0].shape[1]
    copies = []
    for flip in range(slices):
        span = pl.ds(pl.multiple_of((place ^ flip) * width, width), width)
        copies.append(pltpu.make_async_copy(q_hbm.at[:, span], q_outs[flip], sems.at[0, flip]))
        copies.append(pltpu.make_async_copy(g_hbm.at[:, span], g_outs[flip], sems.at[1, flip]))
    for copy in copies:
        copy.start()
    seen = first_ref[0] < lax.axis_index("seq")
    bias_out[...] = jnp.full(bias_out.shape, jnp.where(seen, 0.0, MASKED), jnp.float32)
    for copy in copies:
        copy.wait()


def store_kernel(slices, *refs):
    dq_ins, dq_hbm, sems = refs[:slices], refs[slices], refs[slices + 1]
    place = lax.axis_index("section")
    width = dq_ins[0].shape[1]
    copies = []
    for flip in range(slices):
        span = pl.ds(pl.multiple_of((place ^ flip) * width, width), width)
        copies.append(pltpu.make_async_copy(dq_ins[flip], dq_hbm.at[:, span], sems.at[flip]))
    for copy in copies:
        copy.start()
    for copy in copies:
        copy.wait()


def attention_kernel(bias_ref, q_ref, g_ref, own_ref, prev_ref, *refs):
    _, tok, width = own_ref.shape
    dq_out, own_out, prev_out = refs[-3:]
    for ref in refs[:-3]:
        if ref.dtype == jnp.float32:
            ref[...] = bias_ref[...]
        else:
            prev_out[1] = ref[...]
            prev_out = prev_out.at[0]
    key_pos = lax.broadcasted_iota(jnp.int32, (tok, tok), 0)
    query_pos = lax.broadcasted_iota(jnp.int32, (tok, tok), 1)
    causal = key_pos <= query_pos

    def work(bias):
        groups = []
        for h in range(width // HEAD_DIM):
            cols = slice(h * HEAD_DIM, (h + 1) * HEAD_DIM)
            heads = [
                slice((h * GROUP + a) * HEAD_DIM, (h * GROUP + a + 1) * HEAD_DIM)
                for a in range(GROUP)
            ]
            q4 = jnp.concatenate([q_ref[:, c] for c in heads], axis=0)
            g4 = jnp.concatenate([g_ref[:, c] for c in heads], axis=0)
            k2, v2 = own_ref[0, :, cols], own_ref[1, :, cols]
            if bias is not None:
                k2 = jnp.concatenate([prev_ref[0, :, cols], k2], axis=0)
                v2 = jnp.concatenate([prev_ref[1, :, cols], v2], axis=0)
            groups.append((cols, heads, q4, g4, k2, dot(k2, q4, NT), dot(v2, g4, NT)))
        rounded = [softmax_grads(scores, dprob, bias, causal) for *_, scores, dprob in groups]
        results = []
        for (_, _, q4, g4, k2, _, _), (dscore, wround) in zip(groups, rounded):
            dq_t = dot(k2, dscore, TN).astype(jnp.bfloat16)
            results.append((dq_t, dot(dscore, q4, NN), dot(wround, g4, NN)))
        for (cols, heads, *_), (dq_t, dk, dv) in zip(groups, results):
            for a, head in enumerate(heads):
                dq_out[:, head] = dq_t[:, a * tok : (a + 1) * tok].T
            for kind, grad in enumerate((dk, dv)):
                own_out[kind, :, cols] = grad[-tok:]
                if bias is not None:
                    prev_out[kind, :, cols] = grad[:tok].astype(jnp.bfloat16)

    @pl.when(lax.axis_index("seq") > 0)
    def _():
        work(bias_ref[0:1, 0:1])

    @pl.when(lax.axis_index("seq") == 0)
    def _():
        prev_out[...] = jnp.zeros(prev_out.shape, prev_out.dtype)
        work(None)


def after(x, token):
    return lax.optimization_barrier((x, token))[0]


def body(queries, grad_out, keys, values, key_first):
    slices = lax.axis_size("section")
    tok, width = keys.shape
    q_width = GROUP * width
    vmem = pl.BlockSpec(memory_space=pltpu.VMEM)
    hbm = pl.BlockSpec(memory_space=pltpu.HBM)
    params = pltpu.CompilerParams(vmem_limit_bytes=16 * 1024 * 1024)
    q_slice = jax.ShapeDtypeStruct((tok, q_width), jnp.bfloat16)
    tile = jax.ShapeDtypeStruct((8, 128), jnp.float32)
    order = [0] + list(range(slices - 1, 0, -1))

    pair = jnp.stack([keys, values])
    own = {flip: swap_section(pair, flip) for flip in order[1:]}
    own[0] = pair
    prev = {0: rotate_seq(pair, 1)}
    loaded = pl.pallas_call(
        functools.partial(load_kernel, slices),
        out_shape=[q_slice] * (2 * slices) + [tile],
        in_specs=[pl.BlockSpec(memory_space=pltpu.SMEM), hbm, hbm],
        out_specs=[vmem] * (2 * slices + 1),
        scratch_shapes=[pltpu.SemaphoreType.DMA((2, slices))],
        compiler_params=params,
        name="load_slices",
    )(
        key_first,
        pltpu.with_memory_space_constraint(queries[0], pltpu.HBM),
        pltpu.with_memory_space_constraint(grad_out[0], pltpu.HBM),
    )
    bias = loaded[-1]
    prev[order[1]] = rotate_seq(after(own[order[1]], bias), 1)
    for flip in order[2:]:
        prev[flip] = rotate_seq(own[flip], 1)
    bias = after(bias, [own[flip] for flip in order])
    total, dq_parts, own_grads, back = None, {}, {}, {}
    carry_step = slices - 1
    for step, flip in enumerate(order):
        last = step == slices - 1
        carried = [first_held] if step == carry_step else []
        held_shape = ((2,) if carried else ()) + pair.shape
        *_, dq_parts[flip], own_grads[flip], held = out = pl.pallas_call(
            attention_kernel,
            out_shape=[tile] * (not last)
            + [
                q_slice,
                jax.ShapeDtypeStruct(pair.shape, jnp.float32),
                jax.ShapeDtypeStruct(held_shape, jnp.bfloat16),
            ],
            in_specs=[vmem] * (5 + len(carried)),
            out_specs=[vmem] * (3 if last else 4),
            compiler_params=params,
            name="attention_backward",
        )(bias, loaded[flip], loaded[slices + flip], own[flip], prev[flip], *carried)
        bias = out[0]
        if step == 0:
            first_held = held
        elif carried:
            back[flip], back[0] = rotate_seq(held, -1)
        else:
            back[flip] = rotate_seq(held, -1)
    for flip in order[1:]:
        part = own_grads[flip] + back[flip].astype(jnp.float32)
        part = part.astype(jnp.bfloat16)
        landed = swap_section(part, flip).astype(jnp.float32)
        total = landed if total is None else total + landed
    total = total + (own_grads[0] + back[0].astype(jnp.float32))
    dq = pl.pallas_call(
        functools.partial(store_kernel, slices),
        out_shape=jax.ShapeDtypeStruct(queries.shape[1:], jnp.bfloat16),
        in_specs=[vmem] * slices,
        out_specs=hbm,
        scratch_shapes=[pltpu.SemaphoreType.DMA((slices,))],
        compiler_params=params,
        name="store_slices",
    )(*[dq_parts[flip] for flip in range(slices)])
    return (dq[None], total[0], total[1])


def solution(mesh):
    placed = (
        P("section", "seq", None),
        P("section", "seq", None),
        P("seq", "section"),
        P("seq", "section"),
        P("seq"),
    )
    return jax.shard_map(
        body,
        mesh=mesh,
        in_specs=placed,
        out_specs=(P("section", "seq", None), P("seq", "section"), P("seq", "section")),
        check_vma=False,
    )
```

```python
import functools
import math

import jax
import jax.numpy as jnp
from jax import lax
from jax.experimental import pallas as pl
from jax.experimental.pallas import tpu as pltpu
from jax.sharding import PartitionSpec as P

HEADS = 32
KV_HEADS = 8
HEAD_DIM = 128
GROUP = HEADS // KV_HEADS
MASKED = -1e30
SCALE = 1.0 / math.sqrt(HEAD_DIM)
EXP2_SCALE = SCALE * math.log2(math.e)

NT = (((1,), (1,)), ((), ()))
NN = (((1,), (0,)), ((), ()))
TN = (((0,), (0,)), ((), ()))


def exchanged(x, partner_of):
    sections, shards = lax.axis_size("section"), lax.axis_size("seq")
    pairs = []
    for i in range(sections):
        for s in range(shards):
            j, t = partner_of(i, s, shards)
            pairs.append((i * shards + s, j * shards + t))
    return lax.ppermute(x, ("section", "seq"), pairs)


def swap_section(x, flip):
    return exchanged(x, lambda i, s, shards: (i ^ flip, s))


def rotate_seq(x, by):
    return exchanged(x, lambda i, s, shards: (i, (s + by) % shards))


def dot(a, b, dims):
    return lax.dot_general(a, b, dims, preferred_element_type=jnp.float32)


def softmax_grads(scores, dprob, bias, causal):
    tok = causal.shape[0]
    dscores, wrounds = [], []
    for a in range(GROUP):
        head = slice(a * tok, (a + 1) * tok)
        parts = [jnp.where(causal, scores[-tok:, head], MASKED)]
        grads = [dprob[-tok:, head]]
        if bias is not None:
            parts.insert(0, scores[:tok, head] + bias)
            grads.insert(0, dprob[:tok, head])
        top = jnp.max(functools.reduce(jnp.maximum, parts), axis=0, keepdims=True)
        probs = [jnp.exp2((part - top) * EXP2_SCALE) for part in parts]
        inv = 1.0 / jnp.sum(sum(probs), axis=0, keepdims=True)
        mixed = sum(p * d for p, d in zip(probs, grads))
        row_dot = jnp.sum(mixed, axis=0, keepdims=True) * inv
        weights = [p * inv for p in probs]
        dscores.append([w * (d - row_dot) * SCALE for w, d in zip(weights, grads)])
        wrounds.append(weights)
    return [
        jnp.concatenate(
            [jnp.concatenate([x.astype(jnp.bfloat16) for x in parts], axis=0) for parts in heads],
            axis=1,
        )
        for heads in (dscores, wrounds)
    ]


def load_kernel(slices, first_ref, q_hbm, g_hbm, *refs):
    q_outs, g_outs = refs[:slices], refs[slices : 2 * slices]
    bias_out, sems = refs[2 * slices :]
    place = lax.axis_index("section")
    width = q_outs[0].shape[1]
    copies = []
    for flip in range(slices):
        span = pl.ds(pl.multiple_of((place ^ flip) * width, width), width)
        copies.append(pltpu.make_async_copy(q_hbm.at[:, span], q_outs[flip], sems.at[0, flip]))
        copies.append(pltpu.make_async_copy(g_hbm.at[:, span], g_outs[flip], sems.at[1, flip]))
    for copy in copies:
        copy.start()
    seen = first_ref[0] < lax.axis_index("seq")
    bias_out[...] = jnp.full(bias_out.shape, jnp.where(seen, 0.0, MASKED), jnp.float32)
    for copy in copies:
        copy.wait()


def store_kernel(slices, *refs):
    dq_ins, dq_hbm, sems = refs[:slices], refs[slices], refs[slices + 1]
    place = lax.axis_index("section")
    width = dq_ins[0].shape[1]
    copies = []
    for flip in range(slices):
        span = pl.ds(pl.multiple_of((place ^ flip) * width, width), width)
        copies.append(pltpu.make_async_copy(dq_ins[flip], dq_hbm.at[:, span], sems.at[flip]))
    for copy in copies:
        copy.start()
    for copy in copies:
        copy.wait()


def attention_kernel(bias_ref, q_ref, g_ref, own_ref, prev_ref, *refs):
    _, tok, width = own_ref.shape
    dq_out, own_out, prev_out = refs[-3:]
    for ref in refs[:-3]:
        if ref.dtype == jnp.float32:
            ref[...] = bias_ref[...]
        else:
            prev_out[1] = ref[...]
            prev_out = prev_out.at[0]
    key_pos = lax.broadcasted_iota(jnp.int32, (tok, tok), 0)
    query_pos = lax.broadcasted_iota(jnp.int32, (tok, tok), 1)
    causal = key_pos <= query_pos

    def work(bias):
        groups = []
        for h in range(width // HEAD_DIM):
            cols = slice(h * HEAD_DIM, (h + 1) * HEAD_DIM)
            heads = [
                slice((h * GROUP + a) * HEAD_DIM, (h * GROUP + a + 1) * HEAD_DIM)
                for a in range(GROUP)
            ]
            q4 = jnp.concatenate([q_ref[:, c] for c in heads], axis=0)
            g4 = jnp.concatenate([g_ref[:, c] for c in heads], axis=0)
            k2, v2 = own_ref[0, :, cols], own_ref[1, :, cols]
            if bias is not None:
                k2 = jnp.concatenate([prev_ref[0, :, cols], k2], axis=0)
                v2 = jnp.concatenate([prev_ref[1, :, cols], v2], axis=0)
            groups.append((cols, heads, q4, g4, k2, dot(k2, q4, NT), dot(v2, g4, NT)))
        rounded = [softmax_grads(scores, dprob, bias, causal) for *_, scores, dprob in groups]
        results = []
        for (_, _, q4, g4, k2, _, _), (dscore, wround) in zip(groups, rounded):
            dq_t = dot(k2, dscore, TN).astype(jnp.bfloat16)
            results.append((dq_t, dot(dscore, q4, NN), dot(wround, g4, NN)))
        for (cols, heads, *_), (dq_t, dk, dv) in zip(groups, results):
            for a, head in enumerate(heads):
                dq_out[:, head] = dq_t[:, a * tok : (a + 1) * tok].T
            for kind, grad in enumerate((dk, dv)):
                own_out[kind, :, cols] = grad[-tok:]
                if bias is not None:
                    prev_out[kind, :, cols] = grad[:tok].astype(jnp.bfloat16)

    @pl.when(lax.axis_index("seq") > 0)
    def _():
        work(bias_ref[0:1, 0:1])

    @pl.when(lax.axis_index("seq") == 0)
    def _():
        prev_out[...] = jnp.zeros(prev_out.shape, prev_out.dtype)
        work(None)


def after(x, token):
    return lax.optimization_barrier((x, token))[0]


def body(queries, grad_out, keys, values, key_first):
    slices = lax.axis_size("section")
    tok, width = keys.shape
    q_width = GROUP * width
    vmem = pl.BlockSpec(memory_space=pltpu.VMEM)
    hbm = pl.BlockSpec(memory_space=pltpu.HBM)
    params = pltpu.CompilerParams(vmem_limit_bytes=16 * 1024 * 1024)
    q_slice = jax.ShapeDtypeStruct((tok, q_width), jnp.bfloat16)
    tile = jax.ShapeDtypeStruct((8, 128), jnp.float32)
    order = [0, 1] + list(range(slices - 1, 1, -1))

    pair = jnp.stack([keys, values])
    own = {flip: swap_section(pair, flip) for flip in order[1:]}
    own[0] = pair
    prev = {0: rotate_seq(pair, 1)}
    loaded = pl.pallas_call(
        functools.partial(load_kernel, slices),
        out_shape=[q_slice] * (2 * slices) + [tile],
        in_specs=[pl.BlockSpec(memory_space=pltpu.SMEM), hbm, hbm],
        out_specs=[vmem] * (2 * slices + 1),
        scratch_shapes=[pltpu.SemaphoreType.DMA((2, slices))],
        compiler_params=params,
        name="load_slices",
    )(
        key_first,
        pltpu.with_memory_space_constraint(queries[0], pltpu.HBM),
        pltpu.with_memory_space_constraint(grad_out[0], pltpu.HBM),
    )
    bias = loaded[-1]
    prev[order[1]] = rotate_seq(after(own[order[1]], bias), 1)
    for flip in order[2:]:
        prev[flip] = rotate_seq(own[flip], 1)
    bias = after(bias, [own[flip] for flip in order])
    total, dq_parts, own_grads, back = None, {}, {}, {}
    carry_step = 1
    for step, flip in enumerate(order):
        last = step == slices - 1
        carried = [first_held] if step == carry_step else []
        held_shape = ((2,) if carried else ()) + pair.shape
        *_, dq_parts[flip], own_grads[flip], held = out = pl.pallas_call(
            attention_kernel,
            out_shape=[tile] * (not last)
            + [
                q_slice,
                jax.ShapeDtypeStruct(pair.shape, jnp.float32),
                jax.ShapeDtypeStruct(held_shape, jnp.bfloat16),
            ],
            in_specs=[vmem] * (5 + len(carried)),
            out_specs=[vmem] * (3 if last else 4),
            compiler_params=params,
            name="attention_backward",
        )(bias, loaded[flip], loaded[slices + flip], own[flip], prev[flip], *carried)
        bias = out[0]
        if step == 0:
            first_held = held
        elif carried:
            back[flip], back[0] = rotate_seq(held, -1)
        else:
            back[flip] = rotate_seq(held, -1)
    for flip in order[1:]:
        part = own_grads[flip] + back[flip].astype(jnp.float32)
        part = part.astype(jnp.bfloat16)
        landed = swap_section(part, flip).astype(jnp.float32)
        total = landed if total is None else total + landed
    total = total + (own_grads[0] + back[0].astype(jnp.float32))
    dq = pl.pallas_call(
        functools.partial(store_kernel, slices),
        out_shape=jax.ShapeDtypeStruct(queries.shape[1:], jnp.bfloat16),
        in_specs=[vmem] * slices,
        out_specs=hbm,
        scratch_shapes=[pltpu.SemaphoreType.DMA((slices,))],
        compiler_params=params,
        name="store_slices",
    )(*[dq_parts[flip] for flip in range(slices)])
    return (dq[None], total[0], total[1])


def solution(mesh):
    placed = (
        P("section", "seq", None),
        P("section", "seq", None),
        P("seq", "section"),
        P("seq", "section"),
        P("seq"),
    )
    return jax.shard_map(
        body,
        mesh=mesh,
        in_specs=placed,
        out_specs=(P("section", "seq", None), P("seq", "section"), P("seq", "section")),
        check_vma=False,
    )
```

```python
import functools
import math

import jax
import jax.numpy as jnp
from jax import lax
from jax.experimental import pallas as pl
from jax.experimental.pallas import tpu as pltpu
from jax.sharding import PartitionSpec as P

HEADS = 32
KV_HEADS = 8
HEAD_DIM = 128
GROUP = HEADS // KV_HEADS
MASKED = -1e30
SCALE = 1.0 / math.sqrt(HEAD_DIM)
EXP2_SCALE = SCALE * math.log2(math.e)

NT = (((1,), (1,)), ((), ()))
NN = (((1,), (0,)), ((), ()))
TN = (((0,), (0,)), ((), ()))


def exchanged(x, partner_of):
    sections, shards = lax.axis_size("section"), lax.axis_size("seq")
    pairs = []
    for i in range(sections):
        for s in range(shards):
            j, t = partner_of(i, s, shards)
            pairs.append((i * shards + s, j * shards + t))
    return lax.ppermute(x, ("section", "seq"), pairs)


def swap_section(x, flip):
    return exchanged(x, lambda i, s, shards: (i ^ flip, s))


def rotate_seq(x, by):
    return exchanged(x, lambda i, s, shards: (i, (s + by) % shards))


def dot(a, b, dims):
    return lax.dot_general(a, b, dims, preferred_element_type=jnp.float32)


def softmax_grads(scores, dprob, bias, causal):
    tok = causal.shape[0]
    dscores, wrounds = [], []
    for a in range(GROUP):
        head = slice(a * tok, (a + 1) * tok)
        parts = [jnp.where(causal, scores[-tok:, head], MASKED)]
        grads = [dprob[-tok:, head]]
        if bias is not None:
            parts.insert(0, scores[:tok, head] + bias)
            grads.insert(0, dprob[:tok, head])
        top = jnp.max(functools.reduce(jnp.maximum, parts), axis=0, keepdims=True)
        probs = [jnp.exp2((part - top) * EXP2_SCALE) for part in parts]
        inv = 1.0 / jnp.sum(sum(probs), axis=0, keepdims=True)
        mixed = sum(p * d for p, d in zip(probs, grads))
        row_dot = jnp.sum(mixed, axis=0, keepdims=True) * inv
        weights = [p * inv for p in probs]
        dscores.append([w * (d - row_dot) * SCALE for w, d in zip(weights, grads)])
        wrounds.append(weights)
    return [
        jnp.concatenate(
            [jnp.concatenate([x.astype(jnp.bfloat16) for x in parts], axis=0) for parts in heads],
            axis=1,
        )
        for heads in (dscores, wrounds)
    ]


def load_kernel(slices, first_ref, q_hbm, g_hbm, *refs):
    q_outs, g_outs = refs[:slices], refs[slices : 2 * slices]
    bias_out, sems = refs[2 * slices :]
    place = lax.axis_index("section")
    width = q_outs[0].shape[1]
    copies = []
    for flip in range(slices):
        span = pl.ds(pl.multiple_of((place ^ flip) * width, width), width)
        copies.append(pltpu.make_async_copy(q_hbm.at[:, span], q_outs[flip], sems.at[0, flip]))
        copies.append(pltpu.make_async_copy(g_hbm.at[:, span], g_outs[flip], sems.at[1, flip]))
    for copy in copies:
        copy.start()
    seen = first_ref[0] < lax.axis_index("seq")
    bias_out[...] = jnp.full(bias_out.shape, jnp.where(seen, 0.0, MASKED), jnp.float32)
    for copy in copies:
        copy.wait()


def store_kernel(slices, *refs):
    dq_ins, dq_hbm, sems = refs[:slices], refs[slices], refs[slices + 1]
    place = lax.axis_index("section")
    width = dq_ins[0].shape[1]
    copies = []
    for flip in range(slices):
        span = pl.ds(pl.multiple_of((place ^ flip) * width, width), width)
        copies.append(pltpu.make_async_copy(dq_ins[flip], dq_hbm.at[:, span], sems.at[flip]))
    for copy in copies:
        copy.start()
    for copy in copies:
        copy.wait()


def attention_kernel(bias_ref, q_ref, g_ref, own_ref, prev_ref, *refs):
    _, tok, width = own_ref.shape
    dq_out, own_out, prev_out = refs[-3:]
    for ref in refs[:-3]:
        if ref.dtype == jnp.float32:
            ref[...] = bias_ref[...]
        else:
            prev_out[1] = ref[...]
            prev_out = prev_out.at[0]
    key_pos = lax.broadcasted_iota(jnp.int32, (tok, tok), 0)
    query_pos = lax.broadcasted_iota(jnp.int32, (tok, tok), 1)
    causal = key_pos <= query_pos

    def work(bias):
        groups = []
        for h in range(width // HEAD_DIM):
            cols = slice(h * HEAD_DIM, (h + 1) * HEAD_DIM)
            heads = [
                slice((h * GROUP + a) * HEAD_DIM, (h * GROUP + a + 1) * HEAD_DIM)
                for a in range(GROUP)
            ]
            q4 = jnp.concatenate([q_ref[:, c] for c in heads], axis=0)
            g4 = jnp.concatenate([g_ref[:, c] for c in heads], axis=0)
            k2, v2 = own_ref[0, :, cols], own_ref[1, :, cols]
            if bias is not None:
                k2 = jnp.concatenate([prev_ref[0, :, cols], k2], axis=0)
                v2 = jnp.concatenate([prev_ref[1, :, cols], v2], axis=0)
            groups.append((cols, heads, q4, g4, k2, dot(k2, q4, NT), dot(v2, g4, NT)))
        rounded = [softmax_grads(scores, dprob, bias, causal) for *_, scores, dprob in groups]
        results = []
        for (_, _, q4, g4, k2, _, _), (dscore, wround) in zip(groups, rounded):
            dq_t = dot(k2, dscore, TN).astype(jnp.bfloat16)
            results.append((dq_t, dot(dscore, q4, NN), dot(wround, g4, NN)))
        for (cols, heads, *_), (dq_t, dk, dv) in zip(groups, results):
            for a, head in enumerate(heads):
                dq_out[:, head] = dq_t[:, a * tok : (a + 1) * tok].T
            for kind, grad in enumerate((dk, dv)):
                own_out[kind, :, cols] = grad[-tok:]
                if bias is not None:
                    prev_out[kind, :, cols] = grad[:tok].astype(jnp.bfloat16)

    @pl.when(lax.axis_index("seq") > 0)
    def _():
        work(bias_ref[0:1, 0:1])

    @pl.when(lax.axis_index("seq") == 0)
    def _():
        prev_out[...] = jnp.zeros(prev_out.shape, prev_out.dtype)
        work(None)


def after(x, token):
    return lax.optimization_barrier((x, token))[0]


def body(queries, grad_out, keys, values, key_first):
    slices = lax.axis_size("section")
    tok, width = keys.shape
    q_width = GROUP * width
    vmem = pl.BlockSpec(memory_space=pltpu.VMEM)
    hbm = pl.BlockSpec(memory_space=pltpu.HBM)
    params = pltpu.CompilerParams(vmem_limit_bytes=16 * 1024 * 1024)
    q_slice = jax.ShapeDtypeStruct((tok, q_width), jnp.bfloat16)
    tile = jax.ShapeDtypeStruct((8, 128), jnp.float32)
    order = [0] + list(range(slices - 1, 0, -1))

    pair = jnp.stack([keys, values])
    own = {flip: swap_section(pair, flip) for flip in order[1:]}
    own[0] = pair
    prev = {0: rotate_seq(pair, 1)}
    loaded = pl.pallas_call(
        functools.partial(load_kernel, slices),
        out_shape=[q_slice] * (2 * slices) + [tile],
        in_specs=[pl.BlockSpec(memory_space=pltpu.SMEM), hbm, hbm],
        out_specs=[vmem] * (2 * slices + 1),
        scratch_shapes=[pltpu.SemaphoreType.DMA((2, slices))],
        compiler_params=params,
        name="load_slices",
    )(
        key_first,
        pltpu.with_memory_space_constraint(queries[0], pltpu.HBM),
        pltpu.with_memory_space_constraint(grad_out[0], pltpu.HBM),
    )
    bias = loaded[-1]
    prev[order[1]] = rotate_seq(after(own[order[1]], bias), 1)
    bias = after(bias, own[order[1]])
    total, dq_parts, own_grads, back = None, {}, {}, {}
    carry_step = slices - 1
    for step, flip in enumerate(order):
        last = step == slices - 1
        carried = [first_held] if step == carry_step else []
        held_shape = ((2,) if carried else ()) + pair.shape
        *_, dq_parts[flip], own_grads[flip], held = out = pl.pallas_call(
            attention_kernel,
            out_shape=[tile] * (not last)
            + [
                q_slice,
                jax.ShapeDtypeStruct(pair.shape, jnp.float32),
                jax.ShapeDtypeStruct(held_shape, jnp.bfloat16),
            ],
            in_specs=[vmem] * (5 + len(carried)),
            out_specs=[vmem] * (3 if last else 4),
            compiler_params=params,
            name="attention_backward",
        )(bias, loaded[flip], loaded[slices + flip], own[flip], prev[flip], *carried)
        bias = out[0]
        if step == 0:
            first_held = held
            for later in order[2:]:
                prev[later] = rotate_seq(after(own[later], bias), 1)
            bias = after(bias, [own[later] for later in order])
        elif carried:
            back[flip], back[0] = rotate_seq(held, -1)
        else:
            back[flip] = rotate_seq(held, -1)
    for flip in order[1:]:
        part = own_grads[flip] + back[flip].astype(jnp.float32)
        part = part.astype(jnp.bfloat16)
        landed = swap_section(part, flip).astype(jnp.float32)
        total = landed if total is None else total + landed
    total = total + (own_grads[0] + back[0].astype(jnp.float32))
    dq = pl.pallas_call(
        functools.partial(store_kernel, slices),
        out_shape=jax.ShapeDtypeStruct(queries.shape[1:], jnp.bfloat16),
        in_specs=[vmem] * slices,
        out_specs=hbm,
        scratch_shapes=[pltpu.SemaphoreType.DMA((slices,))],
        compiler_params=params,
        name="store_slices",
    )(*[dq_parts[flip] for flip in range(slices)])
    return (dq[None], total[0], total[1])


def solution(mesh):
    placed = (
        P("section", "seq", None),
        P("section", "seq", None),
        P("seq", "section"),
        P("seq", "section"),
        P("seq"),
    )
    return jax.shard_map(
        body,
        mesh=mesh,
        in_specs=placed,
        out_specs=(P("section", "seq", None), P("seq", "section"), P("seq", "section")),
        check_vma=False,
    )
```

```python
import functools
import math

import jax
import jax.numpy as jnp
from jax import lax
from jax.experimental import pallas as pl
from jax.experimental.pallas import tpu as pltpu
from jax.sharding import PartitionSpec as P

HEADS = 32
KV_HEADS = 8
HEAD_DIM = 128
GROUP = HEADS // KV_HEADS
MASKED = -1e30
SCALE = 1.0 / math.sqrt(HEAD_DIM)
EXP2_SCALE = SCALE * math.log2(math.e)

NT = (((1,), (1,)), ((), ()))
NN = (((1,), (0,)), ((), ()))
TN = (((0,), (0,)), ((), ()))


def exchanged(x, partner_of):
    sections, shards = lax.axis_size("section"), lax.axis_size("seq")
    pairs = []
    for i in range(sections):
        for s in range(shards):
            j, t = partner_of(i, s, shards)
            pairs.append((i * shards + s, j * shards + t))
    return lax.ppermute(x, ("section", "seq"), pairs)


def swap_section(x, flip):
    return exchanged(x, lambda i, s, shards: (i ^ flip, s))


def rotate_seq(x, by):
    return exchanged(x, lambda i, s, shards: (i, (s + by) % shards))


def dot(a, b, dims):
    return lax.dot_general(a, b, dims, preferred_element_type=jnp.float32)


def softmax_grads(scores, dprob, bias, causal):
    tok = causal.shape[0]
    dscores, wrounds = [], []
    for a in range(GROUP):
        head = slice(a * tok, (a + 1) * tok)
        parts = [jnp.where(causal, scores[-tok:, head], MASKED)]
        grads = [dprob[-tok:, head]]
        if bias is not None:
            parts.insert(0, scores[:tok, head] + bias)
            grads.insert(0, dprob[:tok, head])
        top = jnp.max(functools.reduce(jnp.maximum, parts), axis=0, keepdims=True)
        probs = [jnp.exp2((part - top) * EXP2_SCALE) for part in parts]
        inv = 1.0 / jnp.sum(sum(probs), axis=0, keepdims=True)
        mixed = sum(p * d for p, d in zip(probs, grads))
        row_dot = jnp.sum(mixed, axis=0, keepdims=True) * inv
        weights = [p * inv for p in probs]
        dscores.append([w * (d - row_dot) * SCALE for w, d in zip(weights, grads)])
        wrounds.append(weights)
    return [
        jnp.concatenate(
            [jnp.concatenate([x.astype(jnp.bfloat16) for x in parts], axis=0) for parts in heads],
            axis=1,
        )
        for heads in (dscores, wrounds)
    ]


def load_kernel(slices, first_ref, q_hbm, g_hbm, *refs):
    q_outs, g_outs = refs[:slices], refs[slices : 2 * slices]
    bias_out, sems = refs[2 * slices :]
    place = lax.axis_index("section")
    width = q_outs[0].shape[1]
    copies = []
    for flip in range(slices):
        span = pl.ds(pl.multiple_of((place ^ flip) * width, width), width)
        copies.append(pltpu.make_async_copy(q_hbm.at[:, span], q_outs[flip], sems.at[0, flip]))
        copies.append(pltpu.make_async_copy(g_hbm.at[:, span], g_outs[flip], sems.at[1, flip]))
    for copy in copies:
        copy.start()
    seen = first_ref[0] < lax.axis_index("seq")
    bias_out[...] = jnp.full(bias_out.shape, jnp.where(seen, 0.0, MASKED), jnp.float32)
    for copy in copies:
        copy.wait()


def store_kernel(slices, *refs):
    dq_ins, dq_hbm, sems = refs[:slices], refs[slices], refs[slices + 1]
    place = lax.axis_index("section")
    width = dq_ins[0].shape[1]
    copies = []
    for flip in range(slices):
        span = pl.ds(pl.multiple_of((place ^ flip) * width, width), width)
        copies.append(pltpu.make_async_copy(dq_ins[flip], dq_hbm.at[:, span], sems.at[flip]))
    for copy in copies:
        copy.start()
    for copy in copies:
        copy.wait()


def attention_kernel(bias_ref, q_ref, g_ref, own_ref, prev_ref, *refs):
    _, tok, width = own_ref.shape
    dq_out, own_out, prev_out = refs[-3:]
    for ref in refs[:-3]:
        ref[...] = bias_ref[...]
    key_pos = lax.broadcasted_iota(jnp.int32, (tok, tok), 0)
    query_pos = lax.broadcasted_iota(jnp.int32, (tok, tok), 1)
    causal = key_pos <= query_pos

    def work(bias):
        groups = []
        for h in range(width // HEAD_DIM):
            cols = slice(h * HEAD_DIM, (h + 1) * HEAD_DIM)
            heads = [
                slice((h * GROUP + a) * HEAD_DIM, (h * GROUP + a + 1) * HEAD_DIM)
                for a in range(GROUP)
            ]
            q4 = jnp.concatenate([q_ref[:, c] for c in heads], axis=0)
            g4 = jnp.concatenate([g_ref[:, c] for c in heads], axis=0)
            k2, v2 = own_ref[0, :, cols], own_ref[1, :, cols]
            if bias is not None:
                k2 = jnp.concatenate([prev_ref[0, :, cols], k2], axis=0)
                v2 = jnp.concatenate([prev_ref[1, :, cols], v2], axis=0)
            groups.append((cols, heads, q4, g4, k2, dot(k2, q4, NT), dot(v2, g4, NT)))
        rounded = [softmax_grads(scores, dprob, bias, causal) for *_, scores, dprob in groups]
        results = []
        for (_, _, q4, g4, k2, _, _), (dscore, wround) in zip(groups, rounded):
            dq_t = dot(k2, dscore, TN).astype(jnp.bfloat16)
            results.append((dq_t, dot(dscore, q4, NN), dot(wround, g4, NN)))
        for (cols, heads, *_), (dq_t, dk, dv) in zip(groups, results):
            for a, head in enumerate(heads):
                dq_out[:, head] = dq_t[:, a * tok : (a + 1) * tok].T
            for kind, grad in enumerate((dk, dv)):
                own_out[kind, :, cols] = grad[-tok:]
                if bias is not None:
                    prev_out[kind, :, cols] = grad[:tok].astype(jnp.bfloat16)

    @pl.when(lax.axis_index("seq") > 0)
    def _():
        work(bias_ref[0:1, 0:1])

    @pl.when(lax.axis_index("seq") == 0)
    def _():
        prev_out[...] = jnp.zeros(prev_out.shape, prev_out.dtype)
        work(None)


def after(x, token):
    return lax.optimization_barrier((x, token))[0]


def body(queries, grad_out, keys, values, key_first):
    slices = lax.axis_size("section")
    tok, width = keys.shape
    q_width = GROUP * width
    vmem = pl.BlockSpec(memory_space=pltpu.VMEM)
    hbm = pl.BlockSpec(memory_space=pltpu.HBM)
    params = pltpu.CompilerParams(vmem_limit_bytes=16 * 1024 * 1024)
    q_slice = jax.ShapeDtypeStruct((tok, q_width), jnp.bfloat16)
    tile = jax.ShapeDtypeStruct((8, 128), jnp.float32)
    order = [0] + list(range(slices - 1, 0, -1))

    pair = jnp.stack([keys, values])
    own = {flip: swap_section(pair, flip) for flip in order[1:]}
    own[0] = pair
    prev = {0: rotate_seq(pair, 1)}
    loaded = pl.pallas_call(
        functools.partial(load_kernel, slices),
        out_shape=[q_slice] * (2 * slices) + [tile],
        in_specs=[pl.BlockSpec(memory_space=pltpu.SMEM), hbm, hbm],
        out_specs=[vmem] * (2 * slices + 1),
        scratch_shapes=[pltpu.SemaphoreType.DMA((2, slices))],
        compiler_params=params,
        name="load_slices",
    )(
        key_first,
        pltpu.with_memory_space_constraint(queries[0], pltpu.HBM),
        pltpu.with_memory_space_constraint(grad_out[0], pltpu.HBM),
    )
    bias = loaded[-1]
    prev[order[1]] = rotate_seq(after(own[order[1]], bias), 1)
    bias = after(bias, own[order[1]])
    total, dq_parts, own_grads, back = None, {}, {}, {}
    for step, flip in enumerate(order):
        last = step == slices - 1
        *_, dq_parts[flip], own_grads[flip], held = out = pl.pallas_call(
            attention_kernel,
            out_shape=[tile] * (not last)
            + [
                q_slice,
                jax.ShapeDtypeStruct(pair.shape, jnp.float32),
                jax.ShapeDtypeStruct(pair.shape, jnp.bfloat16),
            ],
            in_specs=[vmem] * 5,
            out_specs=[vmem] * (3 if last else 4),
            compiler_params=params,
            name="attention_backward",
        )(bias, loaded[flip], loaded[slices + flip], own[flip], prev[flip])
        bias = out[0]
        if step == 0:
            back[0] = rotate_seq(held, -1)
            for later in order[2:]:
                prev[later] = rotate_seq(after(own[later], bias), 1)
            bias = after(bias, [own[later] for later in order])
        else:
            back[flip] = rotate_seq(held, -1)
    back[order[1]] = after(back[order[1]], back[0])
    for flip in order[1:]:
        part = own_grads[flip] + back[flip].astype(jnp.float32)
        part = part.astype(jnp.bfloat16)
        landed = swap_section(part, flip).astype(jnp.float32)
        total = landed if total is None else total + landed
    total = total + (own_grads[0] + back[0].astype(jnp.float32))
    dq = pl.pallas_call(
        functools.partial(store_kernel, slices),
        out_shape=jax.ShapeDtypeStruct(queries.shape[1:], jnp.bfloat16),
        in_specs=[vmem] * slices,
        out_specs=hbm,
        scratch_shapes=[pltpu.SemaphoreType.DMA((slices,))],
        compiler_params=params,
        name="store_slices",
    )(*[dq_parts[flip] for flip in range(slices)])
    return (dq[None], total[0], total[1])


def solution(mesh):
    placed = (
        P("section", "seq", None),
        P("section", "seq", None),
        P("seq", "section"),
        P("seq", "section"),
        P("seq"),
    )
    return jax.shard_map(
        body,
        mesh=mesh,
        in_specs=placed,
        out_specs=(P("section", "seq", None), P("seq", "section"), P("seq", "section")),
        check_vma=False,
    )
```

```python
import functools
import math

import jax
import jax.numpy as jnp
from jax import lax
from jax.experimental import pallas as pl
from jax.experimental.pallas import tpu as pltpu
from jax.sharding import PartitionSpec as P

HEADS = 32
KV_HEADS = 8
HEAD_DIM = 128
GROUP = HEADS // KV_HEADS
MASKED = -1e30
SCALE = 1.0 / math.sqrt(HEAD_DIM)
EXP2_SCALE = SCALE * math.log2(math.e)

NT = (((1,), (1,)), ((), ()))
NN = (((1,), (0,)), ((), ()))
TN = (((0,), (0,)), ((), ()))


def exchanged(x, partner_of):
    sections, shards = lax.axis_size("section"), lax.axis_size("seq")
    pairs = []
    for i in range(sections):
        for s in range(shards):
            j, t = partner_of(i, s, shards)
            pairs.append((i * shards + s, j * shards + t))
    return lax.ppermute(x, ("section", "seq"), pairs)


def swap_section(x, flip):
    return exchanged(x, lambda i, s, shards: (i ^ flip, s))


def rotate_seq(x, by):
    return exchanged(x, lambda i, s, shards: (i, (s + by) % shards))


def dot(a, b, dims):
    return lax.dot_general(a, b, dims, preferred_element_type=jnp.float32)


def softmax_grads(scores, dprob, causal):
    tok = causal.shape[0]
    dscores, wrounds = [], []
    for a in range(GROUP):
        head = slice(a * tok, (a + 1) * tok)
        parts = [jnp.where(causal, scores[-tok:, head], MASKED)]
        grads = [dprob[-tok:, head]]
        if scores.shape[0] > tok:
            parts.insert(0, scores[:tok, head])
            grads.insert(0, dprob[:tok, head])
        top = jnp.max(functools.reduce(jnp.maximum, parts), axis=0, keepdims=True)
        probs = [jnp.exp2((part - top) * EXP2_SCALE) for part in parts]
        inv = 1.0 / jnp.sum(sum(probs), axis=0, keepdims=True)
        mixed = sum(p * d for p, d in zip(probs, grads))
        row_dot = jnp.sum(mixed, axis=0, keepdims=True) * inv
        weights = [p * inv for p in probs]
        dscores.append([w * (d - row_dot) * SCALE for w, d in zip(weights, grads)])
        wrounds.append(weights)
    return [
        jnp.concatenate(
            [jnp.concatenate([x.astype(jnp.bfloat16) for x in parts], axis=0) for parts in heads],
            axis=1,
        )
        for heads in (dscores, wrounds)
    ]


def load_kernel(slices, q_hbm, g_hbm, *refs):
    q_outs, g_outs = refs[:slices], refs[slices : 2 * slices]
    turn_out, sems = refs[2 * slices :]
    place = lax.axis_index("section")
    width = q_outs[0].shape[1]
    copies = []
    for flip in range(slices):
        span = pl.ds(pl.multiple_of((place ^ flip) * width, width), width)
        copies.append(pltpu.make_async_copy(q_hbm.at[:, span], q_outs[flip], sems.at[0, flip]))
        copies.append(pltpu.make_async_copy(g_hbm.at[:, span], g_outs[flip], sems.at[1, flip]))
    for copy in copies:
        copy.start()
    turn_out[...] = jnp.zeros(turn_out.shape, turn_out.dtype)
    for copy in copies:
        copy.wait()


def store_kernel(slices, *refs):
    dq_ins, dq_hbm, sems = refs[:slices], refs[slices], refs[slices + 1]
    place = lax.axis_index("section")
    width = dq_ins[0].shape[1]
    copies = []
    for flip in range(slices):
        span = pl.ds(pl.multiple_of((place ^ flip) * width, width), width)
        copies.append(pltpu.make_async_copy(dq_ins[flip], dq_hbm.at[:, span], sems.at[flip]))
    for copy in copies:
        copy.start()
    for copy in copies:
        copy.wait()


def attention_kernel(first_ref, turn_ref, q_ref, g_ref, own_ref, prev_ref, *refs):
    _, tok, width = own_ref.shape
    dq_out, own_out, prev_out = refs[-3:]
    for ref in refs[:-3]:
        ref[...] = turn_ref[...]
    key_pos = lax.broadcasted_iota(jnp.int32, (tok, tok), 0)
    query_pos = lax.broadcasted_iota(jnp.int32, (tok, tok), 1)
    causal = key_pos <= query_pos

    def work(with_prev):
        groups = []
        for h in range(width // HEAD_DIM):
            cols = slice(h * HEAD_DIM, (h + 1) * HEAD_DIM)
            heads = [
                slice((h * GROUP + a) * HEAD_DIM, (h * GROUP + a + 1) * HEAD_DIM)
                for a in range(GROUP)
            ]
            q4 = jnp.concatenate([q_ref[:, c] for c in heads], axis=0)
            g4 = jnp.concatenate([g_ref[:, c] for c in heads], axis=0)
            k2, v2 = own_ref[0, :, cols], own_ref[1, :, cols]
            if with_prev:
                k2 = jnp.concatenate([prev_ref[0, :, cols], k2], axis=0)
                v2 = jnp.concatenate([prev_ref[1, :, cols], v2], axis=0)
            groups.append((cols, heads, q4, g4, k2, dot(k2, q4, NT), dot(v2, g4, NT)))
        rounded = [softmax_grads(scores, dprob, causal) for *_, scores, dprob in groups]
        results = []
        for (_, _, q4, g4, k2, _, _), (dscore, wround) in zip(groups, rounded):
            dq_t = dot(k2, dscore, TN).astype(jnp.bfloat16)
            results.append((dq_t, dot(dscore, q4, NN), dot(wround, g4, NN)))
        for (cols, heads, *_), (dq_t, dk, dv) in zip(groups, results):
            for a, head in enumerate(heads):
                dq_out[:, head] = dq_t[:, a * tok : (a + 1) * tok].T
            for kind, grad in enumerate((dk, dv)):
                own_out[kind, :, cols] = grad[-tok:]
                if with_prev:
                    prev_out[kind, :, cols] = grad[:tok].astype(jnp.bfloat16)

    seen = first_ref[0] < lax.axis_index("seq")

    @pl.when(seen)
    def _():
        work(True)

    @pl.when(jnp.logical_not(seen))
    def _():
        prev_out[...] = jnp.zeros(prev_out.shape, prev_out.dtype)
        work(False)


def after(x, token):
    return lax.optimization_barrier((x, token))[0]


def body(queries, grad_out, keys, values, key_first):
    slices = lax.axis_size("section")
    tok, width = keys.shape
    q_width = GROUP * width
    vmem = pl.BlockSpec(memory_space=pltpu.VMEM)
    smem = pl.BlockSpec(memory_space=pltpu.SMEM)
    hbm = pl.BlockSpec(memory_space=pltpu.HBM)
    params = pltpu.CompilerParams(vmem_limit_bytes=16 * 1024 * 1024)
    q_slice = jax.ShapeDtypeStruct((tok, q_width), jnp.bfloat16)
    tile = jax.ShapeDtypeStruct((8, 128), jnp.float32)
    order = [0] + list(range(slices - 1, 0, -1))

    pair = jnp.stack([keys, values])
    own = {flip: swap_section(pair, flip) for flip in order[1:]}
    own[0] = pair
    prev = {0: rotate_seq(pair, 1)}
    loaded = pl.pallas_call(
        functools.partial(load_kernel, slices),
        out_shape=[q_slice] * (2 * slices) + [tile],
        in_specs=[hbm, hbm],
        out_specs=[vmem] * (2 * slices + 1),
        scratch_shapes=[pltpu.SemaphoreType.DMA((2, slices))],
        compiler_params=params,
        name="load_slices",
    )(
        pltpu.with_memory_space_constraint(queries[0], pltpu.HBM),
        pltpu.with_memory_space_constraint(grad_out[0], pltpu.HBM),
    )
    turn = loaded[-1]
    prev[order[1]] = rotate_seq(after(own[order[1]], turn), 1)
    turn = after(turn, own[order[1]])
    total, dq_parts, own_grads, back = None, {}, {}, {}
    for step, flip in enumerate(order):
        last = step == slices - 1
        *_, dq_parts[flip], own_grads[flip], held = out = pl.pallas_call(
            attention_kernel,
            out_shape=[tile] * (not last)
            + [
                q_slice,
                jax.ShapeDtypeStruct(pair.shape, jnp.float32),
                jax.ShapeDtypeStruct(pair.shape, jnp.bfloat16),
            ],
            in_specs=[smem] + [vmem] * 5,
            out_specs=[vmem] * (3 if last else 4),
            compiler_params=params,
            name="attention_backward",
        )(key_first, turn, loaded[flip], loaded[slices + flip], own[flip], prev[flip])
        turn = out[0]
        if step == 0:
            back[0] = rotate_seq(held, -1)
            for later in order[2:]:
                prev[later] = rotate_seq(after(own[later], turn), 1)
            turn = after(turn, [own[later] for later in order])
        else:
            back[flip] = rotate_seq(held, -1)
    back[order[1]] = after(back[order[1]], back[0])
    for flip in order[1:]:
        part = own_grads[flip] + back[flip].astype(jnp.float32)
        part = part.astype(jnp.bfloat16)
        landed = swap_section(part, flip).astype(jnp.float32)
        total = landed if total is None else total + landed
    total = total + (own_grads[0] + back[0].astype(jnp.float32))
    dq = pl.pallas_call(
        functools.partial(store_kernel, slices),
        out_shape=jax.ShapeDtypeStruct(queries.shape[1:], jnp.bfloat16),
        in_specs=[vmem] * slices,
        out_specs=hbm,
        scratch_shapes=[pltpu.SemaphoreType.DMA((slices,))],
        compiler_params=params,
        name="store_slices",
    )(*[dq_parts[flip] for flip in range(slices)])
    return (dq[None], total[0], total[1])


def solution(mesh):
    placed = (
        P("section", "seq", None),
        P("section", "seq", None),
        P("seq", "section"),
        P("seq", "section"),
        P("seq"),
    )
    return jax.shard_map(
        body,
        mesh=mesh,
        in_specs=placed,
        out_specs=(P("section", "seq", None), P("seq", "section"), P("seq", "section")),
        check_vma=False,
    )
```

```python
import functools
import math

import jax
import jax.numpy as jnp
from jax import lax
from jax.experimental import pallas as pl
from jax.experimental.pallas import tpu as pltpu
from jax.sharding import PartitionSpec as P

HEADS = 32
KV_HEADS = 8
HEAD_DIM = 128
GROUP = HEADS // KV_HEADS
MASKED = -1e30
SCALE = 1.0 / math.sqrt(HEAD_DIM)
EXP2_SCALE = SCALE * math.log2(math.e)

NT = (((1,), (1,)), ((), ()))
NN = (((1,), (0,)), ((), ()))
TN = (((0,), (0,)), ((), ()))


def exchanged(x, partner_of):
    sections, shards = lax.axis_size("section"), lax.axis_size("seq")
    pairs = []
    for i in range(sections):
        for s in range(shards):
            j, t = partner_of(i, s, shards)
            pairs.append((i * shards + s, j * shards + t))
    return lax.ppermute(x, ("section", "seq"), pairs)


def swap_section(x, flip):
    return exchanged(x, lambda i, s, shards: (i ^ flip, s))


def rotate_seq(x, by):
    return exchanged(x, lambda i, s, shards: (i, (s + by) % shards))


def dot(a, b, dims):
    return lax.dot_general(a, b, dims, preferred_element_type=jnp.float32)


def softmax_grads(scores, dprob, causal):
    tok = causal.shape[0]
    dscores, wrounds = [], []
    for a in range(GROUP):
        head = slice(a * tok, (a + 1) * tok)
        parts = [jnp.where(causal, scores[-tok:, head], MASKED)]
        grads = [dprob[-tok:, head]]
        if scores.shape[0] > tok:
            parts.insert(0, scores[:tok, head])
            grads.insert(0, dprob[:tok, head])
        top = jnp.max(functools.reduce(jnp.maximum, parts), axis=0, keepdims=True)
        probs = [jnp.exp2((part - top) * EXP2_SCALE) for part in parts]
        inv = 1.0 / jnp.sum(sum(probs), axis=0, keepdims=True)
        mixed = sum(p * d for p, d in zip(probs, grads))
        row_dot = jnp.sum(mixed, axis=0, keepdims=True) * inv
        weights = [p * inv for p in probs]
        dscores.append([w * (d - row_dot) * SCALE for w, d in zip(weights, grads)])
        wrounds.append(weights)
    return [
        jnp.concatenate(
            [jnp.concatenate([x.astype(jnp.bfloat16) for x in parts], axis=0) for parts in heads],
            axis=1,
        )
        for heads in (dscores, wrounds)
    ]


def load_kernel(slices, q_hbm, g_hbm, *refs):
    q_outs, g_outs = refs[:slices], refs[slices : 2 * slices]
    turn_out, sems = refs[2 * slices :]
    place = lax.axis_index("section")
    width = q_outs[0].shape[1]
    copies = []
    for flip in range(slices):
        span = pl.ds(pl.multiple_of((place ^ flip) * width, width), width)
        copies.append(pltpu.make_async_copy(q_hbm.at[:, span], q_outs[flip], sems.at[0, flip]))
        copies.append(pltpu.make_async_copy(g_hbm.at[:, span], g_outs[flip], sems.at[1, flip]))
    for copy in copies:
        copy.start()
    turn_out[...] = jnp.zeros(turn_out.shape, turn_out.dtype)
    for copy in copies:
        copy.wait()


def store_kernel(slices, *refs):
    dq_ins, dq_hbm, sems = refs[:slices], refs[slices], refs[slices + 1]
    place = lax.axis_index("section")
    width = dq_ins[0].shape[1]
    copies = []
    for flip in range(slices):
        span = pl.ds(pl.multiple_of((place ^ flip) * width, width), width)
        copies.append(pltpu.make_async_copy(dq_ins[flip], dq_hbm.at[:, span], sems.at[flip]))
    for copy in copies:
        copy.start()
    for copy in copies:
        copy.wait()


def attention_kernel(first_ref, turn_ref, q_ref, g_ref, own_ref, prev_ref, *refs):
    _, tok, width = own_ref.shape
    dq_out, own_out, prev_out = refs[-3:]
    for ref in refs[:-3]:
        ref[...] = turn_ref[...]
    key_pos = lax.broadcasted_iota(jnp.int32, (tok, tok), 0)
    query_pos = lax.broadcasted_iota(jnp.int32, (tok, tok), 1)
    causal = key_pos <= query_pos

    def work(with_prev):
        groups = []
        for h in range(width // HEAD_DIM):
            cols = slice(h * HEAD_DIM, (h + 1) * HEAD_DIM)
            heads = [
                slice((h * GROUP + a) * HEAD_DIM, (h * GROUP + a + 1) * HEAD_DIM)
                for a in range(GROUP)
            ]
            q4 = jnp.concatenate([q_ref[:, c] for c in heads], axis=0)
            g4 = jnp.concatenate([g_ref[:, c] for c in heads], axis=0)
            k2, v2 = own_ref[0, :, cols], own_ref[1, :, cols]
            if with_prev:
                k2 = jnp.concatenate([prev_ref[0, :, cols], k2], axis=0)
                v2 = jnp.concatenate([prev_ref[1, :, cols], v2], axis=0)
            groups.append((cols, heads, q4, g4, k2, dot(k2, q4, NT), dot(v2, g4, NT)))
        rounded = [softmax_grads(scores, dprob, causal) for *_, scores, dprob in groups]
        results = []
        for (_, _, q4, g4, k2, _, _), (dscore, wround) in zip(groups, rounded):
            dq_t = dot(k2, dscore, TN).astype(jnp.bfloat16)
            results.append((dq_t, dot(dscore, q4, NN), dot(wround, g4, NN)))
        for (cols, heads, *_), (dq_t, dk, dv) in zip(groups, results):
            for a, head in enumerate(heads):
                dq_out[:, head] = dq_t[:, a * tok : (a + 1) * tok].T
            for kind, grad in enumerate((dk, dv)):
                own_out[kind, :, cols] = grad[-tok:]
                if with_prev:
                    prev_out[kind, :, cols] = grad[:tok].astype(jnp.bfloat16)

    seen = first_ref[0] < lax.axis_index("seq")

    @pl.when(seen)
    def _():
        work(True)

    @pl.when(jnp.logical_not(seen))
    def _():
        prev_out[...] = jnp.zeros(prev_out.shape, prev_out.dtype)
        work(False)


def after(x, token):
    return lax.optimization_barrier((x, token))[0]


def body(queries, grad_out, keys, values, key_first):
    slices = lax.axis_size("section")
    tok, width = keys.shape
    q_width = GROUP * width
    vmem = pl.BlockSpec(memory_space=pltpu.VMEM)
    smem = pl.BlockSpec(memory_space=pltpu.SMEM)
    hbm = pl.BlockSpec(memory_space=pltpu.HBM)
    params = pltpu.CompilerParams(vmem_limit_bytes=16 * 1024 * 1024)
    q_slice = jax.ShapeDtypeStruct((tok, q_width), jnp.bfloat16)
    tile = jax.ShapeDtypeStruct((8, 128), jnp.float32)
    order = [0] + list(range(slices - 1, 0, -1))

    pair = jnp.stack([keys, values])
    own = {flip: swap_section(pair, flip) for flip in order[1:]}
    own[0] = pair
    prev = {0: rotate_seq(pair, 1)}
    loaded = pl.pallas_call(
        functools.partial(load_kernel, slices),
        out_shape=[q_slice] * (2 * slices) + [tile],
        in_specs=[hbm, hbm],
        out_specs=[vmem] * (2 * slices + 1),
        scratch_shapes=[pltpu.SemaphoreType.DMA((2, slices))],
        compiler_params=params,
        name="load_slices",
    )(
        pltpu.with_memory_space_constraint(queries[0], pltpu.HBM),
        pltpu.with_memory_space_constraint(grad_out[0], pltpu.HBM),
    )
    turn = loaded[-1]
    prev[order[1]] = rotate_seq(after(own[order[1]], turn), 1)
    for flip in order[2:]:
        prev[flip] = swap_section(prev[0], flip)
    turn = after(turn, own[order[1]])
    total, dq_parts, own_grads, back = None, {}, {}, {}
    for step, flip in enumerate(order):
        last = step == slices - 1
        *_, dq_parts[flip], own_grads[flip], held = out = pl.pallas_call(
            attention_kernel,
            out_shape=[tile] * (not last)
            + [
                q_slice,
                jax.ShapeDtypeStruct(pair.shape, jnp.float32),
                jax.ShapeDtypeStruct(pair.shape, jnp.bfloat16),
            ],
            in_specs=[smem] + [vmem] * 5,
            out_specs=[vmem] * (3 if last else 4),
            compiler_params=params,
            name="attention_backward",
        )(key_first, turn, loaded[flip], loaded[slices + flip], own[flip], prev[flip])
        turn = out[0]
        if step == 0:
            back[0] = rotate_seq(held, -1)
            turn = after(turn, [own[later] for later in order])
        else:
            back[flip] = rotate_seq(held, -1)
    back[order[1]] = after(back[order[1]], back[0])
    for flip in order[1:]:
        part = own_grads[flip] + back[flip].astype(jnp.float32)
        part = part.astype(jnp.bfloat16)
        landed = swap_section(part, flip).astype(jnp.float32)
        total = landed if total is None else total + landed
    total = total + (own_grads[0] + back[0].astype(jnp.float32))
    dq = pl.pallas_call(
        functools.partial(store_kernel, slices),
        out_shape=jax.ShapeDtypeStruct(queries.shape[1:], jnp.bfloat16),
        in_specs=[vmem] * slices,
        out_specs=hbm,
        scratch_shapes=[pltpu.SemaphoreType.DMA((slices,))],
        compiler_params=params,
        name="store_slices",
    )(*[dq_parts[flip] for flip in range(slices)])
    return (dq[None], total[0], total[1])


def solution(mesh):
    placed = (
        P("section", "seq", None),
        P("section", "seq", None),
        P("seq", "section"),
        P("seq", "section"),
        P("seq"),
    )
    return jax.shard_map(
        body,
        mesh=mesh,
        in_specs=placed,
        out_specs=(P("section", "seq", None), P("seq", "section"), P("seq", "section")),
        check_vma=False,
    )
```

```python
import functools
import math

import jax
import jax.numpy as jnp
from jax import lax
from jax.experimental import pallas as pl
from jax.experimental.pallas import tpu as pltpu
from jax.sharding import PartitionSpec as P

HEADS = 32
KV_HEADS = 8
HEAD_DIM = 128
GROUP = HEADS // KV_HEADS
MASKED = -1e30
SCALE = 1.0 / math.sqrt(HEAD_DIM)
EXP2_SCALE = SCALE * math.log2(math.e)

NT = (((1,), (1,)), ((), ()))
NN = (((1,), (0,)), ((), ()))
TN = (((0,), (0,)), ((), ()))


def exchanged(x, partner_of):
    sections, shards = lax.axis_size("section"), lax.axis_size("seq")
    pairs = []
    for i in range(sections):
        for s in range(shards):
            j, t = partner_of(i, s, shards)
            pairs.append((i * shards + s, j * shards + t))
    return lax.ppermute(x, ("section", "seq"), pairs)


def swap_section(x, flip):
    return exchanged(x, lambda i, s, shards: (i ^ flip, s))


def rotate_seq(x, by):
    return exchanged(x, lambda i, s, shards: (i, (s + by) % shards))


def dot(a, b, dims):
    return lax.dot_general(a, b, dims, preferred_element_type=jnp.float32)


def softmax_grads(scores, dprob, causal):
    tok = causal.shape[0]
    dscores, wrounds = [], []
    for a in range(GROUP):
        head = slice(a * tok, (a + 1) * tok)
        parts = [jnp.where(causal, scores[-tok:, head], MASKED)]
        grads = [dprob[-tok:, head]]
        if scores.shape[0] > tok:
            parts.insert(0, scores[:tok, head])
            grads.insert(0, dprob[:tok, head])
        top = jnp.max(functools.reduce(jnp.maximum, parts), axis=0, keepdims=True)
        probs = [jnp.exp2((part - top) * EXP2_SCALE) for part in parts]
        inv = 1.0 / jnp.sum(sum(probs), axis=0, keepdims=True)
        mixed = sum(p * d for p, d in zip(probs, grads))
        row_dot = jnp.sum(mixed, axis=0, keepdims=True) * inv
        weights = [p * inv for p in probs]
        dscores.append([w * (d - row_dot) * SCALE for w, d in zip(weights, grads)])
        wrounds.append(weights)
    return [
        jnp.concatenate(
            [jnp.concatenate([x.astype(jnp.bfloat16) for x in parts], axis=0) for parts in heads],
            axis=1,
        )
        for heads in (dscores, wrounds)
    ]


def load_kernel(slices, q_hbm, g_hbm, *refs):
    q_outs, g_outs = refs[:slices], refs[slices : 2 * slices]
    turn_out, sems = refs[2 * slices :]
    place = lax.axis_index("section")
    width = q_outs[0].shape[1]
    copies = []
    for flip in range(slices):
        span = pl.ds(pl.multiple_of((place ^ flip) * width, width), width)
        copies.append(pltpu.make_async_copy(q_hbm.at[:, span], q_outs[flip], sems.at[0, flip]))
        copies.append(pltpu.make_async_copy(g_hbm.at[:, span], g_outs[flip], sems.at[1, flip]))
    for copy in copies:
        copy.start()
    turn_out[...] = jnp.zeros(turn_out.shape, turn_out.dtype)
    for copy in copies:
        copy.wait()


def store_kernel(slices, *refs):
    dq_ins, dq_hbm, sems = refs[:slices], refs[slices], refs[slices + 1]
    place = lax.axis_index("section")
    width = dq_ins[0].shape[1]
    copies = []
    for flip in range(slices):
        span = pl.ds(pl.multiple_of((place ^ flip) * width, width), width)
        copies.append(pltpu.make_async_copy(dq_ins[flip], dq_hbm.at[:, span], sems.at[flip]))
    for copy in copies:
        copy.start()
    for copy in copies:
        copy.wait()


def attention_kernel(first_ref, turn_ref, q_ref, g_ref, own_ref, prev_ref, *refs):
    _, tok, width = own_ref.shape
    dq_out, own_out, prev_out = refs[-3:]
    for ref in refs[:-3]:
        if ref.dtype == jnp.float32:
            ref[...] = turn_ref[...]
        else:
            prev_out[1] = ref[...]
            prev_out = prev_out.at[0]
    key_pos = lax.broadcasted_iota(jnp.int32, (tok, tok), 0)
    query_pos = lax.broadcasted_iota(jnp.int32, (tok, tok), 1)
    causal = key_pos <= query_pos

    def work(with_prev):
        groups = []
        for h in range(width // HEAD_DIM):
            cols = slice(h * HEAD_DIM, (h + 1) * HEAD_DIM)
            heads = [
                slice((h * GROUP + a) * HEAD_DIM, (h * GROUP + a + 1) * HEAD_DIM)
                for a in range(GROUP)
            ]
            q4 = jnp.concatenate([q_ref[:, c] for c in heads], axis=0)
            g4 = jnp.concatenate([g_ref[:, c] for c in heads], axis=0)
            k2, v2 = own_ref[0, :, cols], own_ref[1, :, cols]
            if with_prev:
                k2 = jnp.concatenate([prev_ref[0, :, cols], k2], axis=0)
                v2 = jnp.concatenate([prev_ref[1, :, cols], v2], axis=0)
            groups.append((cols, heads, q4, g4, k2, dot(k2, q4, NT), dot(v2, g4, NT)))
        rounded = [softmax_grads(scores, dprob, causal) for *_, scores, dprob in groups]
        results = []
        for (_, _, q4, g4, k2, _, _), (dscore, wround) in zip(groups, rounded):
            dq_t = dot(k2, dscore, TN).astype(jnp.bfloat16)
            results.append((dq_t, dot(dscore, q4, NN), dot(wround, g4, NN)))
        for (cols, heads, *_), (dq_t, dk, dv) in zip(groups, results):
            for a, head in enumerate(heads):
                dq_out[:, head] = dq_t[:, a * tok : (a + 1) * tok].T
            for kind, grad in enumerate((dk, dv)):
                own_out[kind, :, cols] = grad[-tok:]
                if with_prev:
                    prev_out[kind, :, cols] = grad[:tok].astype(jnp.bfloat16)

    seen = first_ref[0] < lax.axis_index("seq")

    @pl.when(seen)
    def _():
        work(True)

    @pl.when(jnp.logical_not(seen))
    def _():
        prev_out[...] = jnp.zeros(prev_out.shape, prev_out.dtype)
        work(False)


def after(x, token):
    return lax.optimization_barrier((x, token))[0]


def body(queries, grad_out, keys, values, key_first):
    slices = lax.axis_size("section")
    tok, width = keys.shape
    q_width = GROUP * width
    vmem = pl.BlockSpec(memory_space=pltpu.VMEM)
    smem = pl.BlockSpec(memory_space=pltpu.SMEM)
    hbm = pl.BlockSpec(memory_space=pltpu.HBM)
    params = pltpu.CompilerParams(vmem_limit_bytes=16 * 1024 * 1024)
    q_slice = jax.ShapeDtypeStruct((tok, q_width), jnp.bfloat16)
    tile = jax.ShapeDtypeStruct((8, 128), jnp.float32)
    order = [0] + list(range(slices - 1, 0, -1))

    pair = jnp.stack([keys, values])
    own = {flip: swap_section(pair, flip) for flip in order[1:]}
    own[0] = pair
    prev = {0: rotate_seq(pair, 1)}
    loaded = pl.pallas_call(
        functools.partial(load_kernel, slices),
        out_shape=[q_slice] * (2 * slices) + [tile],
        in_specs=[hbm, hbm],
        out_specs=[vmem] * (2 * slices + 1),
        scratch_shapes=[pltpu.SemaphoreType.DMA((2, slices))],
        compiler_params=params,
        name="load_slices",
    )(
        pltpu.with_memory_space_constraint(queries[0], pltpu.HBM),
        pltpu.with_memory_space_constraint(grad_out[0], pltpu.HBM),
    )
    turn = loaded[-1]
    prev[order[1]] = rotate_seq(after(own[order[1]], turn), 1)
    for flip in order[2:]:
        prev[flip] = swap_section(prev[0], flip)
    turn = after(turn, own[order[1]])
    total, dq_parts, own_grads, back = None, {}, {}, {}
    for step, flip in enumerate(order):
        last = step == slices - 1
        carried = [first_held] if last else []
        held_shape = ((2,) if last else ()) + pair.shape
        *_, dq_parts[flip], own_grads[flip], held = out = pl.pallas_call(
            attention_kernel,
            out_shape=[tile] * (not last)
            + [
                q_slice,
                jax.ShapeDtypeStruct(pair.shape, jnp.float32),
                jax.ShapeDtypeStruct(held_shape, jnp.bfloat16),
            ],
            in_specs=[smem] + [vmem] * (5 + len(carried)),
            out_specs=[vmem] * (3 if last else 4),
            compiler_params=params,
            name="attention_backward",
        )(key_first, turn, loaded[flip], loaded[slices + flip], own[flip], prev[flip], *carried)
        turn = out[0]
        if step == 0:
            first_held = held
            turn = after(turn, [own[later] for later in order])
        elif last:
            back[flip], back[0] = rotate_seq(held, -1)
        else:
            back[flip] = rotate_seq(held, -1)
    for flip in order[1:]:
        part = own_grads[flip] + back[flip].astype(jnp.float32)
        part = part.astype(jnp.bfloat16)
        landed = swap_section(part, flip).astype(jnp.float32)
        total = landed if total is None else total + landed
    total = total + (own_grads[0] + back[0].astype(jnp.float32))
    dq = pl.pallas_call(
        functools.partial(store_kernel, slices),
        out_shape=jax.ShapeDtypeStruct(queries.shape[1:], jnp.bfloat16),
        in_specs=[vmem] * slices,
        out_specs=hbm,
        scratch_shapes=[pltpu.SemaphoreType.DMA((slices,))],
        compiler_params=params,
        name="store_slices",
    )(*[dq_parts[flip] for flip in range(slices)])
    return (dq[None], total[0], total[1])


def solution(mesh):
    placed = (
        P("section", "seq", None),
        P("section", "seq", None),
        P("seq", "section"),
        P("seq", "section"),
        P("seq"),
    )
    return jax.shard_map(
        body,
        mesh=mesh,
        in_specs=placed,
        out_specs=(P("section", "seq", None), P("seq", "section"), P("seq", "section")),
        check_vma=False,
    )
```

```python
import functools
import math

import jax
import jax.numpy as jnp
from jax import lax
from jax.experimental import pallas as pl
from jax.experimental.pallas import tpu as pltpu
from jax.sharding import PartitionSpec as P

HEADS = 32
KV_HEADS = 8
HEAD_DIM = 128
GROUP = HEADS // KV_HEADS
MASKED = -1e30
SCALE = 1.0 / math.sqrt(HEAD_DIM)
EXP2_SCALE = SCALE * math.log2(math.e)

NT = (((1,), (1,)), ((), ()))
NN = (((1,), (0,)), ((), ()))
TN = (((0,), (0,)), ((), ()))


def exchanged(x, partner_of):
    sections, shards = lax.axis_size("section"), lax.axis_size("seq")
    pairs = []
    for i in range(sections):
        for s in range(shards):
            j, t = partner_of(i, s, shards)
            pairs.append((i * shards + s, j * shards + t))
    return lax.ppermute(x, ("section", "seq"), pairs)


def swap_section(x, flip):
    return exchanged(x, lambda i, s, shards: (i ^ flip, s))


def rotate_seq(x, by):
    return exchanged(x, lambda i, s, shards: (i, (s + by) % shards))


def dot(a, b, dims):
    return lax.dot_general(a, b, dims, preferred_element_type=jnp.float32)


def softmax_grads(scores, dprob, bias, causal):
    tok = causal.shape[0]
    dscores, wrounds = [], []
    for a in range(GROUP):
        head = slice(a * tok, (a + 1) * tok)
        parts = [jnp.where(causal, scores[-tok:, head], MASKED)]
        grads = [dprob[-tok:, head]]
        if bias is not None:
            parts.insert(0, scores[:tok, head] + bias)
            grads.insert(0, dprob[:tok, head])
        top = jnp.max(functools.reduce(jnp.maximum, parts), axis=0, keepdims=True)
        probs = [jnp.exp2((part - top) * EXP2_SCALE) for part in parts]
        inv = 1.0 / jnp.sum(sum(probs), axis=0, keepdims=True)
        mixed = sum(p * d for p, d in zip(probs, grads))
        row_dot = jnp.sum(mixed, axis=0, keepdims=True) * inv
        weights = [p * inv for p in probs]
        dscores.append([w * (d - row_dot) * SCALE for w, d in zip(weights, grads)])
        wrounds.append(weights)
    return [
        jnp.concatenate(
            [jnp.concatenate([x.astype(jnp.bfloat16) for x in parts], axis=0) for parts in heads],
            axis=1,
        )
        for heads in (dscores, wrounds)
    ]


def load_kernel(slices, first_ref, q_hbm, g_hbm, *refs):
    q_outs, g_outs = refs[:slices], refs[slices : 2 * slices]
    bias_out, sems = refs[2 * slices :]
    place = lax.axis_index("section")
    width = q_outs[0].shape[1]
    copies = []
    for flip in range(slices):
        span = pl.ds(pl.multiple_of((place ^ flip) * width, width), width)
        copies.append(pltpu.make_async_copy(q_hbm.at[:, span], q_outs[flip], sems.at[0, flip]))
        copies.append(pltpu.make_async_copy(g_hbm.at[:, span], g_outs[flip], sems.at[1, flip]))
    for copy in copies:
        copy.start()
    seen = first_ref[0] < lax.axis_index("seq")
    bias_out[...] = jnp.full(bias_out.shape, jnp.where(seen, 0.0, MASKED), jnp.float32)
    for copy in copies:
        copy.wait()


def store_kernel(slices, *refs):
    dq_ins, dq_hbm, sems = refs[:slices], refs[slices], refs[slices + 1]
    place = lax.axis_index("section")
    width = dq_ins[0].shape[1]
    copies = []
    for flip in range(slices):
        span = pl.ds(pl.multiple_of((place ^ flip) * width, width), width)
        copies.append(pltpu.make_async_copy(dq_ins[flip], dq_hbm.at[:, span], sems.at[flip]))
    for copy in copies:
        copy.start()
    for copy in copies:
        copy.wait()


def attention_kernel(bias_ref, q_ref, g_ref, own_ref, prev_ref, *refs):
    _, tok, width = own_ref.shape
    dq_out, own_out, prev_out = refs[-3:]
    for ref in refs[:-3]:
        ref[...] = bias_ref[...]
    key_pos = lax.broadcasted_iota(jnp.int32, (tok, tok), 0)
    query_pos = lax.broadcasted_iota(jnp.int32, (tok, tok), 1)
    causal = key_pos <= query_pos

    def work(bias):
        groups = []
        for h in range(width // HEAD_DIM):
            cols = slice(h * HEAD_DIM, (h + 1) * HEAD_DIM)
            heads = [
                slice((h * GROUP + a) * HEAD_DIM, (h * GROUP + a + 1) * HEAD_DIM)
                for a in range(GROUP)
            ]
            q4 = jnp.concatenate([q_ref[:, c] for c in heads], axis=0)
            g4 = jnp.concatenate([g_ref[:, c] for c in heads], axis=0)
            k2, v2 = own_ref[0, :, cols], own_ref[1, :, cols]
            if bias is not None:
                k2 = jnp.concatenate([prev_ref[0, :, cols], k2], axis=0)
                v2 = jnp.concatenate([prev_ref[1, :, cols], v2], axis=0)
            groups.append((cols, heads, q4, g4, k2, dot(k2, q4, NT), dot(v2, g4, NT)))
        rounded = [softmax_grads(scores, dprob, bias, causal) for *_, scores, dprob in groups]
        results = []
        for (_, _, q4, g4, k2, _, _), (dscore, wround) in zip(groups, rounded):
            dq_t = dot(k2, dscore, TN).astype(jnp.bfloat16)
            results.append((dq_t, dot(dscore, q4, NN), dot(wround, g4, NN)))
        for (cols, heads, *_), (dq_t, dk, dv) in zip(groups, results):
            for a, head in enumerate(heads):
                dq_out[:, head] = dq_t[:, a * tok : (a + 1) * tok].T
            for kind, grad in enumerate((dk, dv)):
                own_out[kind, :, cols] = grad[-tok:]
                if bias is not None:
                    prev_out[kind, :, cols] = grad[:tok].astype(jnp.bfloat16)

    @pl.when(lax.axis_index("seq") > 0)
    def _():
        work(bias_ref[0:1, 0:1])

    @pl.when(lax.axis_index("seq") == 0)
    def _():
        prev_out[...] = jnp.zeros(prev_out.shape, prev_out.dtype)
        work(None)


def after(x, token):
    return lax.optimization_barrier((x, token))[0]


def body(queries, grad_out, keys, values, key_first):
    slices = lax.axis_size("section")
    tok, width = keys.shape
    q_width = GROUP * width
    vmem = pl.BlockSpec(memory_space=pltpu.VMEM)
    hbm = pl.BlockSpec(memory_space=pltpu.HBM)
    params = pltpu.CompilerParams(vmem_limit_bytes=16 * 1024 * 1024)
    q_slice = jax.ShapeDtypeStruct((tok, q_width), jnp.bfloat16)
    tile = jax.ShapeDtypeStruct((8, 128), jnp.float32)
    order = [0] + list(range(slices - 1, 0, -1))

    pair = jnp.stack([keys, values])
    own = {flip: swap_section(pair, flip) for flip in order[1:]}
    own[0] = pair
    prev = {0: rotate_seq(pair, 1)}
    loaded = pl.pallas_call(
        functools.partial(load_kernel, slices),
        out_shape=[q_slice] * (2 * slices) + [tile],
        in_specs=[pl.BlockSpec(memory_space=pltpu.SMEM), hbm, hbm],
        out_specs=[vmem] * (2 * slices + 1),
        scratch_shapes=[pltpu.SemaphoreType.DMA((2, slices))],
        compiler_params=params,
        name="load_slices",
    )(
        key_first,
        pltpu.with_memory_space_constraint(queries[0], pltpu.HBM),
        pltpu.with_memory_space_constraint(grad_out[0], pltpu.HBM),
    )
    bias = loaded[-1]
    prev[order[1]] = rotate_seq(after(own[order[1]], bias), 1)
    bias = after(bias, own[order[1]])
    total, dq_parts, own_grads, back = None, {}, {}, {}
    for step, flip in enumerate(order):
        last = step == slices - 1
        *_, dq_parts[flip], own_grads[flip], held = out = pl.pallas_call(
            attention_kernel,
            out_shape=[tile] * (not last)
            + [
                q_slice,
                jax.ShapeDtypeStruct(pair.shape, jnp.float32),
                jax.ShapeDtypeStruct(pair.shape, jnp.bfloat16),
            ],
            in_specs=[vmem] * 5,
            out_specs=[vmem] * (3 if last else 4),
            compiler_params=params,
            name="attention_backward",
        )(bias, loaded[flip], loaded[slices + flip], own[flip], prev[flip])
        bias = out[0]
        if step == 0:
            first_held = held
            for later in order[2:]:
                prev[later] = rotate_seq(after(own[later], bias), 1)
            bias = after(bias, [own[later] for later in order])
        else:
            back[flip] = rotate_seq(held, -1)
        if step == 1:
            back[0] = rotate_seq(after(first_held, bias), -1)
    back[order[1]] = after(back[order[1]], back[0])
    for flip in order[1:]:
        part = own_grads[flip] + back[flip].astype(jnp.float32)
        part = part.astype(jnp.bfloat16)
        landed = swap_section(part, flip).astype(jnp.float32)
        total = landed if total is None else total + landed
    total = total + (own_grads[0] + back[0].astype(jnp.float32))
    dq = pl.pallas_call(
        functools.partial(store_kernel, slices),
        out_shape=jax.ShapeDtypeStruct(queries.shape[1:], jnp.bfloat16),
        in_specs=[vmem] * slices,
        out_specs=hbm,
        scratch_shapes=[pltpu.SemaphoreType.DMA((slices,))],
        compiler_params=params,
        name="store_slices",
    )(*[dq_parts[flip] for flip in range(slices)])
    return (dq[None], total[0], total[1])


def solution(mesh):
    placed = (
        P("section", "seq", None),
        P("section", "seq", None),
        P("seq", "section"),
        P("seq", "section"),
        P("seq"),
    )
    return jax.shard_map(
        body,
        mesh=mesh,
        in_specs=placed,
        out_specs=(P("section", "seq", None), P("seq", "section"), P("seq", "section")),
        check_vma=False,
    )
```

```python
import functools
import math

import jax
import jax.numpy as jnp
from jax import lax
from jax.experimental import pallas as pl
from jax.experimental.pallas import tpu as pltpu
from jax.sharding import PartitionSpec as P

HEADS = 32
KV_HEADS = 8
HEAD_DIM = 128
GROUP = HEADS // KV_HEADS
MASKED = -1e30
SCALE = 1.0 / math.sqrt(HEAD_DIM)
EXP2_SCALE = SCALE * math.log2(math.e)

NT = (((1,), (1,)), ((), ()))
NN = (((1,), (0,)), ((), ()))
TN = (((0,), (0,)), ((), ()))


def exchanged(x, partner_of):
    sections, shards = lax.axis_size("section"), lax.axis_size("seq")
    pairs = []
    for i in range(sections):
        for s in range(shards):
            j, t = partner_of(i, s, shards)
            pairs.append((i * shards + s, j * shards + t))
    return lax.ppermute(x, ("section", "seq"), pairs)


def swap_section(x, flip):
    return exchanged(x, lambda i, s, shards: (i ^ flip, s))


def rotate_seq(x, by):
    return exchanged(x, lambda i, s, shards: (i, (s + by) % shards))


def dot(a, b, dims):
    return lax.dot_general(a, b, dims, preferred_element_type=jnp.float32)


def softmax_grads(scores, dprob, bias, causal):
    tok = causal.shape[0]
    dscores, wrounds = [], []
    for a in range(GROUP):
        head = slice(a * tok, (a + 1) * tok)
        parts = [jnp.where(causal, scores[-tok:, head], MASKED)]
        grads = [dprob[-tok:, head]]
        if bias is not None:
            parts.insert(0, scores[:tok, head] + bias)
            grads.insert(0, dprob[:tok, head])
        top = jnp.max(functools.reduce(jnp.maximum, parts), axis=0, keepdims=True)
        probs = [jnp.exp2((part - top) * EXP2_SCALE) for part in parts]
        inv = 1.0 / jnp.sum(sum(probs), axis=0, keepdims=True)
        mixed = sum(p * d for p, d in zip(probs, grads))
        row_dot = jnp.sum(mixed, axis=0, keepdims=True) * inv
        weights = [p * inv for p in probs]
        dscores.append([w * (d - row_dot) * SCALE for w, d in zip(weights, grads)])
        wrounds.append(weights)
    return [
        jnp.concatenate(
            [jnp.concatenate([x.astype(jnp.bfloat16) for x in parts], axis=0) for parts in heads],
            axis=1,
        )
        for heads in (dscores, wrounds)
    ]


def load_kernel(slices, first_ref, q_hbm, g_hbm, *refs):
    q_outs, g_outs = refs[:slices], refs[slices : 2 * slices]
    bias_out, sems = refs[2 * slices :]
    place = lax.axis_index("section")
    width = q_outs[0].shape[1]
    copies = []
    for flip in range(slices):
        span = pl.ds(pl.multiple_of((place ^ flip) * width, width), width)
        copies.append(pltpu.make_async_copy(q_hbm.at[:, span], q_outs[flip], sems.at[0, flip]))
        copies.append(pltpu.make_async_copy(g_hbm.at[:, span], g_outs[flip], sems.at[1, flip]))
    for copy in copies:
        copy.start()
    seen = first_ref[0] < lax.axis_index("seq")
    bias_out[...] = jnp.full(bias_out.shape, jnp.where(seen, 0.0, MASKED), jnp.float32)
    for copy in copies:
        copy.wait()


def store_kernel(slices, *refs):
    dq_ins, dq_hbm, sems = refs[:slices], refs[slices], refs[slices + 1]
    place = lax.axis_index("section")
    width = dq_ins[0].shape[1]
    copies = []
    for flip in range(slices):
        span = pl.ds(pl.multiple_of((place ^ flip) * width, width), width)
        copies.append(pltpu.make_async_copy(dq_ins[flip], dq_hbm.at[:, span], sems.at[flip]))
    for copy in copies:
        copy.start()
    for copy in copies:
        copy.wait()


def attention_kernel(bias_ref, q_ref, g_ref, own_ref, prev_ref, *refs):
    _, tok, width = own_ref.shape
    dq_out, own_out, prev_out = refs[-3:]
    for ref in refs[:-3]:
        ref[...] = bias_ref[...]
    key_pos = lax.broadcasted_iota(jnp.int32, (tok, tok), 0)
    query_pos = lax.broadcasted_iota(jnp.int32, (tok, tok), 1)
    causal = key_pos <= query_pos

    def work(bias):
        groups = []
        for h in range(width // HEAD_DIM):
            cols = slice(h * HEAD_DIM, (h + 1) * HEAD_DIM)
            heads = [
                slice((h * GROUP + a) * HEAD_DIM, (h * GROUP + a + 1) * HEAD_DIM)
                for a in range(GROUP)
            ]
            q4 = jnp.concatenate([q_ref[:, c] for c in heads], axis=0)
            g4 = jnp.concatenate([g_ref[:, c] for c in heads], axis=0)
            k2, v2 = own_ref[0, :, cols], own_ref[1, :, cols]
            if bias is not None:
                k2 = jnp.concatenate([prev_ref[0, :, cols], k2], axis=0)
                v2 = jnp.concatenate([prev_ref[1, :, cols], v2], axis=0)
            groups.append((cols, heads, q4, g4, k2, dot(k2, q4, NT), dot(v2, g4, NT)))
        rounded = [softmax_grads(scores, dprob, bias, causal) for *_, scores, dprob in groups]
        results = []
        for (_, _, q4, g4, k2, _, _), (dscore, wround) in zip(groups, rounded):
            dq_t = dot(k2, dscore, TN).astype(jnp.bfloat16)
            results.append((dq_t, dot(dscore, q4, NN), dot(wround, g4, NN)))
        for (cols, heads, *_), (dq_t, dk, dv) in zip(groups, results):
            for a, head in enumerate(heads):
                dq_out[:, head] = dq_t[:, a * tok : (a + 1) * tok].T
            for kind, grad in enumerate((dk, dv)):
                own_out[kind, :, cols] = grad[-tok:]
                if bias is not None:
                    prev_out[kind, :, cols] = grad[:tok].astype(jnp.bfloat16)

    @pl.when(lax.axis_index("seq") > 0)
    def _():
        work(bias_ref[0:1, 0:1])

    @pl.when(lax.axis_index("seq") == 0)
    def _():
        prev_out[...] = jnp.zeros(prev_out.shape, prev_out.dtype)
        work(None)


def after(x, token):
    return lax.optimization_barrier((x, token))[0]


def body(queries, grad_out, keys, values, key_first):
    slices = lax.axis_size("section")
    tok, width = keys.shape
    q_width = GROUP * width
    vmem = pl.BlockSpec(memory_space=pltpu.VMEM)
    hbm = pl.BlockSpec(memory_space=pltpu.HBM)
    params = pltpu.CompilerParams(vmem_limit_bytes=16 * 1024 * 1024)
    q_slice = jax.ShapeDtypeStruct((tok, q_width), jnp.bfloat16)
    tile = jax.ShapeDtypeStruct((8, 128), jnp.float32)
    order = [0] + list(range(slices - 1, 0, -1))

    pair = jnp.stack([keys, values])
    own = {flip: swap_section(pair, flip) for flip in order[1:]}
    own[0] = pair
    prev = {0: rotate_seq(pair, 1)}
    loaded = pl.pallas_call(
        functools.partial(load_kernel, slices),
        out_shape=[q_slice] * (2 * slices) + [tile],
        in_specs=[pl.BlockSpec(memory_space=pltpu.SMEM), hbm, hbm],
        out_specs=[vmem] * (2 * slices + 1),
        scratch_shapes=[pltpu.SemaphoreType.DMA((2, slices))],
        compiler_params=params,
        name="load_slices",
    )(
        key_first,
        pltpu.with_memory_space_constraint(queries[0], pltpu.HBM),
        pltpu.with_memory_space_constraint(grad_out[0], pltpu.HBM),
    )
    bias = loaded[-1]
    prev[order[1]] = rotate_seq(after(own[order[1]], bias), 1)
    prev[order[-1]] = swap_section(prev[0], order[-1])
    bias = after(bias, own[order[1]])
    total, dq_parts, own_grads, back = None, {}, {}, {}
    for step, flip in enumerate(order):
        last = step == slices - 1
        *_, dq_parts[flip], own_grads[flip], held = out = pl.pallas_call(
            attention_kernel,
            out_shape=[tile] * (not last)
            + [
                q_slice,
                jax.ShapeDtypeStruct(pair.shape, jnp.float32),
                jax.ShapeDtypeStruct(pair.shape, jnp.bfloat16),
            ],
            in_specs=[vmem] * 5,
            out_specs=[vmem] * (3 if last else 4),
            compiler_params=params,
            name="attention_backward",
        )(bias, loaded[flip], loaded[slices + flip], own[flip], prev[flip])
        bias = out[0]
        if step == 0:
            back[0] = rotate_seq(held, -1)
            for later in order[2:-1]:
                prev[later] = rotate_seq(after(own[later], bias), 1)
            bias = after(bias, [own[later] for later in order])
        else:
            back[flip] = rotate_seq(held, -1)
    back[order[1]] = after(back[order[1]], back[0])
    for flip in order[1:]:
        part = own_grads[flip] + back[flip].astype(jnp.float32)
        part = part.astype(jnp.bfloat16)
        landed = swap_section(part, flip).astype(jnp.float32)
        total = landed if total is None else total + landed
    total = total + (own_grads[0] + back[0].astype(jnp.float32))
    dq = pl.pallas_call(
        functools.partial(store_kernel, slices),
        out_shape=jax.ShapeDtypeStruct(queries.shape[1:], jnp.bfloat16),
        in_specs=[vmem] * slices,
        out_specs=hbm,
        scratch_shapes=[pltpu.SemaphoreType.DMA((slices,))],
        compiler_params=params,
        name="store_slices",
    )(*[dq_parts[flip] for flip in range(slices)])
    return (dq[None], total[0], total[1])


def solution(mesh):
    placed = (
        P("section", "seq", None),
        P("section", "seq", None),
        P("seq", "section"),
        P("seq", "section"),
        P("seq"),
    )
    return jax.shard_map(
        body,
        mesh=mesh,
        in_specs=placed,
        out_specs=(P("section", "seq", None), P("seq", "section"), P("seq", "section")),
        check_vma=False,
    )
```
